256 devices in a mesh: qrow: 16 (over x, y_hi, core), kcol: 16 (over y_lo, z).
Axes of the slice: x: 4, y: 4 (y_hi: 2, y_lo: 2; y = y_hi * 2 + y_lo), z: 8, core: 2. Of those that a mesh axis runs over, the one named last changes fastest.
Arguments:
- single: bfloat16 [2, 2048, 768], P(None, ('qrow', 'kcol'))
- restype: int32 [2048], P(('qrow', 'kcol')), may hold values from 0 to 31
- restype_table: bfloat16 [32, 768], replicated, may hold values from -6 to 6
- chain: int32 [2048], replicated, may hold values from 0 to 7, never falling along the last dimension, each value on 1 to 512 neighbouring positions
- live: int32 [2048], P('kcol'), may hold values from 0 to 1, as said below
- pair: bfloat16 [2048, 2048, 128], P('qrow', 'kcol')
- pair_gain: float32 [128], replicated, may hold values from 0.1 to 1.9
- pair_weight: float32 [128, 16], replicated
- chain_bias: float32 [16], replicated, may hold values from -4 to 4
- single_gain: float32 [768], replicated, may hold values from 0.1 to 1.9
- w_qkvg: bfloat16 [768, 3072], replicated
- w_out: bfloat16 [768, 768], replicated, may hold values from -0.875 to 0.875
Outputs:
- update: bfloat16 [2, 2048, 768], P(None, ('qrow', 'kcol'))
The draws below stay inside these ranges and needn't reach their ends.
Inputs may be any that keep to these rules, and one draw needn't show every extreme that they name: Token 0 is always live and the last token is always padding; padding tokens may stand anywhere else. `chain`: chain numbers never fall along the tokens.
All inputs are finite; a program needn't handle non-finite values.
Results may differ from the reference program's by a relative error of at most 0.018.
Values may be sent and summed in bfloat16 or wider, within the bound.
No kernel may reach another device: no remote copies, remote signals or barrier semaphores. Data moves between devices by JAX's collectives and lax.ppermute only.
A program may use at most 64 MiB of HBM per device.

```python
import math
import jax
import jax.numpy as jnp
import numpy as np
from jax import lax

D = 768
HEADS = 16
PAIR_C = 128
RESTYPES = 32
HEAD_SIZE = 48
SAMPLES = 2
TOKENS = 2048


def shared_direction(key):
    return 2.0 * jax.random.bernoulli(key, 0.5, (PAIR_C,)).astype(jnp.float32) - 1.0


def token_direction(key):
    return 2.0 * jax.random.bernoulli(jax.random.fold_in(key, 11), 0.5, (D,)).astype(jnp.float32) - 1.0


def head_direction(key):
    return 2.0 * jax.random.bernoulli(jax.random.fold_in(key, 12), 0.5, (D,)).astype(jnp.float32) - 1.0


def draw_single(key, part):
    direction = token_direction(key)
    key = jax.random.fold_in(key, 4)
    first, second, third = jax.random.split(key, 3)
    base = jax.random.normal(first, (SAMPLES, TOKENS, D), jnp.float32)
    strength = 1.2
    carries = jax.random.bernoulli(second, 0.5, (SAMPLES, TOKENS, 1)).astype(jnp.float32)
    signs = 2.0 * jax.random.bernoulli(third, 0.5, (SAMPLES, TOKENS, 1)).astype(jnp.float32) - 1.0
    result = jnp.clip(base + strength * carries * signs * direction[None, None, :], -6.0, 6.0)
    return result.astype(jnp.bfloat16)


def draw_w_qkvg(key, part):
    row_direction = token_direction(key)
    column_direction = head_direction(key)
    key = jax.random.fold_in(key, 5)
    noise = jnp.clip(jax.random.normal(key, (D, 4 * D), jnp.float32), -6.0, 6.0) * (1.0 / math.sqrt(D))
    coupling = math.sqrt(150.0 / math.sqrt(HEAD_SIZE)) / (0.65 * D)
    columns = jnp.concatenate([column_direction, column_direction, jnp.zeros((2 * D,), jnp.float32)])
    result = noise + coupling * row_direction[:, None] * columns[None, :]
    return result.astype(jnp.bfloat16)


def draw_live(key, part):
    key = jax.random.fold_in(key, 1)
    ticket = jax.random.randint(key, (TOKENS,), 0, 4)
    positions = jnp.arange(TOKENS, dtype=jnp.int32)
    kept = (ticket != 0).astype(jnp.int32)
    kept = jnp.where(positions == 0, 1, kept)
    kept = jnp.where(positions == TOKENS - 1, 0, kept)
    return kept.astype(jnp.int32)


def draw_pair(key, part):
    direction = shared_direction(key)
    key = jax.random.fold_in(key, 2)
    first, second, third = jax.random.split(key, 3)
    base = jax.random.normal(first, (TOKENS, TOKENS, PAIR_C), jnp.float32)
    along = jnp.mean(base * direction, -1, keepdims=True)
    across = base - along * direction
    chosen_rows = jax.random.uniform(second, (TOKENS, 1)) < 0.1
    chosen_cells = jax.random.uniform(third, (TOKENS, TOKENS)) < 4.0 / TOKENS
    aligned = jnp.logical_and(chosen_rows, chosen_cells)
    result = jnp.where(aligned[..., None], 3.0 * direction + 0.2 * base, across)
    return result.astype(jnp.bfloat16)


def draw_pair_weight(key, part):
    direction = shared_direction(key)
    key = jax.random.fold_in(key, 3)
    first, second = jax.random.split(key)
    noise = jax.random.normal(first, (PAIR_C, HEADS), jnp.float32)
    strength = jax.random.uniform(second, (1, HEADS), jnp.float32, 1.0, 2.0) * (120.0 / PAIR_C)
    return direction[:, None] * strength + 0.3 * noise


def touch_ends(drawn, key, low, largest):
    longest = drawn.shape.index(max(drawn.shape))
    spots = []
    for shift in (0, 1):
        where = [jax.random.randint(jax.random.fold_in(key, axis), (), 0, length) for axis, length in enumerate(drawn.shape)]
        where[longest] = (where[longest] + shift) % drawn.shape[longest]
        spots.append(tuple(where))
    return drawn.at[spots[0]].set(low).at[spots[1]].set(largest)


def split_up(count, total, most, skew):
    loads = [(1 << 20) // math.isqrt(standing ** skew) + 1 for standing in range(2, count + 1)]
    surplus, holding = total - most - (count - 1), [1] * (count - 1)
    while surplus > 0:
        candidates = [i for i in range(count - 1) if holding[i] < most]
        pool, left = sum([loads[i] for i in candidates]), surplus
        for i in candidates:
            extra = min(most - holding[i], max(1, left * loads[i] // pool), surplus)
            holding[i] = holding[i] + extra
            surplus = surplus - extra
    return np.array([most] + holding)


def ragged_sizes(stream_key, count, total, limit, skew):
    if count == 2:
        one = jax.random.randint(stream_key, (), max(1, total - limit), min(limit, total - 1) + 1)
        return jnp.stack([one, total - one])
    tallies = jnp.asarray(split_up(count, total, limit, skew), jnp.int32)
    pairs = (count - 1) // 2
    source_of, taker = tallies[1:1 + 2 * pairs:2], tallies[2:2 + 2 * pairs:2]
    slack = jnp.minimum(source_of - 1, limit - taker)
    shifted = jax.random.randint(jax.random.fold_in(stream_key, 1), (pairs,), 0, 1 << 20) % (slack + 1)
    tallies = tallies.at[1:1 + 2 * pairs:2].set(source_of - shifted).at[2:2 + 2 * pairs:2].set(taker + shifted)
    return tallies[jax.random.permutation(jax.random.fold_in(stream_key, 2), count)]


def bell_draw(own_key, dims, spread, limit, kind=jnp.bfloat16):
    return jnp.clip(spread * jax.random.normal(own_key, dims, jnp.float32), -limit, limit).astype(kind)


def setup_inputs(seed: int = 0) -> dict:
    key_list = jax.random.split(jax.random.key(seed), 13)
    single = draw_single(jax.random.fold_in(key_list[12], 71), 0)
    restype = touch_ends(jax.random.randint(key_list[1], (TOKENS,), 0, RESTYPES), jax.random.fold_in(key_list[1], 1), 0, RESTYPES - 1).astype(jnp.int32)
    restype_table = bell_draw(key_list[2], (RESTYPES, D), 1.0, 6.0)
    chain = jnp.searchsorted(jnp.cumsum(ragged_sizes(key_list[3], 8, TOKENS, TOKENS // 4, 2)), jnp.arange(TOKENS), side="right").astype(jnp.int32)
    live = draw_live(jax.random.fold_in(key_list[12], 71), 0)
    pair = draw_pair(jax.random.fold_in(key_list[12], 71), 0)
    pair_gain = jnp.clip(1.0 + 0.18 * jax.random.normal(key_list[6], (PAIR_C,), jnp.float32), 0.1, 1.9)
    pair_weight = draw_pair_weight(jax.random.fold_in(key_list[12], 71), 0)
    chain_bias = bell_draw(key_list[8], (HEADS,), 1.0, 4.0, jnp.float32)
    single_gain = jnp.clip(1.0 + 0.18 * jax.random.normal(key_list[9], (D,), jnp.float32), 0.1, 1.9)
    w_qkvg = draw_w_qkvg(jax.random.fold_in(key_list[12], 71), 0)
    w_out = bell_draw(key_list[11], (D, D), (D // 16) ** -0.5, 0.875)
    return {"single": single, "restype": restype, "restype_table": restype_table, "chain": chain, "live": live, "pair": pair, "pair_gain": pair_gain, "pair_weight": pair_weight, "chain_bias": chain_bias, "single_gain": single_gain, "w_qkvg": w_qkvg, "w_out": w_out}


def layer_norm(inputs, scales):
    average = lax.optimization_barrier(jnp.mean(inputs, -1, keepdims=True))
    centred = inputs - average
    variance = lax.optimization_barrier(jnp.mean(centred * centred, -1, keepdims=True))
    return centred * lax.rsqrt(variance + 1e-05) * scales

def rounded(inputs):
    return lax.optimization_barrier(inputs.astype(jnp.bfloat16)).astype(jnp.float32)

def reference(single, restype, restype_table, chain, live, pair, pair_gain, pair_weight, chain_bias, single_gain, w_qkvg, w_out):
    embedded = single.astype(jnp.float32) + restype_table[restype].astype(jnp.float32)[None]
    normed = layer_norm(embedded, single_gain).astype(jnp.bfloat16)
    flattened = normed.reshape(SAMPLES * TOKENS, D)
    projected = jnp.dot(flattened, w_qkvg, preferred_element_type=jnp.float32).reshape(SAMPLES, TOKENS, 4 * D)
    queries = rounded(projected[..., :D]).reshape(SAMPLES, TOKENS, HEADS, HEAD_SIZE)
    key_rows = rounded(projected[..., D:2 * D]).reshape(SAMPLES, TOKENS, HEADS, HEAD_SIZE)
    value_rows = rounded(projected[..., 2 * D:3 * D]).reshape(SAMPLES, TOKENS, HEADS, HEAD_SIZE)
    gating = jax.nn.sigmoid(projected[..., 3 * D:])
    live_mask = (live == 1)[None, None, None, :]
    block_rows = math.gcd(TOKENS, 128)
    block_count = TOKENS // block_rows

    def one_block(block_index):
        offset = (block_index * block_rows).astype(jnp.int32)
        pair_rows = lax.dynamic_slice_in_dim(pair, offset, block_rows, 0).astype(jnp.float32)
        pair_normed = layer_norm(pair_rows, pair_gain)
        pair_bias = jnp.einsum('qkc,ch->hqk', pair_normed, pair_weight, precision=lax.Precision.HIGHEST)
        row_chain = lax.dynamic_slice_in_dim(chain, offset, block_rows, 0)
        same_chain = (row_chain[:, None] == chain[None, :]).astype(jnp.float32)
        pair_bias = pair_bias + chain_bias[:, None, None] * same_chain[None]
        block_queries = lax.dynamic_slice_in_dim(queries, offset, block_rows, 1)
        scores = jnp.einsum('sqhd,skhd->shqk', block_queries, key_rows, precision=lax.Precision.HIGHEST)
        scores = scores / math.sqrt(HEAD_SIZE) + pair_bias[None]
        scores = jnp.where(live_mask, scores, -1e+30)
        top_score = lax.optimization_barrier(jnp.max(scores, -1, keepdims=True))
        weights = jnp.where(live_mask, jnp.exp(scores - top_score), 0.0)
        denominator = jnp.transpose(lax.optimization_barrier(jnp.sum(weights, -1)), (0, 2, 1))
        numerator = jnp.einsum('shqk,skhd->sqhd', rounded(weights), value_rows, precision=lax.Precision.HIGHEST)
        return (numerator / denominator[..., None]).reshape(SAMPLES, block_rows, D)
    attended = lax.map(one_block, jnp.arange(block_count, dtype=jnp.int32))
    attended = jnp.transpose(attended, (1, 0, 2, 3)).reshape(SAMPLES, TOKENS, D)
    gated = (gating * attended).astype(jnp.bfloat16)
    update = jnp.dot(gated.reshape(SAMPLES * TOKENS, D), w_out, preferred_element_type=jnp.float32)
    return update.astype(jnp.bfloat16).reshape(SAMPLES, TOKENS, D)
```

```python
import math

import jax
import jax.numpy as jnp
from jax import lax
from jax.experimental import pallas as pl
from jax.experimental.pallas import tpu as pltpu
from jax.sharding import PartitionSpec as P

BF = jnp.bfloat16
F32 = jnp.float32
EPS = 1e-05
STATS = 128


def vmem():
    return pl.BlockSpec(memory_space=pltpu.VMEM)


def smem():
    return pl.BlockSpec(memory_space=pltpu.SMEM)


def dot_nt(a, b):
    return lax.dot_general(a, b, (((1,), (1,)), ((), ())), preferred_element_type=F32)


def layer_norm(x):
    centred = x - jnp.mean(x, -1, keepdims=True)
    variance = jnp.mean(centred * centred, -1, keepdims=True)
    return centred * lax.rsqrt(variance + EPS)


def split3(x):
    hi = x.astype(BF)
    rest = x - hi.astype(F32)
    mid = rest.astype(BF)
    low = (rest - mid.astype(F32)).astype(BF)
    return hi, mid, low


def norm_kernel(restype_ref, single_ref, table_ref, gain_ref, normed_ref, copies_ref):
    samples, tok, width = single_ref.shape
    kinds = table_ref.shape[0]
    row = lax.broadcasted_iota(jnp.int32, (tok, kinds), 0)
    col = lax.broadcasted_iota(jnp.int32, (tok, kinds), 1)
    kind = jnp.zeros((tok, kinds), jnp.int32)
    for t in range(tok):
        kind = jnp.where(row == t, restype_ref[t], kind)
    one_hot = jnp.where(kind == col, 1.0, 0.0).astype(BF)
    emb = jnp.dot(one_hot, table_ref[...], preferred_element_type=F32)
    x = single_ref[...].astype(F32) + emb[None]
    normed = (layer_norm(x) * gain_ref[...][None]).reshape(samples * tok, width).astype(BF)
    normed_ref[...] = normed
    for j in range(copies_ref.shape[0]):
        copies_ref[j] = normed


def bias_kernel(
    where_ref, chain_ref, cbias_ref, chain_rows_ref, live_ref, gain_ref, weight_ref, pair_ref, out_ref, lhs_ref, cb_ref
):
    heads, channels = weight_ref.shape
    block, keys, _ = pair_ref.shape
    step = pl.program_id(0)

    @pl.when(step == 0)
    def _():
        hi, mid, low = split3(weight_ref[...] * gain_ref[...])
        lhs_ref[...] = jnp.concatenate(
            [
                jnp.concatenate([hi, hi], 1),
                jnp.concatenate([mid, mid], 1),
                jnp.concatenate([low, jnp.zeros_like(low)], 1),
            ],
            0,
        )
        row = lax.broadcasted_iota(jnp.int32, (heads, keys), 0)
        column = jnp.zeros((heads, keys), F32)
        for h in range(heads):
            column = jnp.where(row == h, cbias_ref[h], column)
        cb_ref[...] = column

    first = where_ref[0] * (block * pl.num_programs(0)) + step * block
    col_chain = chain_rows_ref[pl.ds(where_ref[1], 1), :]
    alive = live_ref[...] == 1
    lhs = lhs_ref[...]
    column = cb_ref[...]
    for q in range(0, block, 2):
        x = pair_ref[q : q + 2].astype(F32).reshape(2 * keys, channels)
        z = layer_norm(x)
        hi = z.astype(BF)
        low = (z - hi.astype(F32)).astype(BF)
        res = dot_nt(lhs, jnp.concatenate([hi, low], 1))
        res = res[:heads] + res[heads : 2 * heads] + res[2 * heads :]
        for i in range(2):
            part = res[:, i * keys : (i + 1) * keys]
            same = col_chain == chain_ref[first + q + i]
            part = part + jnp.where(same, column, 0.0)
            out_ref[:, q + i, :] = jnp.where(alive, part, -1e30)


def query_kernel(rows_ref, own_ref, wq_ref, wg_ref, q_ref, gate_ref):
    parts, per, width = rows_ref.shape
    half = per // 2
    x = rows_ref[...].reshape(parts * per, width)
    proj = jnp.dot(x, wq_ref[...], preferred_element_type=F32)
    proj = proj.reshape(parts, 2, half, width)
    for s in range(2):
        q_ref[s] = proj[:, s].reshape(parts * half, width).astype(BF)
    pre = jnp.dot(own_ref[...], wg_ref[...], preferred_element_type=F32)
    gate_ref[...] = jax.nn.sigmoid(pre)


def attend_kernel(rows_ref, wk_ref, wv_ref, q_ref, bias_ref, out_ref, acc_ref):
    parts, per, width = rows_ref.shape
    half = per // 2
    heads, queries, keys = bias_ref.shape
    size = width // heads
    scale = 1.0 / math.sqrt(size)
    x = rows_ref[...].reshape(parts * per, width)
    kf = jnp.dot(x, wk_ref[...], preferred_element_type=F32).reshape(parts, 2, half, width)
    vf = jnp.dot(x, wv_ref[...], preferred_element_type=F32).reshape(parts, 2, half, width)
    lane = lax.broadcasted_iota(jnp.int32, (queries, STATS), 1)
    for s in range(2):
        k = kf[:, s].reshape(keys, width).astype(BF)
        v = vf[:, s].reshape(keys, width).astype(BF)
        q = q_ref[s]
        sums = [jnp.zeros((queries, 128), F32) for _ in range(width // 128)]
        tops = jnp.zeros((queries, STATS), F32)
        tots = jnp.zeros((queries, STATS), F32)
        for h in range(heads):
            a, b = h * size // 128, -(-(h + 1) * size // 128)
            spot = lax.broadcasted_iota(jnp.int32, (1, (b - a) * 128), 1) + a * 128
            mask = jnp.where((spot >= h * size) & (spot < (h + 1) * size), 1.0, 0.0).astype(BF)
            cut = slice(a * 128, b * 128)
            sc = dot_nt(q[:, cut] * mask, k[:, cut]) * scale + bias_ref[h]
            top = jnp.max(sc, -1, keepdims=True)
            w = jnp.exp(sc - top)
            tot = jnp.sum(w, -1, keepdims=True)
            o = jnp.dot(w.astype(BF), v[:, cut] * mask, preferred_element_type=F32)
            for i in range(b - a):
                sums[a + i] = sums[a + i] + o[:, i * 128 : (i + 1) * 128]
            tops = jnp.where(lane == h, top, tops)
            tots = jnp.where(lane == h, tot, tots)
        hi, mid, low = split3(tops)
        thi, tmid, _ = split3(tots)
        stats = hi.astype(F32)
        for i, p in enumerate((mid, low, thi, tmid)):
            stats = stats + pltpu.roll(p.astype(F32), heads * (i + 1), 1)
        for i, p in enumerate(sums + [stats]):
            acc_ref[:, s * half : (s + 1) * half, i * 128 : (i + 1) * 128] = p.reshape(parts, half, 128)
    out_ref[...] = acc_ref[...].astype(BF)


def merge_kernel(parts_ref, gate_ref, wout_ref, out_ref):
    parts, per, wide = parts_ref.shape
    width = wide - STATS
    heads = 16
    size = width // heads
    st = parts_ref[:, :, width:].astype(F32).reshape(parts * per, STATS)
    top = st + pltpu.roll(st, STATS - heads, 1) + pltpu.roll(st, STATS - 2 * heads, 1)
    tot = pltpu.roll(st, STATS - 3 * heads, 1) + pltpu.roll(st, STATS - 4 * heads, 1)
    lane = lax.broadcasted_iota(jnp.int32, (parts * per, STATS), 1)
    top = jnp.where(lane < heads, top, 0.0).reshape(parts, per, STATS)
    tot = jnp.where(lane < heads, tot, 1.0).reshape(parts, per, STATS)
    e = jnp.exp(top - jnp.max(top, 0, keepdims=True))
    f = e / jnp.sum(e * tot, 0, keepdims=True)
    f = jnp.where(lane < heads, f.reshape(parts * per, STATS), 0.0)
    hrow = lax.broadcasted_iota(jnp.int32, (STATS, width), 0) * size
    col = lax.broadcasted_iota(jnp.int32, (STATS, width), 1)
    spread = jnp.where((col >= hrow) & (col < hrow + size), 1.0, 0.0).astype(BF)
    hi = f.astype(BF)
    low = (f - hi.astype(F32)).astype(BF)
    factor = jnp.dot(jnp.concatenate([hi, low], 1), jnp.concatenate([spread, spread], 0), preferred_element_type=F32)
    num = parts_ref[:, :, :width].astype(F32)
    attended = jnp.sum(num * factor.reshape(parts, per, width), 0)
    gated = (gate_ref[...] * attended).astype(BF)
    update = jnp.dot(gated, wout_ref[...], preferred_element_type=F32)
    out_ref[...] = update.reshape(out_ref.shape).astype(BF)


def params(mib):
    return pltpu.CompilerParams(vmem_limit_bytes=mib << 20)


def shards(
    single,
    restype,
    restype_table,
    chain,
    live,
    pair,
    pair_gain,
    pair_weight,
    chain_bias,
    single_gain,
    w_qkvg,
    w_out,
):
    samples, tok, width = single.shape
    row_len, col_len, channels = pair.shape
    heads = chain_bias.shape[0]
    n_row, n_col = lax.axis_size("qrow"), lax.axis_size("kcol")
    shape = jax.ShapeDtypeStruct
    own = samples * tok

    normed, copies = pl.pallas_call(
        norm_kernel,
        name="norm",
        out_shape=(shape((own, width), BF), shape((n_col, own, width), BF)),
        in_specs=[smem(), vmem(), vmem(), vmem()],
        out_specs=(vmem(), vmem()),
        compiler_params=params(16),
    )(restype, single, restype_table, single_gain.reshape(1, width))

    swap = [(r * n_col + c, c * n_col + r) for r in range(n_row) for c in range(n_col)]
    turned = lax.ppermute(normed, ("qrow", "kcol"), swap)
    row_tokens = lax.all_to_all(copies, "kcol", 0, 0)
    col_tokens = lax.all_to_all(jnp.broadcast_to(turned[None], (n_row, own, width)), "qrow", 0, 0)

    block = 16
    where = jnp.stack([lax.axis_index("qrow"), lax.axis_index("kcol")]).astype(jnp.int32)
    whole = lambda *dims: pl.BlockSpec(dims, lambda i: (0,) * len(dims))
    bias = pl.pallas_call(
        bias_kernel,
        name="bias",
        grid=(row_len // block,),
        out_shape=shape((heads, row_len, col_len), F32),
        in_specs=[
            smem(),
            smem(),
            smem(),
            whole(chain.shape[0] // col_len, col_len),
            whole(1, col_len),
            whole(1, channels),
            whole(heads, channels),
            pl.BlockSpec((block, col_len, channels), lambda i: (i, 0, 0)),
        ],
        out_specs=pl.BlockSpec((heads, block, col_len), lambda i: (0, i, 0)),
        scratch_shapes=[pltpu.VMEM((3 * heads, 2 * channels), BF), pltpu.VMEM((heads, col_len), F32)],
        compiler_params=params(16),
        cost_estimate=pl.CostEstimate(flops=10**9, bytes_accessed=40 * 10**6, transcendentals=0),
    )(
        where,
        chain,
        chain_bias,
        chain.reshape(-1, col_len),
        live.reshape(1, col_len),
        pair_gain.reshape(1, channels),
        pair_weight.T,
        pair,
    )

    cols = lambda i: pl.BlockSpec((width, width), lambda step: (0, i))
    queries, gate = pl.pallas_call(
        query_kernel,
        name="query",
        grid=(1,),
        out_shape=(shape((samples, row_len, width), BF), shape((own, width), F32)),
        in_specs=[vmem(), vmem(), cols(0), cols(3)],
        out_specs=(vmem(), vmem()),
        compiler_params=params(24),
    )(row_tokens, normed, w_qkvg, w_qkvg)

    partial = pl.pallas_call(
        attend_kernel,
        name="attend",
        grid=(1,),
        out_shape=shape((n_col, own, width + STATS), BF),
        in_specs=[vmem(), cols(1), cols(2), vmem(), vmem()],
        out_specs=vmem(),
        scratch_shapes=[pltpu.VMEM((n_col, own, width + STATS), F32)],
        compiler_params=params(32),
    )(col_tokens, w_qkvg, w_qkvg, queries, bias)

    gathered = lax.all_to_all(partial, "kcol", 0, 0)
    return pl.pallas_call(
        merge_kernel,
        name="merge",
        out_shape=shape((samples, tok, width), BF),
        in_specs=[vmem(), vmem(), vmem()],
        out_specs=vmem(),
        compiler_params=params(24),
    )(gathered, gate, w_out)


def solution(mesh):
    return jax.shard_map(
        shards,
        mesh=mesh,
        in_specs=(
            P(None, ("qrow", "kcol"), None),
            P(("qrow", "kcol")),
            P(),
            P(),
            P("kcol"),
            P("qrow", "kcol", None),
            P(),
            P(),
            P(),
            P(),
            P(),
            P(),
        ),
        out_specs=P(None, ("qrow", "kcol"), None),
        check_vma=False,
    )
```

```python
import functools
import math

import jax
import jax.numpy as jnp
from jax import lax
from jax.experimental import pallas as pl
from jax.experimental.pallas import tpu as pltpu
from jax.sharding import PartitionSpec as P

BF = jnp.bfloat16
F32 = jnp.float32
EPS = 1e-05


def vmem():
    return pl.BlockSpec(memory_space=pltpu.VMEM)


def smem():
    return pl.BlockSpec(memory_space=pltpu.SMEM)


def dot_nt(a, b):
    return lax.dot_general(a, b, (((1,), (1,)), ((), ())), preferred_element_type=F32)


def layer_norm(x):
    centred = x - jnp.mean(x, -1, keepdims=True)
    variance = jnp.mean(centred * centred, -1, keepdims=True)
    return centred * lax.rsqrt(variance + EPS)


def split3(x):
    hi = x.astype(BF)
    rest = x - hi.astype(F32)
    mid = rest.astype(BF)
    low = (rest - mid.astype(F32)).astype(BF)
    return hi, mid, low


def fetch(copies, sems):
    started = [pltpu.make_async_copy(src, dst, sems.at[i]) for i, (src, dst) in enumerate(copies)]
    for copy in started:
        copy.start()
    for copy in started:
        copy.wait()


def norm_kernel(
    restype_hbm, single_hbm, table_hbm, gain_hbm, normed_ref, copies_ref, restype_ref, single_ref, table_ref, gain_ref, sems
):
    fetch(
        [
            (restype_hbm, restype_ref),
            (single_hbm, single_ref),
            (table_hbm, table_ref),
            (gain_hbm, gain_ref),
        ],
        sems,
    )
    samples, tok, width = single_ref.shape
    kinds = table_ref.shape[0]
    row = lax.broadcasted_iota(jnp.int32, (tok, kinds), 0)
    col = lax.broadcasted_iota(jnp.int32, (tok, kinds), 1)
    kind = jnp.zeros((tok, kinds), jnp.int32)
    for t in range(tok):
        kind = jnp.where(row == t, restype_ref[t], kind)
    one_hot = jnp.where(kind == col, 1.0, 0.0).astype(BF)
    emb = jnp.dot(one_hot, table_ref[...], preferred_element_type=F32)
    x = single_ref[...].astype(F32) + emb[None]
    normed = layer_norm(x) * gain_ref[...].reshape(1, 1, width)
    normed = normed.reshape(samples * tok, width).astype(BF)
    normed_ref[...] = normed
    for j in range(copies_ref.shape[0]):
        copies_ref[j] = normed


def copies_kernel(one_ref, after_ref, copies_ref):
    for j in range(copies_ref.shape[0]):
        copies_ref[j] = one_ref[...]


def bias_kernel(
    start,
    where_ref,
    normed_ref,
    chain_hbm,
    cbias_hbm,
    chain_rows_hbm,
    live_hbm,
    gain_hbm,
    weight_hbm,
    pair_hbm,
    out_ref,
    chain_ref,
    cbias_ref,
    chain_rows_ref,
    live_ref,
    gain_ref,
    weight_ref,
    pair_ref,
    sems,
    pair_sems,
):
    chunks, block, keys, channels = pair_ref.shape
    heads = weight_ref.shape[0]
    loads = [
        pltpu.make_async_copy(pair_hbm.at[pl.ds(start + i * block, block)], pair_ref.at[i], pair_sems.at[i])
        for i in range(chunks)
    ]
    loads[0].start()
    fetch(
        [
            (chain_hbm, chain_ref),
            (cbias_hbm, cbias_ref),
            (chain_rows_hbm, chain_rows_ref),
            (live_hbm, live_ref),
            (gain_hbm, gain_ref),
            (weight_hbm, weight_ref),
        ],
        sems,
    )
    for load in loads[1:]:
        load.start()
    hi, mid, low = split3(weight_ref[...] * gain_ref[...])
    lhs = jnp.concatenate(
        [
            jnp.concatenate([hi, hi], 1),
            jnp.concatenate([mid, mid], 1),
            jnp.concatenate([low, jnp.zeros_like(low)], 1),
        ],
        0,
    )
    row = lax.broadcasted_iota(jnp.int32, (heads, keys), 0)
    column = jnp.zeros((heads, keys), F32)
    for h in range(heads):
        column = jnp.where(row == h, cbias_ref[h], column)
    base = where_ref[0] * pair_hbm.shape[0] + start
    col_chain = chain_rows_ref[pl.ds(where_ref[1], 1), :]
    alive = live_ref[...] == 1
    for i in range(chunks):
        loads[i].wait()
        for q in range(0, block, 2):
            x = pair_ref[i, q : q + 2].astype(F32).reshape(2 * keys, channels)
            z = layer_norm(x)
            hi = z.astype(BF)
            low = (z - hi.astype(F32)).astype(BF)
            res = dot_nt(lhs, jnp.concatenate([hi, low], 1))
            res = res[:heads] + res[heads : 2 * heads] + res[2 * heads :]
            for k in range(2):
                at = i * block + q + k
                part = res[:, k * keys : (k + 1) * keys]
                same = col_chain == chain_ref[base + at]
                part = part + jnp.where(same, column, 0.0)
                out_ref[:, at, :] = jnp.where(alive, part, -1e30)


def query_kernel(rows_ref, own_ref, w_hbm, q_ref, gate_ref, wkv_ref, wqg_ref, sems):
    parts, per, width = rows_ref.shape
    half = per // 2
    cut = lambda i, n: w_hbm.at[:, pl.ds(i * width, n * width)]
    ahead = pltpu.make_async_copy(cut(1, 2), wkv_ref, sems.at[2])
    load_q = pltpu.make_async_copy(cut(0, 1), wqg_ref.at[0], sems.at[0])
    load_g = pltpu.make_async_copy(cut(3, 1), wqg_ref.at[1], sems.at[1])
    load_q.start()
    load_g.start()
    ahead.start()
    load_q.wait()
    x = rows_ref[...].reshape(parts * per, width)
    proj = jnp.dot(x, wqg_ref[0], preferred_element_type=F32)
    proj = proj.reshape(parts, 2, half, width)
    for s in range(2):
        q_ref[s] = proj[:, s].reshape(parts * half, width).astype(BF)
    load_g.wait()
    pre = jnp.dot(own_ref[...], wqg_ref[1], preferred_element_type=F32)
    gate_ref[...] = jax.nn.sigmoid(pre)
    ahead.wait()


def attend_kernel(order_ref, rows_ref, wkv_ref, q_ref, bias_a_ref, bias_b_ref, out_ref, x_ref):
    parts, per, width = rows_ref.shape
    half = per // 2
    heads, few, keys = bias_a_ref.shape
    queries = 2 * few
    size = width // heads
    tiles = width // 128
    scale = 1.0 / math.sqrt(size)
    for i in range(parts):
        x_ref[pl.ds(order_ref[i], 1)] = rows_ref[pl.ds(i, 1)]
    x = x_ref[...].reshape(parts * per, width)
    kf = jnp.dot(x, wkv_ref[:, :width], preferred_element_type=F32).reshape(parts, 2, half, width)
    vf = jnp.dot(x, wkv_ref[:, width:], preferred_element_type=F32).reshape(parts, 2, half, width)
    lane = lax.broadcasted_iota(jnp.int32, (queries, 128), 1)
    both = []
    for s in range(2):
        k = kf[:, s].reshape(keys, width).astype(BF)
        v = vf[:, s].reshape(keys, width).astype(BF)
        q = q_ref[s]
        sums = [jnp.zeros((queries, 128), F32) for _ in range(tiles)]
        tops = jnp.zeros((queries, 128), F32)
        tots = jnp.zeros((queries, 128), F32)
        for h in range(heads):
            a, b = h * size // 128, -(-(h + 1) * size // 128)
            spot = lax.broadcasted_iota(jnp.int32, (1, (b - a) * 128), 1) + a * 128
            mask = jnp.where((spot >= h * size) & (spot < (h + 1) * size), 1.0, 0.0).astype(BF)
            cut = slice(a * 128, b * 128)
            sc = dot_nt(q[:, cut] * mask, k[:, cut]) * scale + jnp.concatenate([bias_a_ref[h], bias_b_ref[h]], 0)
            top = jnp.max(sc, -1, keepdims=True)
            w = jnp.exp(sc - top)
            tot = jnp.sum(w, -1, keepdims=True)
            o = jnp.dot(w.astype(BF), v[:, cut] * mask, preferred_element_type=F32)
            for i in range(b - a):
                sums[a + i] = sums[a + i] + o[:, i * 128 : (i + 1) * 128]
            tops = jnp.where(lane == h, top, tops)
            tots = jnp.where(lane == h, tot, tots)
        hi, mid, low = split3(tops)
        stats = hi.astype(F32)
        for i, p in enumerate((mid.astype(F32), low.astype(F32), tots)):
            stats = stats + pltpu.roll(p, heads * (i + 1), 1)
        both.append([p.reshape(parts, 1, half, 128) for p in sums + [stats]])
    for i in range(tiles):
        pair = jnp.concatenate([both[0][i], both[1][i]], 1)
        out_ref[:, i * per : (i + 1) * per, :] = pair.reshape(parts, per, 128).astype(BF)
    first, second = [p[tiles].reshape(queries, 128) for p in both]
    stats = first + pltpu.roll(second, 64, 1)
    out_ref[:, tiles * per :, :] = stats.reshape(parts, half, 128).astype(BF)


def merge_kernel(parts_ref, gate_ref, wout_ref, out_ref):
    parts, rows, _ = parts_ref.shape
    per, width = gate_ref.shape
    half = per // 2
    tiles = width // 128
    heads = 16
    size = width // heads
    both = parts_ref[:, tiles * per :, :].astype(F32).reshape(parts, 1, half, 128)
    other = pltpu.roll(both.reshape(parts * half, 128), 64, 1).reshape(parts, 1, half, 128)
    st = jnp.concatenate([both, other], 1).reshape(parts * per, 128)
    top = st + pltpu.roll(st, 128 - heads, 1) + pltpu.roll(st, 128 - 2 * heads, 1)
    tot = pltpu.roll(st, 128 - 3 * heads, 1)
    lane = lax.broadcasted_iota(jnp.int32, (parts * per, 128), 1)
    top = jnp.where(lane < heads, top, 0.0).reshape(parts, per, 128)
    tot = jnp.where(lane < heads, tot, 1.0).reshape(parts, per, 128)
    e = jnp.exp(top - jnp.max(top, 0, keepdims=True))
    f = e / jnp.sum(e * tot, 0, keepdims=True)
    f = jnp.where(lane < heads, f.reshape(parts * per, 128), 0.0)
    hrow = lax.broadcasted_iota(jnp.int32, (128, width), 0) * size
    col = lax.broadcasted_iota(jnp.int32, (128, width), 1)
    spread = jnp.where((col >= hrow) & (col < hrow + size), 1.0, 0.0).astype(BF)
    hi = f.astype(BF)
    low = (f - hi.astype(F32)).astype(BF)
    factor = jnp.dot(jnp.concatenate([hi, low], 1), jnp.concatenate([spread, spread], 0), preferred_element_type=F32)
    attended = []
    for i in range(tiles):
        num = parts_ref[:, i * per : (i + 1) * per, :].astype(F32)
        attended.append(jnp.sum(num * factor[:, i * 128 : (i + 1) * 128].reshape(parts, per, 128), 0))
    gated = (gate_ref[...] * jnp.concatenate(attended, 1)).astype(BF)
    update = jnp.dot(gated, wout_ref[...], preferred_element_type=F32)
    out_ref[...] = update.reshape(out_ref.shape).astype(BF)


def near_swap(n):
    ring = lambda a, b, size: min((a - b) % size, (b - a) % size)
    table = []
    for c in range(n):
        cx, cyh, cco = c // 4, c // 2 % 2, c % 2
        cyl, cz = c // 8, c % 8

        def cost(j, i):
            hops = ring(cx, i // 4, 4) + ring(j % 8, cz, 8)
            hops += ring(cyh * 2 + j // 8, (i // 2 % 2) * 2 + cyl, 4)
            return 2 * hops + (cco != i % 2)

        for most in range(100):
            taken = {}

            def place(j, seen):
                for i in range(n):
                    if cost(j, i) <= most and i not in seen:
                        seen.add(i)
                        if i not in taken or place(taken[i], seen):
                            taken[i] = j
                            return True
                return False

            if all(place(j, set()) for j in range(n)):
                break
        table.append([taken[i] for i in range(n)])
    return table


def params(mib):
    return pltpu.CompilerParams(vmem_limit_bytes=mib << 20)


def shards(
    single,
    restype,
    restype_table,
    chain,
    live,
    pair,
    pair_gain,
    pair_weight,
    chain_bias,
    single_gain,
    w_qkvg,
    w_out,
):
    samples, tok, width = single.shape
    row_len, col_len, channels = pair.shape
    heads = chain_bias.shape[0]
    n_row, n_col = lax.axis_size("qrow"), lax.axis_size("kcol")
    shape = jax.ShapeDtypeStruct
    own = samples * tok

    stay = lambda *arrays: [pltpu.with_memory_space_constraint(x, pltpu.HBM) for x in arrays]
    hbm = lambda count: [pl.BlockSpec(memory_space=pltpu.HBM)] * count
    dma = pltpu.SemaphoreType.DMA
    normed, copies = pl.pallas_call(
        norm_kernel,
        name="norm",
        out_shape=(shape((own, width), BF), shape((n_col, own, width), BF)),
        in_specs=hbm(4),
        out_specs=(vmem(), vmem()),
        scratch_shapes=[
            pltpu.SMEM((tok,), jnp.int32),
            pltpu.VMEM((samples, tok, width), BF),
            pltpu.VMEM(restype_table.shape, BF),
            pltpu.VMEM((width,), F32),
            dma((4,)),
        ],
        compiler_params=params(4),
    )(*stay(restype, single, restype_table, single_gain))

    table = near_swap(n_row)
    swap = [(c * n_col + j, i * n_col + c) for c in range(n_row) for i, j in enumerate(table[c])]
    turned = lax.ppermute(normed, ("qrow", "kcol"), swap)
    row_tokens = lax.all_to_all(copies, "kcol", 0, 0)

    row_at, col_at = lax.axis_index("qrow"), lax.axis_index("kcol")
    where = jnp.stack([row_at, col_at]).astype(jnp.int32)
    order = jnp.asarray(table, jnp.int32)[col_at]
    chunks = 4
    half = row_len // 2

    def bias_of(part):
        return pl.pallas_call(
            functools.partial(bias_kernel, part * half),
            name="bias_" + str(part),
            out_shape=shape((heads, half, col_len), F32),
            in_specs=[smem()] + hbm(8),
            out_specs=vmem(),
            scratch_shapes=[
                pltpu.SMEM(chain.shape, jnp.int32),
                pltpu.SMEM((heads,), F32),
                pltpu.VMEM((chain.shape[0] // col_len, col_len), jnp.int32),
                pltpu.VMEM((1, col_len), jnp.int32),
                pltpu.VMEM((1, channels), F32),
                pltpu.VMEM((heads, channels), F32),
                pltpu.VMEM((chunks, half // chunks, col_len, channels), BF),
                dma((6,)),
                dma((chunks,)),
            ],
            compiler_params=params(6),
            cost_estimate=pl.CostEstimate(flops=5 * 10**8, bytes_accessed=10 * 10**6, transcendentals=0),
        )(
            where,
            normed,
            *stay(
                chain,
                chain_bias,
                chain.reshape(-1, col_len),
                live.reshape(1, col_len),
                pair_gain.reshape(1, channels),
                pair_weight.T,
                pair,
            ),
        )

    bias = [bias_of(part) for part in range(2)]
    turned_copies = pl.pallas_call(
        copies_kernel,
        name="copies",
        out_shape=shape((n_row, own, width), BF),
        in_specs=[vmem(), pl.BlockSpec(memory_space=pl.ANY)],
        out_specs=vmem(),
        compiler_params=params(4),
    )(turned, bias[0])
    col_tokens = lax.all_to_all(turned_copies, "qrow", 0, 0)

    queries, gate, w_kv = pl.pallas_call(
        query_kernel,
        name="query",
        out_shape=(
            shape((samples, row_len, width), BF),
            shape((own, width), F32),
            shape((width, 2 * width), BF),
        ),
        in_specs=[vmem(), vmem()] + hbm(1),
        out_specs=(vmem(), vmem(), vmem()),
        scratch_shapes=[pltpu.VMEM((2, width, width), BF), dma((3,))],
        compiler_params=params(10),
    )(row_tokens, normed, *stay(w_qkvg))

    rows = own * width // 128 + tok
    partial = pl.pallas_call(
        attend_kernel,
        name="attend",
        out_shape=shape((n_col, rows, 128), BF),
        in_specs=[smem()] + [vmem()] * 5,
        out_specs=vmem(),
        scratch_shapes=[pltpu.VMEM(col_tokens.shape, BF)],
        compiler_params=params(12),
    )(order, col_tokens, w_kv, queries, *bias)

    gathered = lax.all_to_all(partial, "kcol", 0, 0)
    return pl.pallas_call(
        merge_kernel,
        name="merge",
        out_shape=shape((samples, tok, width), BF),
        in_specs=[vmem(), vmem(), vmem()],
        out_specs=vmem(),
        compiler_params=params(8),
    )(gathered, gate, w_out)


def solution(mesh):
    return jax.shard_map(
        shards,
        mesh=mesh,
        in_specs=(
            P(None, ("qrow", "kcol"), None),
            P(("qrow", "kcol")),
            P(),
            P(),
            P("kcol"),
            P("qrow", "kcol", None),
            P(),
            P(),
            P(),
            P(),
            P(),
            P(),
        ),
        out_specs=P(None, ("qrow", "kcol"), None),
        check_vma=False,
    )
```

```python
import functools
import math

import jax
import jax.numpy as jnp
from jax import lax
from jax.experimental import pallas as pl
from jax.experimental.pallas import tpu as pltpu
from jax.sharding import PartitionSpec as P

BF = jnp.bfloat16
F32 = jnp.float32
EPS = 1e-05


def vmem():
    return pl.BlockSpec(memory_space=pltpu.VMEM)


def smem():
    return pl.BlockSpec(memory_space=pltpu.SMEM)


def dot_nt(a, b):
    return lax.dot_general(a, b, (((1,), (1,)), ((), ())), preferred_element_type=F32)


def layer_norm(x):
    centred = x - jnp.mean(x, -1, keepdims=True)
    variance = jnp.mean(centred * centred, -1, keepdims=True)
    return centred * lax.rsqrt(variance + EPS)


def split3(x):
    hi = x.astype(BF)
    rest = x - hi.astype(F32)
    mid = rest.astype(BF)
    low = (rest - mid.astype(F32)).astype(BF)
    return hi, mid, low


def fetch(copies, sems):
    started = [pltpu.make_async_copy(src, dst, sems.at[i]) for i, (src, dst) in enumerate(copies)]
    for copy in started:
        copy.start()
    for copy in started:
        copy.wait()


def norm_kernel(
    restype_hbm, single_hbm, table_hbm, gain_hbm, normed_ref, copies_ref, restype_ref, single_ref, table_ref, gain_ref, sems
):
    fetch(
        [
            (restype_hbm, restype_ref),
            (single_hbm, single_ref),
            (table_hbm, table_ref),
            (gain_hbm, gain_ref),
        ],
        sems,
    )
    samples, tok, width = single_ref.shape
    kinds = table_ref.shape[0]
    row = lax.broadcasted_iota(jnp.int32, (tok, kinds), 0)
    col = lax.broadcasted_iota(jnp.int32, (tok, kinds), 1)
    kind = jnp.zeros((tok, kinds), jnp.int32)
    for t in range(tok):
        kind = jnp.where(row == t, restype_ref[t], kind)
    one_hot = jnp.where(kind == col, 1.0, 0.0).astype(BF)
    emb = jnp.dot(one_hot, table_ref[...], preferred_element_type=F32)
    x = single_ref[...].astype(F32) + emb[None]
    normed = layer_norm(x) * gain_ref[...].reshape(1, 1, width)
    normed = normed.reshape(samples * tok, width).astype(BF)
    normed_ref[...] = normed
    for j in range(copies_ref.shape[0]):
        copies_ref[j] = normed


def copies_kernel(one_ref, after_ref, copies_ref):
    for j in range(copies_ref.shape[0]):
        copies_ref[j] = one_ref[...]


def bias_kernel(start, ahead, where_ref, normed_ref, *refs):
    ins, refs = refs[: 7 + ahead], refs[7 + ahead :]
    pair_hbm = ins[6]
    out_ref, refs = refs[0], refs[1:]
    if ahead:
        (gate_ref, w_ref), refs = refs[:2], refs[2:]
    chain_ref, cbias_ref, chain_rows_ref, live_ref, gain_ref, weight_ref, pair_ref, sems, pair_sems = refs[:9]
    chunks, block, keys, channels = pair_ref.shape
    heads = weight_ref.shape[0]
    loads = [
        pltpu.make_async_copy(pair_hbm.at[pl.ds(start + i * block, block)], pair_ref.at[i], pair_sems.at[i])
        for i in range(chunks)
    ]
    for load in loads[:2]:
        load.start()
    small = list(zip(ins[:6], (chain_ref, cbias_ref, chain_rows_ref, live_ref, gain_ref, weight_ref)))
    small = [pltpu.make_async_copy(src, dst, sems.at[i]) for i, (src, dst) in enumerate(small)]
    for load in small + loads[2:]:
        load.start()
    if ahead:
        width = normed_ref.shape[1]
        wg_ref, w_sems = refs[9:]
        w_hbm = ins[7]
        load_g = pltpu.make_async_copy(w_hbm.at[:, pl.ds(3 * width, width)], wg_ref, w_sems.at[0])
        load_w = pltpu.make_async_copy(w_hbm.at[:, pl.ds(width, 2 * width)], w_ref, w_sems.at[1])
        load_g.start()
        load_w.start()
    for load in small:
        load.wait()
    weight = weight_ref[...] * gain_ref[...]
    lhs = jnp.concatenate(split3(weight), 0)
    total = jnp.sum(weight, -1, keepdims=True)
    row = lax.broadcasted_iota(jnp.int32, (heads, keys), 0)
    column = jnp.zeros((heads, keys), F32)
    for h in range(heads):
        column = jnp.where(row == h, cbias_ref[h], column)
    base = where_ref[0] * pair_hbm.shape[0] + start
    col_chain = chain_rows_ref[pl.ds(where_ref[1], 1), :]
    alive = jnp.broadcast_to(live_ref[...] == 1, (heads, keys))
    for i in range(chunks):
        loads[i].wait()
        for q in range(0, block, 2):
            turned = pair_ref[i, q : q + 2].reshape(2 * keys, channels).T
            x = turned.astype(F32)
            mean = jnp.sum(x, 0, keepdims=True) * (1.0 / channels)
            centred = x - mean
            variance = jnp.sum(centred * centred, 0, keepdims=True) * (1.0 / channels)
            res = jnp.dot(lhs, turned, preferred_element_type=F32)
            res = res[:heads] + res[heads : 2 * heads] + res[2 * heads :]
            res = (res - total * mean) * lax.rsqrt(variance + EPS)
            for k in range(2):
                at = i * block + q + k
                part = res[:, k * keys : (k + 1) * keys]
                same = col_chain == chain_ref[base + at]
                part = part + jnp.where(same, column, 0.0)
                out_ref[:, at, :] = jnp.where(alive, part, -1e30)
    if ahead:
        load_g.wait()
        pre = jnp.dot(normed_ref[...], wg_ref[...], preferred_element_type=F32)
        gate_ref[...] = jax.nn.sigmoid(pre)
        load_w.wait()


def attend_kernel(
    where_ref,
    order_ref,
    rows_ref,
    cols_hbm,
    wkv_ref,
    w_hbm,
    bias_a_hbm,
    bias_b_hbm,
    out_ref,
    x_ref,
    wq_ref,
    bias_ref,
    sems,
):
    parts, per, width = rows_ref.shape
    half = per // 2
    heads, queries, keys = bias_ref.shape
    few = queries // 2
    size = width // heads
    scale = 1.0 / math.sqrt(size)
    loads = [
        pltpu.make_async_copy(w_hbm.at[:, pl.ds(0, width)], wq_ref, sems.at[0]),
        pltpu.make_async_copy(bias_a_hbm, bias_ref.at[:, pl.ds(0, few)], sems.at[1]),
        pltpu.make_async_copy(bias_b_hbm, bias_ref.at[:, pl.ds(few, few)], sems.at[2]),
    ]
    tokens = [
        pltpu.make_async_copy(cols_hbm.at[i], x_ref.at[order_ref[where_ref[1] * parts + i]], sems.at[3 + i])
        for i in range(parts)
    ]
    for load in tokens + loads:
        load.start()
    for load in tokens:
        load.wait()

    def project(tokens, w):
        x = tokens[...].reshape(parts * per, width)
        return jnp.dot(x, w, preferred_element_type=F32).reshape(parts, 2, half, width)

    kf, vf = project(x_ref, wkv_ref[:, :width]), project(x_ref, wkv_ref[:, width:])
    for load in loads:
        load.wait()
    qf = project(rows_ref, wq_ref[...])
    span = 256
    wins = width // span

    def members(t):
        return [h for h in range(heads) if h * size < (t + 1) * span and (h + 1) * size > t * span]

    def mask_of(h, t):
        spot = lax.broadcasted_iota(jnp.int32, (1, span), 1) + t * span
        return jnp.where((spot >= h * size) & (spot < (h + 1) * size), 1.0, 0.0).astype(BF)

    lane = lax.broadcasted_iota(jnp.int32, (queries, 128), 1)
    stats = jnp.zeros((queries, 128), F32)
    for s in range(2):
        q = qf[:, s].reshape(queries, width).astype(BF)
        k = kf[:, s].reshape(keys, width).astype(BF)
        v = vf[:, s].reshape(keys, width).astype(BF)
        raw = {}
        for t in range(wins):
            cut = slice(t * span, (t + 1) * span)
            lhs = jnp.concatenate([q[:, cut] * mask_of(h, t) for h in members(t)], 0)
            res = dot_nt(lhs, k[:, cut])
            for i, h in enumerate(members(t)):
                piece = res[i * queries : (i + 1) * queries]
                raw[h] = raw[h] + piece if h in raw else piece
        tops = jnp.zeros((queries, 128), F32)
        tots = jnp.zeros((queries, 128), F32)
        rounded = []
        for h in range(heads):
            sc = raw[h] * scale + bias_ref[h]
            top = jnp.max(sc, -1, keepdims=True)
            w = jnp.exp(sc - top)
            rounded.append(w.astype(BF))
            tots = jnp.where(lane == h, jnp.sum(w, -1, keepdims=True), tots)
            tops = jnp.where(lane == h, top, tops)
        for t in range(wins):
            cut = slice(t * span, (t + 1) * span)
            o = jnp.dot(
                jnp.concatenate([rounded[h] for h in members(t)], 1),
                jnp.concatenate([v[:, cut] * mask_of(h, t) for h in members(t)], 0),
                preferred_element_type=F32,
            )
            at = (s * wins + t) * per
            tiles = [o[:, i * 128 : (i + 1) * 128].reshape(parts, half, 128) for i in range(2)]
            out_ref[:, at : at + per, :] = jnp.concatenate(tiles, 1).astype(BF)
        hi, mid, low = split3(tops)
        mine = hi.astype(F32)
        for i, p in enumerate((mid.astype(F32), low.astype(F32), tots)):
            mine = mine + pltpu.roll(p, heads * (i + 1), 1)
        stats = stats + (pltpu.roll(mine, 64, 1) if s else mine)
    out_ref[:, 2 * wins * per :, :] = stats.reshape(parts, half, 128).astype(BF)


def merge_kernel(parts_ref, gate_ref, wout_ref, out_ref):
    parts, rows, _ = parts_ref.shape
    per, width = gate_ref.shape
    half = per // 2
    tiles = width // 128
    heads = 16
    size = width // heads
    both = parts_ref[:, tiles * per :, :].astype(F32).reshape(parts, 1, half, 128)
    other = pltpu.roll(both.reshape(parts * half, 128), 64, 1).reshape(parts, 1, half, 128)
    st = jnp.concatenate([both, other], 1).reshape(parts * per, 128)
    top = st + pltpu.roll(st, 128 - heads, 1) + pltpu.roll(st, 128 - 2 * heads, 1)
    tot = pltpu.roll(st, 128 - 3 * heads, 1)
    lane = lax.broadcasted_iota(jnp.int32, (parts * per, 128), 1)
    top = jnp.where(lane < heads, top, 0.0).reshape(parts, per, 128)
    tot = jnp.where(lane < heads, tot, 1.0).reshape(parts, per, 128)
    e = jnp.exp(top - jnp.max(top, 0, keepdims=True))
    f = e / jnp.sum(e * tot, 0, keepdims=True)
    f = jnp.where(lane < heads, f.reshape(parts * per, 128), 0.0)
    hrow = lax.broadcasted_iota(jnp.int32, (128, width), 0) * size
    col = lax.broadcasted_iota(jnp.int32, (128, width), 1)
    spread = jnp.where((col >= hrow) & (col < hrow + size), 1.0, 0.0).astype(BF)
    hi = f.astype(BF)
    low = (f - hi.astype(F32)).astype(BF)
    factor = jnp.dot(jnp.concatenate([hi, low], 1), jnp.concatenate([spread, spread], 0), preferred_element_type=F32)
    attended = []
    for i in range(tiles):
        at = [(s * (tiles // 2) + i // 2) * per for s in range(2)]
        num = [parts_ref[:, a : a + per, :].astype(F32)[:, i % 2 * half : i % 2 * half + half] for a in at]
        num = jnp.concatenate(num, 1)
        attended.append(jnp.sum(num * factor[:, i * 128 : (i + 1) * 128].reshape(parts, per, 128), 0))
    gated = (gate_ref[...] * jnp.concatenate(attended, 1)).astype(BF)
    update = jnp.dot(gated, wout_ref[...], preferred_element_type=F32)
    out_ref[...] = update.reshape(out_ref.shape).astype(BF)


def near_swap(n):
    ring = lambda a, b, size: min((a - b) % size, (b - a) % size)
    table = []
    for c in range(n):
        cx, cyh, cco = c // 4, c // 2 % 2, c % 2
        cyl, cz = c // 8, c % 8

        def cost(j, i):
            hops = ring(cx, i // 4, 4) + ring(j % 8, cz, 8)
            hops += ring(cyh * 2 + j // 8, (i // 2 % 2) * 2 + cyl, 4)
            return 2 * hops + (cco != i % 2)

        for most in range(100):
            taken = {}

            def place(j, seen):
                for i in range(n):
                    if cost(j, i) <= most and i not in seen:
                        seen.add(i)
                        if i not in taken or place(taken[i], seen):
                            taken[i] = j
                            return True
                return False

            if all(place(j, set()) for j in range(n)):
                break
        table.append([taken[i] for i in range(n)])
    return table


def params(mib):
    return pltpu.CompilerParams(vmem_limit_bytes=mib << 20)


def shards(
    single,
    restype,
    restype_table,
    chain,
    live,
    pair,
    pair_gain,
    pair_weight,
    chain_bias,
    single_gain,
    w_qkvg,
    w_out,
):
    samples, tok, width = single.shape
    row_len, col_len, channels = pair.shape
    heads = chain_bias.shape[0]
    n_row, n_col = lax.axis_size("qrow"), lax.axis_size("kcol")
    shape = jax.ShapeDtypeStruct
    own = samples * tok

    stay = lambda *arrays: [pltpu.with_memory_space_constraint(x, pltpu.HBM) for x in arrays]
    hbm = lambda count: [pl.BlockSpec(memory_space=pltpu.HBM)] * count
    dma = pltpu.SemaphoreType.DMA
    normed, copies = pl.pallas_call(
        norm_kernel,
        name="norm",
        out_shape=(shape((own, width), BF), shape((n_col, own, width), BF)),
        in_specs=hbm(4),
        out_specs=(vmem(), vmem()),
        scratch_shapes=[
            pltpu.SMEM((tok,), jnp.int32),
            pltpu.VMEM((samples, tok, width), BF),
            pltpu.VMEM(restype_table.shape, BF),
            pltpu.VMEM((width,), F32),
            dma((4,)),
        ],
        compiler_params=params(4),
    )(*stay(restype, single, restype_table, single_gain))

    table = near_swap(n_row)
    swap = [(c * n_col + j, i * n_col + c) for c in range(n_row) for i, j in enumerate(table[c])]
    turned = lax.ppermute(normed, ("qrow", "kcol"), swap)
    row_tokens = lax.all_to_all(copies, "kcol", 0, 0)

    where = jnp.stack([lax.axis_index("qrow"), lax.axis_index("kcol")]).astype(jnp.int32)
    chunks = 4
    half = row_len // 2

    def bias_of(part):
        out = [shape((heads, half, col_len), F32)]
        scratch = [
            pltpu.SMEM(chain.shape, jnp.int32),
            pltpu.SMEM((heads,), F32),
            pltpu.VMEM((chain.shape[0] // col_len, col_len), jnp.int32),
            pltpu.VMEM((1, col_len), jnp.int32),
            pltpu.VMEM((1, channels), F32),
            pltpu.VMEM((heads, channels), F32),
            pltpu.VMEM((chunks, half // chunks, col_len, channels), BF),
            dma((6,)),
            dma((chunks,)),
        ]
        if part:
            out += [shape((own, width), F32), shape((width, 2 * width), BF)]
            scratch += [pltpu.VMEM((width, width), BF), dma((2,))]
        return pl.pallas_call(
            functools.partial(bias_kernel, part * half, part),
            name="bias_" + str(part),
            out_shape=out,
            in_specs=[smem(), vmem()] + hbm(7 + part),
            out_specs=[vmem()] * len(out),
            scratch_shapes=scratch,
            compiler_params=params(12 if part else 6),
            cost_estimate=pl.CostEstimate(flops=5 * 10**8, bytes_accessed=10 * 10**6, transcendentals=0),
        )(
            where,
            normed,
            *stay(
                chain,
                chain_bias,
                chain.reshape(-1, col_len),
                live.reshape(1, col_len),
                pair_gain.reshape(1, channels),
                pair_weight.T,
                pair,
                *[w_qkvg][:part],
            ),
        )

    (bias_a,) = bias_of(0)
    bias_b, gate, w_kv = bias_of(1)
    turned_copies = pl.pallas_call(
        copies_kernel,
        name="copies",
        out_shape=shape((n_row, own, width), BF),
        in_specs=[vmem(), pl.BlockSpec(memory_space=pl.ANY)],
        out_specs=vmem(),
        compiler_params=params(4),
    )(turned, bias_a)
    turned_copies, row_tokens = lax.optimization_barrier((turned_copies, row_tokens))
    col_tokens = lax.all_to_all(turned_copies, "qrow", 0, 0)

    order = jnp.asarray(table, jnp.int32).reshape(-1)
    rows = own * width // 128 + tok
    partial = pl.pallas_call(
        attend_kernel,
        name="attend",
        out_shape=shape((n_col, rows, 128), BF),
        in_specs=[smem()] * 2 + [vmem()] + hbm(1) + [vmem()] + hbm(3),
        out_specs=vmem(),
        scratch_shapes=[
            pltpu.VMEM(col_tokens.shape, BF),
            pltpu.VMEM((width, width), BF),
            pltpu.VMEM((heads, row_len, col_len), F32),
            dma((3 + n_row,)),
        ],
        compiler_params=params(16),
    )(where, order, row_tokens, *stay(col_tokens), w_kv, *stay(w_qkvg, bias_a, bias_b))

    gathered = lax.all_to_all(partial, "kcol", 0, 0)
    return pl.pallas_call(
        merge_kernel,
        name="merge",
        out_shape=shape((samples, tok, width), BF),
        in_specs=[vmem(), vmem(), vmem()],
        out_specs=vmem(),
        compiler_params=params(8),
    )(gathered, gate, w_out)


def solution(mesh):
    return jax.shard_map(
        shards,
        mesh=mesh,
        in_specs=(
            P(None, ("qrow", "kcol"), None),
            P(("qrow", "kcol")),
            P(),
            P(),
            P("kcol"),
            P("qrow", "kcol", None),
            P(),
            P(),
            P(),
            P(),
            P(),
            P(),
        ),
        out_specs=P(None, ("qrow", "kcol"), None),
        check_vma=False,
    )
```

```python
import functools
import math

import jax
import jax.numpy as jnp
from jax import lax
from jax.experimental import pallas as pl
from jax.experimental.pallas import tpu as pltpu
from jax.sharding import PartitionSpec as P

BF = jnp.bfloat16
F32 = jnp.float32
EPS = 1e-05


def vmem():
    return pl.BlockSpec(memory_space=pltpu.VMEM)


def smem():
    return pl.BlockSpec(memory_space=pltpu.SMEM)


def dot_nt(a, b):
    return lax.dot_general(a, b, (((1,), (1,)), ((), ())), preferred_element_type=F32)


def layer_norm(x):
    centred = x - jnp.mean(x, -1, keepdims=True)
    variance = jnp.mean(centred * centred, -1, keepdims=True)
    return centred * lax.rsqrt(variance + EPS)


def split3(x):
    hi = x.astype(BF)
    rest = x - hi.astype(F32)
    mid = rest.astype(BF)
    low = (rest - mid.astype(F32)).astype(BF)
    return hi, mid, low


def fetch(copies, sems):
    started = [pltpu.make_async_copy(src, dst, sems.at[i]) for i, (src, dst) in enumerate(copies)]
    for copy in started:
        copy.start()
    for copy in started:
        copy.wait()


def norm_kernel(
    restype_hbm, single_hbm, table_hbm, gain_hbm, normed_ref, copies_ref, restype_ref, single_ref, table_ref, gain_ref, sems
):
    fetch(
        [
            (restype_hbm, restype_ref),
            (single_hbm, single_ref),
            (table_hbm, table_ref),
            (gain_hbm, gain_ref),
        ],
        sems,
    )
    samples, tok, width = single_ref.shape
    kinds = table_ref.shape[0]
    row = lax.broadcasted_iota(jnp.int32, (tok, kinds), 0)
    col = lax.broadcasted_iota(jnp.int32, (tok, kinds), 1)
    kind = jnp.zeros((tok, kinds), jnp.int32)
    for t in range(tok):
        kind = jnp.where(row == t, restype_ref[t], kind)
    one_hot = jnp.where(kind == col, 1.0, 0.0).astype(BF)
    emb = jnp.dot(one_hot, table_ref[...], preferred_element_type=F32)
    x = single_ref[...].astype(F32) + emb[None]
    normed = layer_norm(x) * gain_ref[...].reshape(1, 1, width)
    normed = normed.reshape(samples * tok, width).astype(BF)
    normed_ref[...] = normed
    for j in range(copies_ref.shape[0]):
        copies_ref[j] = normed


def copies_kernel(one_ref, after_ref, copies_ref):
    for j in range(copies_ref.shape[0]):
        copies_ref[j] = one_ref[...]


def bias_kernel(start, ahead, where_ref, normed_ref, *refs):
    ins, refs = refs[: 7 + ahead], refs[7 + ahead :]
    pair_hbm = ins[6]
    out_ref, refs = refs[0], refs[1:]
    if ahead:
        (gate_ref, w_ref), refs = refs[:2], refs[2:]
    chain_ref, cbias_ref, chain_rows_ref, live_ref, gain_ref, weight_ref, pair_ref, sems, pair_sems = refs[:9]
    chunks, block, keys, channels = pair_ref.shape
    heads = weight_ref.shape[0]
    loads = [
        pltpu.make_async_copy(pair_hbm.at[pl.ds(start + i * block, block)], pair_ref.at[i], pair_sems.at[i])
        for i in range(chunks)
    ]
    for load in loads[:2]:
        load.start()
    small = list(zip(ins[:6], (chain_ref, cbias_ref, chain_rows_ref, live_ref, gain_ref, weight_ref)))
    small = [pltpu.make_async_copy(src, dst, sems.at[i]) for i, (src, dst) in enumerate(small)]
    for load in small + loads[2:]:
        load.start()
    if ahead:
        width = normed_ref.shape[1]
        wg_ref, w_sems = refs[9:]
        w_hbm = ins[7]
        load_g = pltpu.make_async_copy(w_hbm.at[:, pl.ds(3 * width, width)], wg_ref, w_sems.at[0])
        load_w = pltpu.make_async_copy(w_hbm.at[:, pl.ds(width, 2 * width)], w_ref, w_sems.at[1])
        load_g.start()
        load_w.start()
    for load in small:
        load.wait()
    weight = weight_ref[...] * gain_ref[...]
    lhs = jnp.concatenate(split3(weight), 0)
    total = jnp.sum(weight, -1, keepdims=True)
    row = lax.broadcasted_iota(jnp.int32, (heads, keys), 0)
    column = jnp.zeros((heads, keys), F32)
    for h in range(heads):
        column = jnp.where(row == h, cbias_ref[h], column)
    base = where_ref[0] * pair_hbm.shape[0] + start
    col_chain = chain_rows_ref[pl.ds(where_ref[1], 1), :]
    alive = jnp.broadcast_to(live_ref[...] == 1, (heads, keys))
    for i in range(chunks):
        loads[i].wait()
        for q in range(0, block, 2):
            turned = pair_ref[i, q : q + 2].reshape(2 * keys, channels).T
            x = turned.astype(F32)
            mean = jnp.sum(x, 0, keepdims=True) * (1.0 / channels)
            centred = x - mean
            variance = jnp.sum(centred * centred, 0, keepdims=True) * (1.0 / channels)
            res = jnp.dot(lhs, turned, preferred_element_type=F32)
            res = res[:heads] + res[heads : 2 * heads] + res[2 * heads :]
            res = (res - total * mean) * lax.rsqrt(variance + EPS)
            for k in range(2):
                at = i * block + q + k
                part = res[:, k * keys : (k + 1) * keys]
                same = col_chain == chain_ref[base + at]
                part = part + jnp.where(same, column, 0.0)
                out_ref[:, at, :] = jnp.where(alive, part, -1e30)
    if ahead:
        load_g.wait()
        pre = jnp.dot(normed_ref[...], wg_ref[...], preferred_element_type=F32)
        gate_ref[...] = jax.nn.sigmoid(pre)
        load_w.wait()


def attend_kernel(
    where_ref,
    order_ref,
    rows_ref,
    cols_hbm,
    wkv_ref,
    w_hbm,
    bias_a_hbm,
    bias_b_hbm,
    out_ref,
    x_ref,
    wq_ref,
    bias_ref,
    sems,
):
    parts, per, width = rows_ref.shape
    half = per // 2
    heads, queries, keys = bias_ref.shape
    few = queries // 2
    size = width // heads
    scale = 1.0 / math.sqrt(size)
    loads = [
        pltpu.make_async_copy(w_hbm.at[:, pl.ds(0, width)], wq_ref, sems.at[0]),
        pltpu.make_async_copy(bias_a_hbm, bias_ref.at[:, pl.ds(0, few)], sems.at[1]),
        pltpu.make_async_copy(bias_b_hbm, bias_ref.at[:, pl.ds(few, few)], sems.at[2]),
    ]
    tokens = [
        pltpu.make_async_copy(cols_hbm.at[i], x_ref.at[order_ref[where_ref[1] * parts + i]], sems.at[3 + i])
        for i in range(parts)
    ]
    for load in tokens + loads:
        load.start()
    for load in tokens:
        load.wait()

    def project(tokens, w):
        x = tokens[...].reshape(parts * per, width)
        return jnp.dot(x, w, preferred_element_type=F32).reshape(parts, 2, half, width)

    kf, vf = project(x_ref, wkv_ref[:, :width]), project(x_ref, wkv_ref[:, width:])
    for load in loads:
        load.wait()
    qf = project(rows_ref, wq_ref[...])
    span = 256
    wins = width // span

    def members(t):
        return [h for h in range(heads) if h * size < (t + 1) * span and (h + 1) * size > t * span]

    def mask_of(h, t):
        spot = lax.broadcasted_iota(jnp.int32, (1, span), 1) + t * span
        return jnp.where((spot >= h * size) & (spot < (h + 1) * size), 1.0, 0.0).astype(BF)

    lane = lax.broadcasted_iota(jnp.int32, (queries, 128), 1)
    stats = jnp.zeros((queries, 128), F32)
    for s in range(2):
        q = qf[:, s].reshape(queries, width).astype(BF)
        k = kf[:, s].reshape(keys, width).astype(BF)
        v = vf[:, s].reshape(keys, width).astype(BF)
        raw = {}
        for t in range(wins):
            cut = slice(t * span, (t + 1) * span)
            lhs = jnp.concatenate([q[:, cut] * mask_of(h, t) for h in members(t)], 0)
            res = dot_nt(lhs, k[:, cut])
            for i, h in enumerate(members(t)):
                piece = res[i * queries : (i + 1) * queries]
                raw[h] = raw[h] + piece if h in raw else piece
        tops = jnp.zeros((queries, 128), F32)
        tots = jnp.zeros((queries, 128), F32)
        rounded = []
        for h in range(heads):
            sc = raw[h] * scale + bias_ref[h]
            top = jnp.max(sc, -1, keepdims=True)
            w = jnp.exp(sc - top)
            rounded.append(w.astype(BF))
            tots = jnp.where(lane == h, jnp.sum(w, -1, keepdims=True), tots)
            tops = jnp.where(lane == h, top, tops)
        for t in range(wins):
            cut = slice(t * span, (t + 1) * span)
            o = jnp.dot(
                jnp.concatenate([rounded[h] for h in members(t)], 1),
                jnp.concatenate([v[:, cut] * mask_of(h, t) for h in members(t)], 0),
                preferred_element_type=F32,
            )
            at = (s * wins + t) * per
            tiles = [o[:, i * 128 : (i + 1) * 128].reshape(parts, half, 128) for i in range(2)]
            out_ref[:, at : at + per, :] = jnp.concatenate(tiles, 1).astype(BF)
        hi, mid, low = split3(tops)
        mine = hi.astype(F32)
        for i, p in enumerate((mid.astype(F32), low.astype(F32), tots)):
            mine = mine + pltpu.roll(p, heads * (i + 1), 1)
        stats = stats + (pltpu.roll(mine, 64, 1) if s else mine)
    out_ref[:, 2 * wins * per :, :] = stats.reshape(parts, half, 128).astype(BF)


def merge_kernel(parts_ref, gate_ref, wout_ref, out_ref):
    parts, rows, _ = parts_ref.shape
    per, width = gate_ref.shape
    half = per // 2
    tiles = width // 128
    heads = 16
    size = width // heads
    both = parts_ref[:, tiles * per :, :].astype(F32).reshape(parts, 1, half, 128)
    other = pltpu.roll(both.reshape(parts * half, 128), 64, 1).reshape(parts, 1, half, 128)
    st = jnp.concatenate([both, other], 1).reshape(parts * per, 128)
    top = st + pltpu.roll(st, 128 - heads, 1) + pltpu.roll(st, 128 - 2 * heads, 1)
    tot = pltpu.roll(st, 128 - 3 * heads, 1)
    lane = lax.broadcasted_iota(jnp.int32, (parts * per, 128), 1)
    top = jnp.where(lane < heads, top, 0.0).reshape(parts, per, 128)
    tot = jnp.where(lane < heads, tot, 1.0).reshape(parts, per, 128)
    e = jnp.exp(top - jnp.max(top, 0, keepdims=True))
    f = e / jnp.sum(e * tot, 0, keepdims=True)
    f = jnp.where(lane < heads, f.reshape(parts * per, 128), 0.0)
    hrow = lax.broadcasted_iota(jnp.int32, (128, width), 0) * size
    col = lax.broadcasted_iota(jnp.int32, (128, width), 1)
    spread = jnp.where((col >= hrow) & (col < hrow + size), 1.0, 0.0).astype(BF)
    hi = f.astype(BF)
    low = (f - hi.astype(F32)).astype(BF)
    factor = jnp.dot(jnp.concatenate([hi, low], 1), jnp.concatenate([spread, spread], 0), preferred_element_type=F32)
    attended = []
    for i in range(tiles):
        at = [(s * (tiles // 2) + i // 2) * per for s in range(2)]
        num = [parts_ref[:, a : a + per, :].astype(F32)[:, i % 2 * half : i % 2 * half + half] for a in at]
        num = jnp.concatenate(num, 1)
        attended.append(jnp.sum(num * factor[:, i * 128 : (i + 1) * 128].reshape(parts, per, 128), 0))
    gated = (gate_ref[...] * jnp.concatenate(attended, 1)).astype(BF)
    update = jnp.dot(gated, wout_ref[...], preferred_element_type=F32)
    out_ref[...] = update.reshape(out_ref.shape).astype(BF)


def near_swap(n):
    ring = lambda a, b, size: min((a - b) % size, (b - a) % size)
    table = []
    for c in range(n):
        cx, cyh, cco = c // 4, c // 2 % 2, c % 2
        cyl, cz = c // 8, c % 8

        def cost(j, i):
            hops = ring(cx, i // 4, 4) + ring(j % 8, cz, 8)
            hops += ring(cyh * 2 + j // 8, (i // 2 % 2) * 2 + cyl, 4)
            return 2 * hops + (cco != i % 2)

        for most in range(100):
            taken = {}

            def place(j, seen):
                for i in range(n):
                    if cost(j, i) <= most and i not in seen:
                        seen.add(i)
                        if i not in taken or place(taken[i], seen):
                            taken[i] = j
                            return True
                return False

            if all(place(j, set()) for j in range(n)):
                break
        table.append([taken[i] for i in range(n)])
    return table


def params(mib):
    return pltpu.CompilerParams(vmem_limit_bytes=mib << 20)


def shards(
    single,
    restype,
    restype_table,
    chain,
    live,
    pair,
    pair_gain,
    pair_weight,
    chain_bias,
    single_gain,
    w_qkvg,
    w_out,
):
    samples, tok, width = single.shape
    row_len, col_len, channels = pair.shape
    heads = chain_bias.shape[0]
    n_row, n_col = lax.axis_size("qrow"), lax.axis_size("kcol")
    shape = jax.ShapeDtypeStruct
    own = samples * tok

    stay = lambda *arrays: [pltpu.with_memory_space_constraint(x, pltpu.HBM) for x in arrays]
    hbm = lambda count: [pl.BlockSpec(memory_space=pltpu.HBM)] * count
    dma = pltpu.SemaphoreType.DMA
    normed, copies = pl.pallas_call(
        norm_kernel,
        name="norm",
        out_shape=(shape((own, width), BF), shape((n_col, own, width), BF)),
        in_specs=hbm(4),
        out_specs=(vmem(), vmem()),
        scratch_shapes=[
            pltpu.SMEM((tok,), jnp.int32),
            pltpu.VMEM((samples, tok, width), BF),
            pltpu.VMEM(restype_table.shape, BF),
            pltpu.VMEM((width,), F32),
            dma((4,)),
        ],
        compiler_params=params(4),
    )(*stay(restype, single, restype_table, single_gain))

    table = near_swap(n_row)
    swap = [(c * n_col + j, i * n_col + c) for c in range(n_row) for i, j in enumerate(table[c])]
    turned = lax.ppermute(normed, ("qrow", "kcol"), swap)
    row_tokens = lax.all_to_all(copies, "kcol", 0, 0)

    where = jnp.stack([lax.axis_index("qrow"), lax.axis_index("kcol")]).astype(jnp.int32)
    chunks = 4
    half = row_len // 2

    def bias_of(part):
        out = [pltpu.HBM((heads, half, col_len), F32)]
        scratch = [
            pltpu.SMEM(chain.shape, jnp.int32),
            pltpu.SMEM((heads,), F32),
            pltpu.VMEM((chain.shape[0] // col_len, col_len), jnp.int32),
            pltpu.VMEM((1, col_len), jnp.int32),
            pltpu.VMEM((1, channels), F32),
            pltpu.VMEM((heads, channels), F32),
            pltpu.VMEM((chunks, half // chunks, col_len, channels), BF),
            dma((6,)),
            dma((chunks,)),
        ]
        if part:
            out += [shape((own, width), F32), shape((width, 2 * width), BF)]
            scratch += [pltpu.VMEM((width, width), BF), dma((2,))]
        return pl.pallas_call(
            functools.partial(bias_kernel, part * half, part),
            name="bias_" + str(part),
            out_shape=out,
            in_specs=[smem(), vmem()] + hbm(7 + part),
            out_specs=[vmem()] * len(out),
            scratch_shapes=scratch,
            compiler_params=params(12 if part else 6),
            cost_estimate=pl.CostEstimate(flops=5 * 10**8, bytes_accessed=10 * 10**6, transcendentals=0),
        )(
            where,
            normed,
            *stay(
                chain,
                chain_bias,
                chain.reshape(-1, col_len),
                live.reshape(1, col_len),
                pair_gain.reshape(1, channels),
                pair_weight.T,
                pair,
                *[w_qkvg][:part],
            ),
        )

    (bias_a,) = bias_of(0)
    bias_b, gate, w_kv = bias_of(1)
    turned_copies = pl.pallas_call(
        copies_kernel,
        name="copies",
        out_shape=shape((n_row, own, width), BF),
        in_specs=[vmem()] + hbm(1),
        out_specs=vmem(),
        compiler_params=params(4),
    )(turned, *stay(bias_a))
    turned_copies, row_tokens = lax.optimization_barrier((turned_copies, row_tokens))
    col_tokens = lax.all_to_all(turned_copies, "qrow", 0, 0)

    order = jnp.asarray(table, jnp.int32).reshape(-1)
    rows = own * width // 128 + tok
    partial = pl.pallas_call(
        attend_kernel,
        name="attend",
        out_shape=shape((n_col, rows, 128), BF),
        in_specs=[smem()] * 2 + [vmem()] + hbm(1) + [vmem()] + hbm(3),
        out_specs=vmem(),
        scratch_shapes=[
            pltpu.VMEM(col_tokens.shape, BF),
            pltpu.VMEM((width, width), BF),
            pltpu.VMEM((heads, row_len, col_len), F32),
            dma((3 + n_row,)),
        ],
        compiler_params=params(16),
    )(where, order, row_tokens, col_tokens, w_kv, *stay(w_qkvg, bias_a, bias_b))

    gathered = lax.all_to_all(partial, "kcol", 0, 0)
    return pl.pallas_call(
        merge_kernel,
        name="merge",
        out_shape=shape((samples, tok, width), BF),
        in_specs=[vmem(), vmem(), vmem()],
        out_specs=vmem(),
        compiler_params=params(8),
    )(gathered, gate, w_out)


def solution(mesh):
    return jax.shard_map(
        shards,
        mesh=mesh,
        in_specs=(
            P(None, ("qrow", "kcol"), None),
            P(("qrow", "kcol")),
            P(),
            P(),
            P("kcol"),
            P("qrow", "kcol", None),
            P(),
            P(),
            P(),
            P(),
            P(),
            P(),
        ),
        out_specs=P(None, ("qrow", "kcol"), None),
        check_vma=False,
    )
```

```python
import functools
import math

import jax
import jax.numpy as jnp
from jax import lax
from jax.experimental import pallas as pl
from jax.experimental.pallas import tpu as pltpu
from jax.sharding import PartitionSpec as P

BF = jnp.bfloat16
F32 = jnp.float32
EPS = 1e-05


def vmem():
    return pl.BlockSpec(memory_space=pltpu.VMEM)


def smem():
    return pl.BlockSpec(memory_space=pltpu.SMEM)


def dot_nt(a, b):
    return lax.dot_general(a, b, (((1,), (1,)), ((), ())), preferred_element_type=F32)


def layer_norm(x):
    centred = x - jnp.mean(x, -1, keepdims=True)
    variance = jnp.mean(centred * centred, -1, keepdims=True)
    return centred * lax.rsqrt(variance + EPS)


def split3(x):
    hi = x.astype(BF)
    rest = x - hi.astype(F32)
    mid = rest.astype(BF)
    low = (rest - mid.astype(F32)).astype(BF)
    return hi, mid, low


def fetch(copies, sems):
    started = [pltpu.make_async_copy(src, dst, sems.at[i]) for i, (src, dst) in enumerate(copies)]
    for copy in started:
        copy.start()
    for copy in started:
        copy.wait()


def norm_kernel(
    restype_hbm, single_hbm, table_hbm, gain_hbm, normed_ref, copies_ref, restype_ref, single_ref, table_ref, gain_ref, sems
):
    fetch(
        [
            (restype_hbm, restype_ref),
            (single_hbm, single_ref),
            (table_hbm, table_ref),
            (gain_hbm, gain_ref),
        ],
        sems,
    )
    samples, tok, width = single_ref.shape
    kinds = table_ref.shape[0]
    row = lax.broadcasted_iota(jnp.int32, (tok, kinds), 0)
    col = lax.broadcasted_iota(jnp.int32, (tok, kinds), 1)
    kind = jnp.zeros((tok, kinds), jnp.int32)
    for t in range(tok):
        kind = jnp.where(row == t, restype_ref[t], kind)
    one_hot = jnp.where(kind == col, 1.0, 0.0).astype(BF)
    emb = jnp.dot(one_hot, table_ref[...], preferred_element_type=F32)
    x = single_ref[...].astype(F32) + emb[None]
    normed = layer_norm(x) * gain_ref[...].reshape(1, 1, width)
    normed = normed.reshape(samples * tok, width).astype(BF)
    normed_ref[...] = normed
    for j in range(copies_ref.shape[0]):
        copies_ref[j] = normed


def copies_kernel(one_ref, after_ref, copies_ref):
    for j in range(copies_ref.shape[0]):
        copies_ref[j] = one_ref[...]


def bias_kernel(start, late, tokens_ref, where_ref, *refs):
    ins, refs = refs[:8], refs[8:]
    pair_hbm, w_hbm = ins[6:]
    out_ref, extra_ref, refs = refs[0], refs[1], refs[2:]
    if late:
        w_ref, refs = refs[0], refs[1:]
    chain_ref, cbias_ref, chain_rows_ref, live_ref, gain_ref, weight_ref, pair_ref, sems, pair_sems = refs[:9]
    mine_ref, w_sems = refs[9:]
    chunks, block, keys, channels = pair_ref.shape
    heads = weight_ref.shape[0]
    width = mine_ref.shape[0]
    loads = [
        pltpu.make_async_copy(pair_hbm.at[pl.ds(start + i * block, block)], pair_ref.at[i], pair_sems.at[i])
        for i in range(chunks)
    ]
    for load in loads[:2]:
        load.start()
    small = list(zip(ins[:6], (chain_ref, cbias_ref, chain_rows_ref, live_ref, gain_ref, weight_ref)))
    small = [pltpu.make_async_copy(src, dst, sems.at[i]) for i, (src, dst) in enumerate(small)]
    for load in small + loads[2:]:
        load.start()
    own = 0 if late else 3 * width
    load_mine = pltpu.make_async_copy(w_hbm.at[:, pl.ds(own, width)], mine_ref, w_sems.at[0])
    load_mine.start()
    if late:
        load_w = pltpu.make_async_copy(w_hbm.at[:, pl.ds(width, 2 * width)], w_ref, w_sems.at[1])
        load_w.start()
    for load in small:
        load.wait()
    weight = weight_ref[...] * gain_ref[...]
    lhs = jnp.concatenate(split3(weight), 0)
    total = jnp.sum(weight, -1, keepdims=True)
    row = lax.broadcasted_iota(jnp.int32, (heads, keys), 0)
    column = jnp.zeros((heads, keys), F32)
    for h in range(heads):
        column = jnp.where(row == h, cbias_ref[h], column)
    base = where_ref[0] * pair_hbm.shape[0] + start
    col_chain = chain_rows_ref[pl.ds(where_ref[1], 1), :]
    alive = jnp.broadcast_to(live_ref[...] == 1, (heads, keys))
    for i in range(chunks):
        loads[i].wait()
        for q in range(0, block, 2):
            turned = pair_ref[i, q : q + 2].reshape(2 * keys, channels).T
            x = turned.astype(F32)
            mean = jnp.sum(x, 0, keepdims=True) * (1.0 / channels)
            centred = x - mean
            variance = jnp.sum(centred * centred, 0, keepdims=True) * (1.0 / channels)
            res = jnp.dot(lhs, turned, preferred_element_type=F32)
            res = res[:heads] + res[heads : 2 * heads] + res[2 * heads :]
            res = (res - total * mean) * lax.rsqrt(variance + EPS)
            for k in range(2):
                at = i * block + q + k
                part = res[:, k * keys : (k + 1) * keys]
                same = col_chain == chain_ref[base + at]
                part = part + jnp.where(same, column, 0.0)
                out_ref[:, at, :] = jnp.where(alive, part, -1e30)
    load_mine.wait()
    parts, per, _ = tokens_ref.shape
    res = jnp.dot(tokens_ref[...].reshape(parts * per, width), mine_ref[...], preferred_element_type=F32)
    if late:
        res = res.reshape(parts, 2, per // 2, width)
        for s in range(2):
            extra_ref[s] = res[:, s].reshape(parts * per // 2, width).astype(BF)
        load_w.wait()
    else:
        extra_ref[...] = jax.nn.sigmoid(res)


def attend_kernel(
    where_ref, order_ref, cols_ref, wkv_ref, q_ref, bias_a_hbm, bias_b_hbm, out_ref, x_ref, bias_ref, sems
):
    parts, per, width = cols_ref.shape
    half = per // 2
    heads, queries, keys = bias_ref.shape
    few = queries // 2
    size = width // heads
    scale = 1.0 / math.sqrt(size)
    loads = [
        pltpu.make_async_copy(bias_a_hbm, bias_ref.at[:, pl.ds(0, few)], sems.at[0]),
        pltpu.make_async_copy(bias_b_hbm, bias_ref.at[:, pl.ds(few, few)], sems.at[1]),
    ]
    for load in loads:
        load.start()
    for i in range(parts):
        x_ref[pl.ds(order_ref[where_ref[1] * parts + i], 1)] = cols_ref[pl.ds(i, 1)]
    x = x_ref[...].reshape(parts * per, width)

    def project(w):
        return jnp.dot(x, w, preferred_element_type=F32).reshape(parts, 2, half, width)

    kf, vf = project(wkv_ref[:, :width]), project(wkv_ref[:, width:])
    for load in loads:
        load.wait()
    span = 256
    wins = width // span

    def members(t):
        return [h for h in range(heads) if h * size < (t + 1) * span and (h + 1) * size > t * span]

    def mask_of(h, t):
        spot = lax.broadcasted_iota(jnp.int32, (1, span), 1) + t * span
        return jnp.where((spot >= h * size) & (spot < (h + 1) * size), 1.0, 0.0).astype(BF)

    lane = lax.broadcasted_iota(jnp.int32, (queries, 128), 1)
    stats = jnp.zeros((queries, 128), F32)
    for s in range(2):
        q = q_ref[s]
        k = kf[:, s].reshape(keys, width).astype(BF)
        v = vf[:, s].reshape(keys, width).astype(BF)
        raw = {}
        for t in range(wins):
            cut = slice(t * span, (t + 1) * span)
            lhs = jnp.concatenate([q[:, cut] * mask_of(h, t) for h in members(t)], 0)
            res = dot_nt(lhs, k[:, cut])
            for i, h in enumerate(members(t)):
                piece = res[i * queries : (i + 1) * queries]
                raw[h] = raw[h] + piece if h in raw else piece
        tops = jnp.zeros((queries, 128), F32)
        tots = jnp.zeros((queries, 128), F32)
        rounded = []
        for h in range(heads):
            sc = raw[h] * scale + bias_ref[h]
            top = jnp.max(sc, -1, keepdims=True)
            w = jnp.exp(sc - top)
            rounded.append(w.astype(BF))
            tots = jnp.where(lane == h, jnp.sum(w, -1, keepdims=True), tots)
            tops = jnp.where(lane == h, top, tops)
        for t in range(wins):
            cut = slice(t * span, (t + 1) * span)
            o = jnp.dot(
                jnp.concatenate([rounded[h] for h in members(t)], 1),
                jnp.concatenate([v[:, cut] * mask_of(h, t) for h in members(t)], 0),
                preferred_element_type=F32,
            )
            at = (s * wins + t) * per
            tiles = [o[:, i * 128 : (i + 1) * 128].reshape(parts, half, 128) for i in range(2)]
            out_ref[:, at : at + per, :] = jnp.concatenate(tiles, 1).astype(BF)
        hi, mid, low = split3(tops)
        mine = hi.astype(F32)
        for i, p in enumerate((mid.astype(F32), low.astype(F32), tots)):
            mine = mine + pltpu.roll(p, heads * (i + 1), 1)
        stats = stats + (pltpu.roll(mine, 64, 1) if s else mine)
    out_ref[:, 2 * wins * per :, :] = stats.reshape(parts, half, 128).astype(BF)


def merge_kernel(parts_ref, gate_ref, wout_ref, out_ref):
    parts, rows, _ = parts_ref.shape
    per, width = gate_ref.shape
    half = per // 2
    tiles = width // 128
    heads = 16
    size = width // heads
    both = parts_ref[:, tiles * per :, :].astype(F32).reshape(parts, 1, half, 128)
    other = pltpu.roll(both.reshape(parts * half, 128), 64, 1).reshape(parts, 1, half, 128)
    st = jnp.concatenate([both, other], 1).reshape(parts * per, 128)
    top = st + pltpu.roll(st, 128 - heads, 1) + pltpu.roll(st, 128 - 2 * heads, 1)
    tot = pltpu.roll(st, 128 - 3 * heads, 1)
    lane = lax.broadcasted_iota(jnp.int32, (parts * per, 128), 1)
    top = jnp.where(lane < heads, top, 0.0).reshape(parts, per, 128)
    tot = jnp.where(lane < heads, tot, 1.0).reshape(parts, per, 128)
    e = jnp.exp(top - jnp.max(top, 0, keepdims=True))
    f = e / jnp.sum(e * tot, 0, keepdims=True)
    f = jnp.where(lane < heads, f.reshape(parts * per, 128), 0.0)
    hrow = lax.broadcasted_iota(jnp.int32, (128, width), 0) * size
    col = lax.broadcasted_iota(jnp.int32, (128, width), 1)
    spread = jnp.where((col >= hrow) & (col < hrow + size), 1.0, 0.0).astype(BF)
    hi = f.astype(BF)
    low = (f - hi.astype(F32)).astype(BF)
    factor = jnp.dot(jnp.concatenate([hi, low], 1), jnp.concatenate([spread, spread], 0), preferred_element_type=F32)
    attended = []
    for i in range(tiles):
        at = [(s * (tiles // 2) + i // 2) * per for s in range(2)]
        num = [parts_ref[:, a : a + per, :].astype(F32)[:, i % 2 * half : i % 2 * half + half] for a in at]
        num = jnp.concatenate(num, 1)
        attended.append(jnp.sum(num * factor[:, i * 128 : (i + 1) * 128].reshape(parts, per, 128), 0))
    gated = (gate_ref[...] * jnp.concatenate(attended, 1)).astype(BF)
    update = jnp.dot(gated, wout_ref[...], preferred_element_type=F32)
    out_ref[...] = update.reshape(out_ref.shape).astype(BF)


def near_swap(n):
    ring = lambda a, b, size: min((a - b) % size, (b - a) % size)
    table = []
    for c in range(n):
        cx, cyh, cco = c // 4, c // 2 % 2, c % 2
        cyl, cz = c // 8, c % 8

        def cost(j, i):
            hops = ring(cx, i // 4, 4) + ring(j % 8, cz, 8)
            hops += ring(cyh * 2 + j // 8, (i // 2 % 2) * 2 + cyl, 4)
            return 2 * hops + (cco != i % 2)

        for most in range(100):
            taken = {}

            def place(j, seen):
                for i in range(n):
                    if cost(j, i) <= most and i not in seen:
                        seen.add(i)
                        if i not in taken or place(taken[i], seen):
                            taken[i] = j
                            return True
                return False

            if all(place(j, set()) for j in range(n)):
                break
        table.append([taken[i] for i in range(n)])
    return table


def params(mib):
    return pltpu.CompilerParams(vmem_limit_bytes=mib << 20)


def shards(
    single,
    restype,
    restype_table,
    chain,
    live,
    pair,
    pair_gain,
    pair_weight,
    chain_bias,
    single_gain,
    w_qkvg,
    w_out,
):
    samples, tok, width = single.shape
    row_len, col_len, channels = pair.shape
    heads = chain_bias.shape[0]
    n_row, n_col = lax.axis_size("qrow"), lax.axis_size("kcol")
    shape = jax.ShapeDtypeStruct
    own = samples * tok

    stay = lambda *arrays: [pltpu.with_memory_space_constraint(x, pltpu.HBM) for x in arrays]
    hbm = lambda count: [pl.BlockSpec(memory_space=pltpu.HBM)] * count
    dma = pltpu.SemaphoreType.DMA
    normed, copies = pl.pallas_call(
        norm_kernel,
        name="norm",
        out_shape=(shape((own, width), BF), shape((n_col, own, width), BF)),
        in_specs=hbm(4),
        out_specs=(vmem(), vmem()),
        scratch_shapes=[
            pltpu.SMEM((tok,), jnp.int32),
            pltpu.VMEM((samples, tok, width), BF),
            pltpu.VMEM(restype_table.shape, BF),
            pltpu.VMEM((width,), F32),
            dma((4,)),
        ],
        compiler_params=params(4),
    )(*stay(restype, single, restype_table, single_gain))

    table = near_swap(n_row)
    swap = [(c * n_col + j, i * n_col + c) for c in range(n_row) for i, j in enumerate(table[c])]
    turned = lax.ppermute(normed, ("qrow", "kcol"), swap)
    row_tokens = lax.all_to_all(copies, "kcol", 0, 0)

    where = jnp.stack([lax.axis_index("qrow"), lax.axis_index("kcol")]).astype(jnp.int32)
    chunks = 4
    half = row_len // 2

    def bias_of(late, tokens):
        out = [pltpu.HBM((heads, half, col_len), F32)]
        out += [shape((samples, row_len, width), BF) if late else pltpu.HBM((own, width), F32)]
        out += [shape((width, 2 * width), BF)] * late
        return pl.pallas_call(
            functools.partial(bias_kernel, late * half, late),
            name="bias_" + str(late),
            out_shape=out,
            in_specs=[vmem(), smem()] + hbm(8),
            out_specs=[vmem()] * len(out),
            scratch_shapes=[
                pltpu.SMEM(chain.shape, jnp.int32),
                pltpu.SMEM((heads,), F32),
                pltpu.VMEM((chain.shape[0] // col_len, col_len), jnp.int32),
                pltpu.VMEM((1, col_len), jnp.int32),
                pltpu.VMEM((1, channels), F32),
                pltpu.VMEM((heads, channels), F32),
                pltpu.VMEM((chunks, half // chunks, col_len, channels), BF),
                dma((6,)),
                dma((chunks,)),
                pltpu.VMEM((width, width), BF),
                dma((2,)),
            ],
            compiler_params=params(12 if late else 8),
            cost_estimate=pl.CostEstimate(flops=5 * 10**8, bytes_accessed=10 * 10**6, transcendentals=0),
        )(
            tokens,
            where,
            *stay(
                chain,
                chain_bias,
                chain.reshape(-1, col_len),
                live.reshape(1, col_len),
                pair_gain.reshape(1, channels),
                pair_weight.T,
                pair,
                w_qkvg,
            ),
        )

    bias_a, gate = bias_of(0, normed[None])
    bias_b, queries, w_kv = bias_of(1, row_tokens)
    turned_copies = pl.pallas_call(
        copies_kernel,
        name="copies",
        out_shape=shape((n_row, own, width), BF),
        in_specs=[vmem()] + hbm(1),
        out_specs=vmem(),
        compiler_params=params(4),
    )(turned, *stay(bias_a))
    turned_copies, row_tokens = lax.optimization_barrier((turned_copies, row_tokens))
    col_tokens = lax.all_to_all(turned_copies, "qrow", 0, 0)

    order = jnp.asarray(table, jnp.int32).reshape(-1)
    rows = own * width // 128 + tok
    partial = pl.pallas_call(
        attend_kernel,
        name="attend",
        out_shape=shape((n_col, rows, 128), BF),
        in_specs=[smem()] * 2 + [vmem()] * 3 + hbm(2),
        out_specs=vmem(),
        scratch_shapes=[
            pltpu.VMEM(col_tokens.shape, BF),
            pltpu.VMEM((heads, row_len, col_len), F32),
            dma((2,)),
        ],
        compiler_params=params(16),
    )(where, order, col_tokens, w_kv, queries, *stay(bias_a, bias_b))

    gathered = lax.all_to_all(partial, "kcol", 0, 0)
    return pl.pallas_call(
        merge_kernel,
        name="merge",
        out_shape=shape((samples, tok, width), BF),
        in_specs=[vmem(), vmem(), vmem()],
        out_specs=vmem(),
        compiler_params=params(8),
    )(gathered, gate, w_out)


def solution(mesh):
    return jax.shard_map(
        shards,
        mesh=mesh,
        in_specs=(
            P(None, ("qrow", "kcol"), None),
            P(("qrow", "kcol")),
            P(),
            P(),
            P("kcol"),
            P("qrow", "kcol", None),
            P(),
            P(),
            P(),
            P(),
            P(),
            P(),
        ),
        out_specs=P(None, ("qrow", "kcol"), None),
        check_vma=False,
    )
```

```python
import functools
import math

import jax
import jax.numpy as jnp
from jax import lax
from jax.experimental import pallas as pl
from jax.experimental.pallas import tpu as pltpu
from jax.sharding import PartitionSpec as P

BF = jnp.bfloat16
F32 = jnp.float32
EPS = 1e-05


def vmem():
    return pl.BlockSpec(memory_space=pltpu.VMEM)


def smem():
    return pl.BlockSpec(memory_space=pltpu.SMEM)


def dot_nt(a, b):
    return lax.dot_general(a, b, (((1,), (1,)), ((), ())), preferred_element_type=F32)


def layer_norm(x):
    centred = x - jnp.mean(x, -1, keepdims=True)
    variance = jnp.mean(centred * centred, -1, keepdims=True)
    return centred * lax.rsqrt(variance + EPS)


def split3(x):
    hi = x.astype(BF)
    rest = x - hi.astype(F32)
    mid = rest.astype(BF)
    low = (rest - mid.astype(F32)).astype(BF)
    return hi, mid, low


def fetch(copies, sems):
    started = [pltpu.make_async_copy(src, dst, sems.at[i]) for i, (src, dst) in enumerate(copies)]
    for copy in started:
        copy.start()
    for copy in started:
        copy.wait()


def norm_kernel(
    restype_hbm, single_hbm, table_hbm, gain_hbm, normed_ref, copies_ref, restype_ref, single_ref, table_ref, gain_ref, sems
):
    fetch(
        [
            (restype_hbm, restype_ref),
            (single_hbm, single_ref),
            (table_hbm, table_ref),
            (gain_hbm, gain_ref),
        ],
        sems,
    )
    samples, tok, width = single_ref.shape
    kinds = table_ref.shape[0]
    row = lax.broadcasted_iota(jnp.int32, (tok, kinds), 0)
    col = lax.broadcasted_iota(jnp.int32, (tok, kinds), 1)
    kind = jnp.zeros((tok, kinds), jnp.int32)
    for t in range(tok):
        kind = jnp.where(row == t, restype_ref[t], kind)
    one_hot = jnp.where(kind == col, 1.0, 0.0).astype(BF)
    emb = jnp.dot(one_hot, table_ref[...], preferred_element_type=F32)
    x = single_ref[...].astype(F32) + emb[None]
    normed = layer_norm(x) * gain_ref[...].reshape(1, 1, width)
    normed = normed.reshape(samples * tok, width).astype(BF)
    normed_ref[...] = normed
    for j in range(copies_ref.shape[0]):
        copies_ref[j] = normed


def pack_kernel(cols_ref, own_ref, after_ref, out_ref):
    per = own_ref.shape[0]
    for c in range(out_ref.shape[0]):
        out_ref[c, :per] = cols_ref[c]
        out_ref[c, per:] = own_ref[...]


def bias_kernel(start, late, own_ref, where_ref, *refs):
    ins, refs = refs[:8], refs[8:]
    pair_hbm, w_hbm = ins[6:]
    out_ref, extra_ref, refs = refs[0], refs[1], refs[2:]
    chain_ref, cbias_ref, chain_rows_ref, live_ref, gain_ref, weight_ref, pair_ref, sems, pair_sems = refs[:9]
    w_ref, w_sem = refs[9:] if not late else (extra_ref, refs[9])
    chunks, block, keys, channels = pair_ref.shape
    heads = weight_ref.shape[0]
    width = own_ref.shape[1]
    loads = [
        pltpu.make_async_copy(pair_hbm.at[pl.ds(start + i * block, block)], pair_ref.at[i], pair_sems.at[i])
        for i in range(chunks)
    ]
    for load in loads[:2]:
        load.start()
    small = list(zip(ins[:6], (chain_ref, cbias_ref, chain_rows_ref, live_ref, gain_ref, weight_ref)))
    small = [pltpu.make_async_copy(src, dst, sems.at[i]) for i, (src, dst) in enumerate(small)]
    for load in small + loads[2:]:
        load.start()
    place = pl.ds(width, 2 * width) if late else pl.ds(3 * width, width)
    load_w = pltpu.make_async_copy(w_hbm.at[:, place], w_ref, w_sem.at[0])
    load_w.start()
    for load in small:
        load.wait()
    weight = weight_ref[...] * gain_ref[...]
    lhs = jnp.concatenate(split3(weight), 0)
    total = jnp.sum(weight, -1, keepdims=True)
    row = lax.broadcasted_iota(jnp.int32, (heads, keys), 0)
    column = jnp.zeros((heads, keys), F32)
    for h in range(heads):
        column = jnp.where(row == h, cbias_ref[h], column)
    base = where_ref[0] * pair_hbm.shape[0] + start
    col_chain = chain_rows_ref[pl.ds(where_ref[1], 1), :]
    alive = jnp.broadcast_to(live_ref[...] == 1, (heads, keys))
    for i in range(chunks):
        loads[i].wait()
        for q in range(0, block, 2):
            turned = pair_ref[i, q : q + 2].reshape(2 * keys, channels).T
            x = turned.astype(F32)
            mean = jnp.sum(x, 0, keepdims=True) * (1.0 / channels)
            centred = x - mean
            variance = jnp.sum(centred * centred, 0, keepdims=True) * (1.0 / channels)
            res = jnp.dot(lhs, turned, preferred_element_type=F32)
            res = res[:heads] + res[heads : 2 * heads] + res[2 * heads :]
            res = (res - total * mean) * lax.rsqrt(variance + EPS)
            for k in range(2):
                at = i * block + q + k
                part = res[:, k * keys : (k + 1) * keys]
                same = col_chain == chain_ref[base + at]
                part = part + jnp.where(same, column, 0.0)
                out_ref[:, at, :] = jnp.where(alive, part, -1e30)
    load_w.wait()
    if not late:
        pre = jnp.dot(own_ref[...], w_ref[...], preferred_element_type=F32)
        extra_ref[...] = jax.nn.sigmoid(pre)


def attend_kernel(tokens_ref, wkv_ref, w_hbm, bias_a_hbm, bias_b_hbm, out_ref, wq_ref, bias_ref, sems):
    parts, per, width = tokens_ref.shape
    per = per // 2
    half = per // 2
    heads, queries, keys = bias_ref.shape
    few = queries // 2
    size = width // heads
    scale = 1.0 / math.sqrt(size)
    loads = [
        pltpu.make_async_copy(w_hbm.at[:, pl.ds(0, width)], wq_ref, sems.at[0]),
        pltpu.make_async_copy(bias_a_hbm, bias_ref.at[:, pl.ds(0, few)], sems.at[1]),
        pltpu.make_async_copy(bias_b_hbm, bias_ref.at[:, pl.ds(few, few)], sems.at[2]),
    ]
    for load in loads:
        load.start()

    def project(at, w):
        x = tokens_ref[:, at : at + per].reshape(parts * per, width)
        return jnp.dot(x, w, preferred_element_type=F32).reshape(parts, 2, half, width)

    kf, vf = project(0, wkv_ref[:, :width]), project(0, wkv_ref[:, width:])
    loads[0].wait()
    qf = project(per, wq_ref[...])
    for load in loads[1:]:
        load.wait()
    span = 256
    wins = width // span

    def members(t):
        return [h for h in range(heads) if h * size < (t + 1) * span and (h + 1) * size > t * span]

    def mask_of(h, t):
        spot = lax.broadcasted_iota(jnp.int32, (1, span), 1) + t * span
        return jnp.where((spot >= h * size) & (spot < (h + 1) * size), 1.0, 0.0).astype(BF)

    lane = lax.broadcasted_iota(jnp.int32, (queries, 128), 1)
    stats = jnp.zeros((queries, 128), F32)
    for s in range(2):
        q = qf[:, s].reshape(queries, width).astype(BF)
        k = kf[:, s].reshape(keys, width).astype(BF)
        v = vf[:, s].reshape(keys, width).astype(BF)
        raw = {}
        for t in range(wins):
            cut = slice(t * span, (t + 1) * span)
            lhs = jnp.concatenate([q[:, cut] * mask_of(h, t) for h in members(t)], 0)
            res = dot_nt(lhs, k[:, cut])
            for i, h in enumerate(members(t)):
                piece = res[i * queries : (i + 1) * queries]
                raw[h] = raw[h] + piece if h in raw else piece
        tops = jnp.zeros((queries, 128), F32)
        tots = jnp.zeros((queries, 128), F32)
        rounded = []
        for h in range(heads):
            sc = raw[h] * scale + bias_ref[h]
            top = jnp.max(sc, -1, keepdims=True)
            w = jnp.exp(sc - top)
            rounded.append(w.astype(BF))
            tots = jnp.where(lane == h, jnp.sum(w, -1, keepdims=True), tots)
            tops = jnp.where(lane == h, top, tops)
        for t in range(wins):
            cut = slice(t * span, (t + 1) * span)
            o = jnp.dot(
                jnp.concatenate([rounded[h] for h in members(t)], 1),
                jnp.concatenate([v[:, cut] * mask_of(h, t) for h in members(t)], 0),
                preferred_element_type=F32,
            )
            at = (s * wins + t) * per
            tiles = [o[:, i * 128 : (i + 1) * 128].reshape(parts, half, 128) for i in range(2)]
            out_ref[:, at : at + per, :] = jnp.concatenate(tiles, 1).astype(BF)
        hi, mid, low = split3(tops)
        mine = hi.astype(F32)
        for i, p in enumerate((mid.astype(F32), low.astype(F32), tots)):
            mine = mine + pltpu.roll(p, heads * (i + 1), 1)
        stats = stats + (pltpu.roll(mine, 64, 1) if s else mine)
    out_ref[:, 2 * wins * per :, :] = stats.reshape(parts, half, 128).astype(BF)


def merge_kernel(parts_ref, gate_ref, wout_ref, out_ref):
    parts, rows, _ = parts_ref.shape
    per, width = gate_ref.shape
    half = per // 2
    tiles = width // 128
    heads = 16
    size = width // heads
    both = parts_ref[:, tiles * per :, :].astype(F32).reshape(parts, 1, half, 128)
    other = pltpu.roll(both.reshape(parts * half, 128), 64, 1).reshape(parts, 1, half, 128)
    st = jnp.concatenate([both, other], 1).reshape(parts * per, 128)
    top = st + pltpu.roll(st, 128 - heads, 1) + pltpu.roll(st, 128 - 2 * heads, 1)
    tot = pltpu.roll(st, 128 - 3 * heads, 1)
    lane = lax.broadcasted_iota(jnp.int32, (parts * per, 128), 1)
    top = jnp.where(lane < heads, top, 0.0).reshape(parts, per, 128)
    tot = jnp.where(lane < heads, tot, 1.0).reshape(parts, per, 128)
    e = jnp.exp(top - jnp.max(top, 0, keepdims=True))
    f = e / jnp.sum(e * tot, 0, keepdims=True)
    f = jnp.where(lane < heads, f.reshape(parts * per, 128), 0.0)
    hrow = lax.broadcasted_iota(jnp.int32, (128, width), 0) * size
    col = lax.broadcasted_iota(jnp.int32, (128, width), 1)
    spread = jnp.where((col >= hrow) & (col < hrow + size), 1.0, 0.0).astype(BF)
    hi = f.astype(BF)
    low = (f - hi.astype(F32)).astype(BF)
    factor = jnp.dot(jnp.concatenate([hi, low], 1), jnp.concatenate([spread, spread], 0), preferred_element_type=F32)
    attended = []
    for i in range(tiles):
        at = [(s * (tiles // 2) + i // 2) * per for s in range(2)]
        num = [parts_ref[:, a : a + per, :].astype(F32)[:, i % 2 * half : i % 2 * half + half] for a in at]
        num = jnp.concatenate(num, 1)
        attended.append(jnp.sum(num * factor[:, i * 128 : (i + 1) * 128].reshape(parts, per, 128), 0))
    gated = (gate_ref[...] * jnp.concatenate(attended, 1)).astype(BF)
    update = jnp.dot(gated, wout_ref[...], preferred_element_type=F32)
    out_ref[...] = update.reshape(out_ref.shape).astype(BF)


def params(mib):
    return pltpu.CompilerParams(vmem_limit_bytes=mib << 20)


def shards(
    single,
    restype,
    restype_table,
    chain,
    live,
    pair,
    pair_gain,
    pair_weight,
    chain_bias,
    single_gain,
    w_qkvg,
    w_out,
):
    samples, tok, width = single.shape
    row_len, col_len, channels = pair.shape
    heads = chain_bias.shape[0]
    n_row, n_col = lax.axis_size("qrow"), lax.axis_size("kcol")
    shape = jax.ShapeDtypeStruct
    own = samples * tok

    stay = lambda *arrays: [pltpu.with_memory_space_constraint(x, pltpu.HBM) for x in arrays]
    hbm = lambda count: [pl.BlockSpec(memory_space=pltpu.HBM)] * count
    dma = pltpu.SemaphoreType.DMA
    normed, copies = pl.pallas_call(
        norm_kernel,
        name="norm",
        out_shape=(shape((own, width), BF), shape((n_row, own, width), BF)),
        in_specs=hbm(4),
        out_specs=(vmem(), vmem()),
        scratch_shapes=[
            pltpu.SMEM((tok,), jnp.int32),
            pltpu.VMEM((samples, tok, width), BF),
            pltpu.VMEM(restype_table.shape, BF),
            pltpu.VMEM((width,), F32),
            dma((4,)),
        ],
        compiler_params=params(4),
    )(*stay(restype, single, restype_table, single_gain))

    col_tokens = lax.all_to_all(copies, "qrow", 0, 0)
    where = jnp.stack([lax.axis_index("qrow"), lax.axis_index("kcol")]).astype(jnp.int32)
    chunks = 4
    half = row_len // 2

    def bias_of(late):
        out = [pltpu.HBM((heads, half, col_len), F32)]
        out += [shape((width, 2 * width), BF) if late else pltpu.HBM((own, width), F32)]
        return pl.pallas_call(
            functools.partial(bias_kernel, late * half, late),
            name="bias_" + str(late),
            out_shape=out,
            in_specs=[vmem(), smem()] + hbm(8),
            out_specs=[vmem()] * len(out),
            scratch_shapes=[
                pltpu.SMEM(chain.shape, jnp.int32),
                pltpu.SMEM((heads,), F32),
                pltpu.VMEM((chain.shape[0] // col_len, col_len), jnp.int32),
                pltpu.VMEM((1, col_len), jnp.int32),
                pltpu.VMEM((1, channels), F32),
                pltpu.VMEM((heads, channels), F32),
                pltpu.VMEM((chunks, half // chunks, col_len, channels), BF),
                dma((6,)),
                dma((chunks,)),
            ]
            + ([] if late else [pltpu.VMEM((width, width), BF)])
            + [dma((1,))],
            compiler_params=params(8),
            cost_estimate=pl.CostEstimate(flops=5 * 10**8, bytes_accessed=10 * 10**6, transcendentals=0),
        )(
            normed,
            where,
            *stay(
                chain,
                chain_bias,
                chain.reshape(-1, col_len),
                live.reshape(1, col_len),
                pair_gain.reshape(1, channels),
                pair_weight.T,
                pair,
                w_qkvg,
            ),
        )

    bias_a, gate = bias_of(0)
    bias_b, w_kv = bias_of(1)
    packed = pl.pallas_call(
        pack_kernel,
        name="pack",
        out_shape=shape((n_col, 2 * own, width), BF),
        in_specs=[vmem(), vmem()] + hbm(1),
        out_specs=vmem(),
        compiler_params=params(6),
    )(col_tokens, normed, *stay(bias_a))
    tokens = lax.all_to_all(packed, "kcol", 0, 0)

    rows = own * width // 128 + tok
    partial = pl.pallas_call(
        attend_kernel,
        name="attend",
        out_shape=shape((n_col, rows, 128), BF),
        in_specs=[vmem()] * 2 + hbm(3),
        out_specs=vmem(),
        scratch_shapes=[
            pltpu.VMEM((width, width), BF),
            pltpu.VMEM((heads, row_len, col_len), F32),
            dma((3,)),
        ],
        compiler_params=params(16),
    )(tokens, w_kv, *stay(w_qkvg, bias_a, bias_b))

    gathered = lax.all_to_all(partial, "kcol", 0, 0)
    return pl.pallas_call(
        merge_kernel,
        name="merge",
        out_shape=shape((samples, tok, width), BF),
        in_specs=[vmem(), vmem(), vmem()],
        out_specs=vmem(),
        compiler_params=params(8),
    )(gathered, gate, w_out)


def solution(mesh):
    return jax.shard_map(
        shards,
        mesh=mesh,
        in_specs=(
            P(None, ("qrow", "kcol"), None),
            P(("qrow", "kcol")),
            P(),
            P(),
            P("kcol"),
            P("qrow", "kcol", None),
            P(),
            P(),
            P(),
            P(),
            P(),
            P(),
        ),
        out_specs=P(None, ("qrow", "kcol"), None),
        check_vma=False,
    )
```

```python
import functools
import math

import jax
import jax.numpy as jnp
from jax import lax
from jax.experimental import pallas as pl
from jax.experimental.pallas import tpu as pltpu
from jax.sharding import PartitionSpec as P

BF = jnp.bfloat16
F32 = jnp.float32
EPS = 1e-05


def vmem():
    return pl.BlockSpec(memory_space=pltpu.VMEM)


def smem():
    return pl.BlockSpec(memory_space=pltpu.SMEM)


def dot_nt(a, b):
    return lax.dot_general(a, b, (((1,), (1,)), ((), ())), preferred_element_type=F32)


def layer_norm(x):
    centred = x - jnp.mean(x, -1, keepdims=True)
    variance = jnp.mean(centred * centred, -1, keepdims=True)
    return centred * lax.rsqrt(variance + EPS)


def split3(x):
    hi = x.astype(BF)
    rest = x - hi.astype(F32)
    mid = rest.astype(BF)
    low = (rest - mid.astype(F32)).astype(BF)
    return hi, mid, low


def fetch(copies, sems):
    started = [pltpu.make_async_copy(src, dst, sems.at[i]) for i, (src, dst) in enumerate(copies)]
    for copy in started:
        copy.start()
    for copy in started:
        copy.wait()


def norm_kernel(
    restype_hbm, single_hbm, table_hbm, gain_hbm, normed_ref, copies_ref, restype_ref, single_ref, table_ref, gain_ref, sems
):
    fetch(
        [
            (restype_hbm, restype_ref),
            (single_hbm, single_ref),
            (table_hbm, table_ref),
            (gain_hbm, gain_ref),
        ],
        sems,
    )
    samples, tok, width = single_ref.shape
    kinds = table_ref.shape[0]
    row = lax.broadcasted_iota(jnp.int32, (tok, kinds), 0)
    col = lax.broadcasted_iota(jnp.int32, (tok, kinds), 1)
    kind = jnp.zeros((tok, kinds), jnp.int32)
    for t in range(tok):
        kind = jnp.where(row == t, restype_ref[t], kind)
    one_hot = jnp.where(kind == col, 1.0, 0.0).astype(BF)
    emb = jnp.dot(one_hot, table_ref[...], preferred_element_type=F32)
    x = single_ref[...].astype(F32) + emb[None]
    normed = layer_norm(x) * gain_ref[...].reshape(1, 1, width)
    normed = normed.reshape(samples * tok, width).astype(BF)
    normed_ref[...] = normed
    for j in range(copies_ref.shape[0]):
        copies_ref[j] = normed


def copies_kernel(one_ref, two_ref, after_ref, copies_ref):
    per = one_ref.shape[0]
    for j in range(copies_ref.shape[0]):
        copies_ref[j, :per] = one_ref[...]
        copies_ref[j, per:] = two_ref[...]


def bias_kernel(start, late, tokens_ref, where_ref, *refs):
    ins, refs = refs[:8], refs[8:]
    pair_hbm, w_hbm = ins[6:]
    out_ref, extra_ref, refs = refs[0], refs[1], refs[2:]
    if late:
        w_ref, refs = refs[0], refs[1:]
    chain_ref, cbias_ref, chain_rows_ref, live_ref, gain_ref, weight_ref, pair_ref, sems, pair_sems = refs[:9]
    mine_ref, w_sems = refs[9:]
    chunks, block, keys, channels = pair_ref.shape
    heads = weight_ref.shape[0]
    width = mine_ref.shape[0]
    loads = [
        pltpu.make_async_copy(pair_hbm.at[pl.ds(start + i * block, block)], pair_ref.at[i], pair_sems.at[i])
        for i in range(chunks)
    ]
    for load in loads[:2]:
        load.start()
    small = list(zip(ins[:6], (chain_ref, cbias_ref, chain_rows_ref, live_ref, gain_ref, weight_ref)))
    small = [pltpu.make_async_copy(src, dst, sems.at[i]) for i, (src, dst) in enumerate(small)]
    for load in small + loads[2:]:
        load.start()
    own = 0 if late else 3 * width
    load_mine = pltpu.make_async_copy(w_hbm.at[:, pl.ds(own, width)], mine_ref, w_sems.at[0])
    load_mine.start()
    if late:
        load_w = pltpu.make_async_copy(w_hbm.at[:, pl.ds(width, 2 * width)], w_ref, w_sems.at[1])
        load_w.start()
    for load in small:
        load.wait()
    weight = weight_ref[...] * gain_ref[...]
    lhs = jnp.concatenate(split3(weight), 0)
    total = jnp.sum(weight, -1, keepdims=True)
    row = lax.broadcasted_iota(jnp.int32, (heads, keys), 0)
    column = jnp.zeros((heads, keys), F32)
    for h in range(heads):
        column = jnp.where(row == h, cbias_ref[h], column)
    base = where_ref[0] * pair_hbm.shape[0] + start
    col_chain = chain_rows_ref[pl.ds(where_ref[1], 1), :]
    alive = jnp.broadcast_to(live_ref[...] == 1, (heads, keys))
    for i in range(chunks):
        loads[i].wait()
        for q in range(0, block, 2):
            turned = pair_ref[i, q : q + 2].reshape(2 * keys, channels).T
            x = turned.astype(F32)
            mean = jnp.sum(x, 0, keepdims=True) * (1.0 / channels)
            centred = x - mean
            variance = jnp.sum(centred * centred, 0, keepdims=True) * (1.0 / channels)
            res = jnp.dot(lhs, turned, preferred_element_type=F32)
            res = res[:heads] + res[heads : 2 * heads] + res[2 * heads :]
            res = (res - total * mean) * lax.rsqrt(variance + EPS)
            for k in range(2):
                at = i * block + q + k
                part = res[:, k * keys : (k + 1) * keys]
                same = col_chain == chain_ref[base + at]
                part = part + jnp.where(same, column, 0.0)
                out_ref[:, at, :] = jnp.where(alive, part, -1e30)
    load_mine.wait()
    parts, per, _ = tokens_ref.shape
    res = jnp.dot(tokens_ref[...].reshape(parts * per, width), mine_ref[...], preferred_element_type=F32)
    if late:
        res = res.reshape(parts, 2, per // 2, width)
        for s in range(2):
            extra_ref[s] = res[:, s].reshape(parts * per // 2, width).astype(BF)
        load_w.wait()
    else:
        extra_ref[...] = jax.nn.sigmoid(res)


def attend_kernel(
    where_ref, order_ref, cols_ref, wkv_ref, q_ref, bias_a_hbm, bias_b_hbm, out_ref, x_ref, bias_ref, sems
):
    parts, per, width = cols_ref.shape
    half = per // 2
    heads, queries, keys = bias_ref.shape
    few = bias_a_hbm.shape[1]
    size = width // heads
    scale = 1.0 / math.sqrt(size)
    loads = [
        pltpu.make_async_copy(bias_a_hbm, bias_ref.at[:, pl.ds(0, few)], sems.at[0]),
        pltpu.make_async_copy(bias_b_hbm, bias_ref.at[:, pl.ds(few, queries - few)], sems.at[1]),
    ]
    for load in loads:
        load.start()
    base = (where_ref[1] * 2 + lax.rem(lax.div(where_ref[0], 2), 2)) * parts
    for i in range(parts):
        x_ref[pl.ds(order_ref[base + i], 1)] = cols_ref[pl.ds(i, 1)]
    x = x_ref[...].reshape(parts * per, width)

    def project(w):
        return jnp.dot(x, w, preferred_element_type=F32).reshape(parts, 2, half, width)

    kf, vf = project(wkv_ref[:, :width]), project(wkv_ref[:, width:])
    span = 256
    wins = width // span

    def members(t):
        return [h for h in range(heads) if h * size < (t + 1) * span and (h + 1) * size > t * span]

    def mask_of(h, t):
        spot = lax.broadcasted_iota(jnp.int32, (1, span), 1) + t * span
        return jnp.where((spot >= h * size) & (spot < (h + 1) * size), 1.0, 0.0).astype(BF)

    lane = lax.broadcasted_iota(jnp.int32, (queries, 128), 1)
    stats = jnp.zeros((queries, 128), F32)
    for s in range(2):
        q = q_ref[s]
        k = kf[:, s].reshape(keys, width).astype(BF)
        v = vf[:, s].reshape(keys, width).astype(BF)
        raw = {}
        for t in range(wins):
            cut = slice(t * span, (t + 1) * span)
            lhs = jnp.concatenate([q[:, cut] * mask_of(h, t) for h in members(t)], 0)
            res = dot_nt(lhs, k[:, cut])
            for i, h in enumerate(members(t)):
                piece = res[i * queries : (i + 1) * queries]
                raw[h] = raw[h] + piece if h in raw else piece
        if s == 0:
            for load in loads:
                load.wait()
        tops = jnp.zeros((queries, 128), F32)
        tots = jnp.zeros((queries, 128), F32)
        rounded = []
        for h in range(heads):
            sc = raw[h] * scale + bias_ref[h]
            top = jnp.max(sc, -1, keepdims=True)
            w = jnp.exp(sc - top)
            rounded.append(w.astype(BF))
            tots = jnp.where(lane == h, jnp.sum(w, -1, keepdims=True), tots)
            tops = jnp.where(lane == h, top, tops)
        for t in range(wins):
            cut = slice(t * span, (t + 1) * span)
            o = jnp.dot(
                jnp.concatenate([rounded[h] for h in members(t)], 1),
                jnp.concatenate([v[:, cut] * mask_of(h, t) for h in members(t)], 0),
                preferred_element_type=F32,
            )
            at = (s * wins + t) * per
            tiles = [o[:, i * 128 : (i + 1) * 128].reshape(parts, half, 128) for i in range(2)]
            out_ref[:, at : at + per, :] = jnp.concatenate(tiles, 1).astype(BF)
        hi, mid, low = split3(tops)
        mine = hi.astype(F32)
        for i, p in enumerate((mid.astype(F32), low.astype(F32), tots)):
            mine = mine + pltpu.roll(p, heads * (i + 1), 1)
        stats = stats + (pltpu.roll(mine, 64, 1) if s else mine)
    out_ref[:, 2 * wins * per :, :] = stats.reshape(parts, half, 128).astype(BF)


def merge_kernel(parts_ref, gate_ref, wout_ref, out_ref):
    parts, rows, _ = parts_ref.shape
    per, width = gate_ref.shape
    half = per // 2
    tiles = width // 128
    heads = 16
    size = width // heads
    both = parts_ref[:, tiles * per :, :].astype(F32).reshape(parts, 1, half, 128)
    other = pltpu.roll(both.reshape(parts * half, 128), 64, 1).reshape(parts, 1, half, 128)
    st = jnp.concatenate([both, other], 1).reshape(parts * per, 128)
    top = st + pltpu.roll(st, 128 - heads, 1) + pltpu.roll(st, 128 - 2 * heads, 1)
    tot = pltpu.roll(st, 128 - 3 * heads, 1)
    lane = lax.broadcasted_iota(jnp.int32, (parts * per, 128), 1)
    top = jnp.where(lane < heads, top, 0.0).reshape(parts, per, 128)
    tot = jnp.where(lane < heads, tot, 1.0).reshape(parts, per, 128)
    e = jnp.exp(top - jnp.max(top, 0, keepdims=True))
    f = e / jnp.sum(e * tot, 0, keepdims=True)
    f = jnp.where(lane < heads, f.reshape(parts * per, 128), 0.0)
    hrow = lax.broadcasted_iota(jnp.int32, (128, width), 0) * size
    col = lax.broadcasted_iota(jnp.int32, (128, width), 1)
    spread = jnp.where((col >= hrow) & (col < hrow + size), 1.0, 0.0).astype(BF)
    hi = f.astype(BF)
    low = (f - hi.astype(F32)).astype(BF)
    factor = jnp.dot(jnp.concatenate([hi, low], 1), jnp.concatenate([spread, spread], 0), preferred_element_type=F32)
    attended = []
    for i in range(tiles):
        at = [(s * (tiles // 2) + i // 2) * per for s in range(2)]
        num = [parts_ref[:, a : a + per, :].astype(F32)[:, i % 2 * half : i % 2 * half + half] for a in at]
        num = jnp.concatenate(num, 1)
        attended.append(jnp.sum(num * factor[:, i * 128 : (i + 1) * 128].reshape(parts, per, 128), 0))
    gated = (gate_ref[...] * jnp.concatenate(attended, 1)).astype(BF)
    update = jnp.dot(gated, wout_ref[...], preferred_element_type=F32)
    out_ref[...] = update.reshape(out_ref.shape).astype(BF)


def near_swaps(n):
    ring = lambda a, b, size: min((a - b) % size, (b - a) % size)
    upper = lambda i: i // 2 % 2
    tables = ([], [])
    for c in range(n):

        def cost(j, i):
            hops = ring(c // 4, i // 4, 4) + ring(j % 8, c % 8, 8)
            hops += ring(upper(c) * 2 + j // 8, upper(i) * 2 + c // 8, 4)
            return 2 * hops + (c % 2 != i % 2)

        first = {}
        for table in tables:
            for most in range(100):
                taken = {}

                def place(j, seen):
                    for i in range(n):
                        other = j not in first or upper(first[j]) != upper(i)
                        if other and cost(j, i) <= most and i not in seen:
                            seen.add(i)
                            if i not in taken or place(taken[i], seen):
                                taken[i] = j
                                return True
                    return False

                if all(place(j, set()) for j in range(n)):
                    break
            table.append([taken[i] for i in range(n)])
            first = {j: i for i, j in taken.items()}
    return tables


def params(mib):
    return pltpu.CompilerParams(vmem_limit_bytes=mib << 20)


def shards(
    single,
    restype,
    restype_table,
    chain,
    live,
    pair,
    pair_gain,
    pair_weight,
    chain_bias,
    single_gain,
    w_qkvg,
    w_out,
):
    samples, tok, width = single.shape
    row_len, col_len, channels = pair.shape
    heads = chain_bias.shape[0]
    n_row, n_col = lax.axis_size("qrow"), lax.axis_size("kcol")
    shape = jax.ShapeDtypeStruct
    own = samples * tok

    stay = lambda *arrays: [pltpu.with_memory_space_constraint(x, pltpu.HBM) for x in arrays]
    hbm = lambda count: [pl.BlockSpec(memory_space=pltpu.HBM)] * count
    dma = pltpu.SemaphoreType.DMA
    normed, copies = pl.pallas_call(
        norm_kernel,
        name="norm",
        out_shape=(shape((own, width), BF), shape((n_col, own, width), BF)),
        in_specs=hbm(4),
        out_specs=(vmem(), vmem()),
        scratch_shapes=[
            pltpu.SMEM((tok,), jnp.int32),
            pltpu.VMEM((samples, tok, width), BF),
            pltpu.VMEM(restype_table.shape, BF),
            pltpu.VMEM((width,), F32),
            dma((4,)),
        ],
        compiler_params=params(4),
    )(*stay(restype, single, restype_table, single_gain))

    tables = near_swaps(n_row)
    turned = []
    for table in tables:
        swap = [(c * n_col + j, i * n_col + c) for c in range(n_row) for i, j in enumerate(table[c])]
        turned.append(lax.ppermute(normed, ("qrow", "kcol"), swap))
    row_tokens = lax.all_to_all(copies, "kcol", 0, 0)

    where = jnp.stack([lax.axis_index("qrow"), lax.axis_index("kcol")]).astype(jnp.int32)
    block = row_len // 8

    def bias_of(late, tokens):
        chunks = 2 if late else 6
        out = [pltpu.HBM((heads, chunks * block, col_len), F32)]
        out += [shape((samples, row_len, width), BF) if late else pltpu.HBM((own, width), F32)]
        out += [shape((width, 2 * width), BF)] * late
        return pl.pallas_call(
            functools.partial(bias_kernel, late * (row_len - 2 * block), late),
            name="bias_" + str(late),
            out_shape=out,
            in_specs=[vmem(), smem()] + hbm(8),
            out_specs=[vmem()] * len(out),
            scratch_shapes=[
                pltpu.SMEM(chain.shape, jnp.int32),
                pltpu.SMEM((heads,), F32),
                pltpu.VMEM((chain.shape[0] // col_len, col_len), jnp.int32),
                pltpu.VMEM((1, col_len), jnp.int32),
                pltpu.VMEM((1, channels), F32),
                pltpu.VMEM((heads, channels), F32),
                pltpu.VMEM((chunks, block, col_len, channels), BF),
                dma((6,)),
                dma((chunks,)),
                pltpu.VMEM((width, width), BF),
                dma((2,)),
            ],
            compiler_params=params(10),
            cost_estimate=pl.CostEstimate(flops=5 * 10**8, bytes_accessed=10 * 10**6, transcendentals=0),
        )(
            tokens,
            where,
            *stay(
                chain,
                chain_bias,
                chain.reshape(-1, col_len),
                live.reshape(1, col_len),
                pair_gain.reshape(1, channels),
                pair_weight.T,
                pair,
                w_qkvg,
            ),
        )

    bias_a, gate = bias_of(0, normed[None])
    bias_b, queries, w_kv = bias_of(1, row_tokens)
    sides = [[i for i in range(n_row) if i // 2 % 2 == side] for side in range(2)]
    turned_copies = pl.pallas_call(
        copies_kernel,
        name="copies",
        out_shape=shape((n_row // 2, 2 * own, width), BF),
        in_specs=[vmem()] * 2 + hbm(1),
        out_specs=vmem(),
        compiler_params=params(4),
    )(*turned, *stay(bias_a))
    turned_copies, row_tokens = lax.optimization_barrier((turned_copies, row_tokens))
    col_tokens = lax.all_to_all(turned_copies, "qrow", 0, 0, axis_index_groups=sides)
    col_tokens = col_tokens.reshape(n_row, own, width)
    order = [tables[k][c][i] for c in range(n_col) for side in sides for i in side for k in range(2)]
    order = jnp.asarray(order, jnp.int32)

    rows = own * width // 128 + tok
    partial = pl.pallas_call(
        attend_kernel,
        name="attend",
        out_shape=shape((n_col, rows, 128), BF),
        in_specs=[smem()] * 2 + [vmem()] * 3 + hbm(2),
        out_specs=vmem(),
        scratch_shapes=[
            pltpu.VMEM(col_tokens.shape, BF),
            pltpu.VMEM((heads, row_len, col_len), F32),
            dma((2,)),
        ],
        compiler_params=params(16),
    )(where, order, col_tokens, w_kv, queries, *stay(bias_a, bias_b))

    gathered = lax.all_to_all(partial, "kcol", 0, 0)
    return pl.pallas_call(
        merge_kernel,
        name="merge",
        out_shape=shape((samples, tok, width), BF),
        in_specs=[vmem(), vmem(), vmem()],
        out_specs=vmem(),
        compiler_params=params(8),
    )(gathered, gate, w_out)


def solution(mesh):
    return jax.shard_map(
        shards,
        mesh=mesh,
        in_specs=(
            P(None, ("qrow", "kcol"), None),
            P(("qrow", "kcol")),
            P(),
            P(),
            P("kcol"),
            P("qrow", "kcol", None),
            P(),
            P(),
            P(),
            P(),
            P(),
            P(),
        ),
        out_specs=P(None, ("qrow", "kcol"), None),
        check_vma=False,
    )
```

```python
import functools
import math

import jax
import jax.numpy as jnp
from jax import lax
from jax.experimental import pallas as pl
from jax.experimental.pallas import tpu as pltpu
from jax.sharding import PartitionSpec as P

BF = jnp.bfloat16
F32 = jnp.float32
EPS = 1e-05


def vmem():
    return pl.BlockSpec(memory_space=pltpu.VMEM)


def smem():
    return pl.BlockSpec(memory_space=pltpu.SMEM)


def dot_nt(a, b):
    return lax.dot_general(a, b, (((1,), (1,)), ((), ())), preferred_element_type=F32)


def layer_norm(x):
    centred = x - jnp.mean(x, -1, keepdims=True)
    variance = jnp.mean(centred * centred, -1, keepdims=True)
    return centred * lax.rsqrt(variance + EPS)


def split3(x):
    hi = x.astype(BF)
    rest = x - hi.astype(F32)
    mid = rest.astype(BF)
    low = (rest - mid.astype(F32)).astype(BF)
    return hi, mid, low


def fetch(copies, sems):
    started = [pltpu.make_async_copy(src, dst, sems.at[i]) for i, (src, dst) in enumerate(copies)]
    for copy in started:
        copy.start()
    for copy in started:
        copy.wait()


def norm_kernel(
    restype_hbm, single_hbm, table_hbm, gain_hbm, normed_ref, copies_ref, restype_ref, single_ref, table_ref, gain_ref, sems
):
    fetch(
        [
            (restype_hbm, restype_ref),
            (single_hbm, single_ref),
            (table_hbm, table_ref),
            (gain_hbm, gain_ref),
        ],
        sems,
    )
    samples, tok, width = single_ref.shape
    kinds = table_ref.shape[0]
    row = lax.broadcasted_iota(jnp.int32, (tok, kinds), 0)
    col = lax.broadcasted_iota(jnp.int32, (tok, kinds), 1)
    kind = jnp.zeros((tok, kinds), jnp.int32)
    for t in range(tok):
        kind = jnp.where(row == t, restype_ref[t], kind)
    one_hot = jnp.where(kind == col, 1.0, 0.0).astype(BF)
    emb = jnp.dot(one_hot, table_ref[...], preferred_element_type=F32)
    x = single_ref[...].astype(F32) + emb[None]
    normed = layer_norm(x) * gain_ref[...].reshape(1, 1, width)
    normed = normed.reshape(samples * tok, width).astype(BF)
    normed_ref[...] = normed
    for j in range(copies_ref.shape[0]):
        copies_ref[j] = normed


def copies_kernel(one_ref, two_ref, after_ref, copies_ref):
    per = one_ref.shape[0]
    for j in range(copies_ref.shape[0]):
        copies_ref[j, :per] = one_ref[...]
        copies_ref[j, per:] = two_ref[...]


def bias_kernel(start, late, own_ref, where_ref, *refs):
    ins, refs = refs[:8], refs[8:]
    pair_hbm, w_hbm = ins[6:]
    out_ref, extra_ref, refs = refs[0], refs[1], refs[2:]
    if late:
        wq_ref, refs = refs[0], refs[1:]
    chain_ref, cbias_ref, chain_rows_ref, live_ref, gain_ref, weight_ref, pair_ref, sems, pair_sems = refs[:9]
    w_ref, w_sem = (extra_ref, refs[9]) if late else refs[9:]
    chunks, block, keys, channels = pair_ref.shape
    heads = weight_ref.shape[0]
    width = own_ref.shape[1]
    loads = [
        pltpu.make_async_copy(pair_hbm.at[pl.ds(start + i * block, block)], pair_ref.at[i], pair_sems.at[i])
        for i in range(chunks)
    ]
    for load in loads[:2]:
        load.start()
    small = list(zip(ins[:6], (chain_ref, cbias_ref, chain_rows_ref, live_ref, gain_ref, weight_ref)))
    small = [pltpu.make_async_copy(src, dst, sems.at[i]) for i, (src, dst) in enumerate(small)]
    for load in small + loads[2:]:
        load.start()
    place = pl.ds(width, 2 * width) if late else pl.ds(3 * width, width)
    load_w = [pltpu.make_async_copy(w_hbm.at[:, place], w_ref, w_sem.at[0])]
    if late:
        load_w.append(pltpu.make_async_copy(w_hbm.at[:, pl.ds(0, width)], wq_ref, w_sem.at[1]))
    for load in small:
        load.wait()
    weight = weight_ref[...] * gain_ref[...]
    lhs = jnp.concatenate(split3(weight), 0)
    total = jnp.sum(weight, -1, keepdims=True)
    row = lax.broadcasted_iota(jnp.int32, (heads, keys), 0)
    column = jnp.zeros((heads, keys), F32)
    for h in range(heads):
        column = jnp.where(row == h, cbias_ref[h], column)
    base = where_ref[0] * pair_hbm.shape[0] + start
    col_chain = chain_rows_ref[pl.ds(where_ref[1], 1), :]
    alive = jnp.broadcast_to(live_ref[...] == 1, (heads, keys))
    for i in range(chunks):
        loads[i].wait()
        if i == 0:
            for load in load_w:
                load.start()
        for q in range(0, block, 2):
            turned = pair_ref[i, q : q + 2].reshape(2 * keys, channels).T
            x = turned.astype(F32)
            mean = jnp.sum(x, 0, keepdims=True) * (1.0 / channels)
            centred = x - mean
            variance = jnp.sum(centred * centred, 0, keepdims=True) * (1.0 / channels)
            res = jnp.dot(lhs, turned, preferred_element_type=F32)
            res = res[:heads] + res[heads : 2 * heads] + res[2 * heads :]
            res = (res - total * mean) * lax.rsqrt(variance + EPS)
            for k in range(2):
                at = i * block + q + k
                part = res[:, k * keys : (k + 1) * keys]
                same = col_chain == chain_ref[base + at]
                part = part + jnp.where(same, column, 0.0)
                out_ref[:, at, :] = jnp.where(alive, part, -1e30)
    for load in load_w:
        load.wait()
    if not late:
        pre = jnp.dot(own_ref[...], w_ref[...], preferred_element_type=F32)
        extra_ref[...] = jax.nn.sigmoid(pre)


def query_kernel(where_ref, rows_ref, others_ref, w_ref, q_ref, x_ref):
    near, per, width = rows_ref.shape
    ours = lax.div(where_ref[1], near) * near
    x_ref[pl.ds(ours, near)] = rows_ref[...]
    x_ref[pl.ds(near - ours, near)] = others_ref[...]
    x = x_ref[...].reshape(2 * near * per, width)
    query = jnp.dot(x, w_ref[...], preferred_element_type=F32).reshape(2 * near, 2, per // 2, width)
    for s in range(2):
        q_ref[s] = query[:, s].reshape(near * per, width).astype(BF)


def attend_kernel(
    where_ref, order_ref, cols_ref, wkv_ref, q_ref, bias_a_hbm, bias_b_hbm, out_ref, x_ref, bias_ref, sems
):
    parts, per, width = cols_ref.shape
    half = per // 2
    heads, queries, keys = bias_ref.shape
    few = bias_a_hbm.shape[1]
    size = width // heads
    scale = 1.0 / math.sqrt(size)
    loads = [
        pltpu.make_async_copy(bias_a_hbm, bias_ref.at[:, pl.ds(0, few)], sems.at[0]),
        pltpu.make_async_copy(bias_b_hbm, bias_ref.at[:, pl.ds(few, queries - few)], sems.at[1]),
    ]
    for load in loads:
        load.start()
    base = (where_ref[1] * 2 + lax.rem(lax.div(where_ref[0], 2), 2)) * parts
    for i in range(parts):
        x_ref[pl.ds(order_ref[base + i], 1)] = cols_ref[pl.ds(i, 1)]
    x = x_ref[...].reshape(parts * per, width)

    def project(w):
        return jnp.dot(x, w, preferred_element_type=F32).reshape(parts, 2, half, width)

    kf, vf = project(wkv_ref[:, :width]), project(wkv_ref[:, width:])
    span = 256
    wins = width // span

    def members(t):
        return [h for h in range(heads) if h * size < (t + 1) * span and (h + 1) * size > t * span]

    def mask_of(h, t):
        spot = lax.broadcasted_iota(jnp.int32, (1, span), 1) + t * span
        return jnp.where((spot >= h * size) & (spot < (h + 1) * size), 1.0, 0.0).astype(BF)

    lane = lax.broadcasted_iota(jnp.int32, (queries, 128), 1)
    stats = jnp.zeros((queries, 128), F32)
    for s in range(2):
        q = q_ref[s]
        k = kf[:, s].reshape(keys, width).astype(BF)
        v = vf[:, s].reshape(keys, width).astype(BF)
        raw = {}
        for t in range(wins):
            cut = slice(t * span, (t + 1) * span)
            lhs = jnp.concatenate([q[:, cut] * mask_of(h, t) for h in members(t)], 0)
            res = dot_nt(lhs, k[:, cut])
            for i, h in enumerate(members(t)):
                piece = res[i * queries : (i + 1) * queries]
                raw[h] = raw[h] + piece if h in raw else piece
        if s == 0:
            for load in loads:
                load.wait()
        tops = jnp.zeros((queries, 128), F32)
        tots = jnp.zeros((queries, 128), F32)
        rounded = []
        for h in range(heads):
            sc = raw[h] * scale + bias_ref[h]
            top = jnp.max(sc, -1, keepdims=True)
            w = jnp.exp(sc - top)
            rounded.append(w.astype(BF))
            tots = jnp.where(lane == h, jnp.sum(w, -1, keepdims=True), tots)
            tops = jnp.where(lane == h, top, tops)
        for t in range(wins):
            cut = slice(t * span, (t + 1) * span)
            o = jnp.dot(
                jnp.concatenate([rounded[h] for h in members(t)], 1),
                jnp.concatenate([v[:, cut] * mask_of(h, t) for h in members(t)], 0),
                preferred_element_type=F32,
            )
            at = (s * wins + t) * per
            tiles = [o[:, i * 128 : (i + 1) * 128].reshape(parts, half, 128) for i in range(2)]
            out_ref[:, at : at + per, :] = jnp.concatenate(tiles, 1).astype(BF)
        hi, mid, low = split3(tops)
        mine = hi.astype(F32)
        for i, p in enumerate((mid.astype(F32), low.astype(F32), tots)):
            mine = mine + pltpu.roll(p, heads * (i + 1), 1)
        stats = stats + (pltpu.roll(mine, 64, 1) if s else mine)
    out_ref[:, 2 * wins * per :, :] = stats.reshape(parts, half, 128).astype(BF)


def merge_kernel(parts_ref, gate_ref, wout_ref, out_ref):
    parts, rows, _ = parts_ref.shape
    per, width = gate_ref.shape
    half = per // 2
    tiles = width // 128
    heads = 16
    size = width // heads
    both = parts_ref[:, tiles * per :, :].astype(F32).reshape(parts, 1, half, 128)
    other = pltpu.roll(both.reshape(parts * half, 128), 64, 1).reshape(parts, 1, half, 128)
    st = jnp.concatenate([both, other], 1).reshape(parts * per, 128)
    top = st + pltpu.roll(st, 128 - heads, 1) + pltpu.roll(st, 128 - 2 * heads, 1)
    tot = pltpu.roll(st, 128 - 3 * heads, 1)
    lane = lax.broadcasted_iota(jnp.int32, (parts * per, 128), 1)
    top = jnp.where(lane < heads, top, 0.0).reshape(parts, per, 128)
    tot = jnp.where(lane < heads, tot, 1.0).reshape(parts, per, 128)
    e = jnp.exp(top - jnp.max(top, 0, keepdims=True))
    f = e / jnp.sum(e * tot, 0, keepdims=True)
    f = jnp.where(lane < heads, f.reshape(parts * per, 128), 0.0)
    hrow = lax.broadcasted_iota(jnp.int32, (128, width), 0) * size
    col = lax.broadcasted_iota(jnp.int32, (128, width), 1)
    spread = jnp.where((col >= hrow) & (col < hrow + size), 1.0, 0.0).astype(BF)
    hi = f.astype(BF)
    low = (f - hi.astype(F32)).astype(BF)
    factor = jnp.dot(jnp.concatenate([hi, low], 1), jnp.concatenate([spread, spread], 0), preferred_element_type=F32)
    attended = []
    for i in range(tiles):
        at = [(s * (tiles // 2) + i // 2) * per for s in range(2)]
        num = [parts_ref[:, a : a + per, :].astype(F32)[:, i % 2 * half : i % 2 * half + half] for a in at]
        num = jnp.concatenate(num, 1)
        attended.append(jnp.sum(num * factor[:, i * 128 : (i + 1) * 128].reshape(parts, per, 128), 0))
    gated = (gate_ref[...] * jnp.concatenate(attended, 1)).astype(BF)
    update = jnp.dot(gated, wout_ref[...], preferred_element_type=F32)
    out_ref[...] = update.reshape(out_ref.shape).astype(BF)


def near_swaps(n):
    ring = lambda a, b, size: min((a - b) % size, (b - a) % size)
    upper = lambda i: i // 2 % 2
    tables = ([], [])
    for c in range(n):

        def cost(j, i):
            hops = ring(c // 4, i // 4, 4) + ring(j % 8, c % 8, 8)
            hops += ring(upper(c) * 2 + j // 8, upper(i) * 2 + c // 8, 4)
            return 2 * hops + (c % 2 != i % 2)

        first = {}
        for table in tables:
            for most in range(100):
                taken = {}

                def place(j, seen):
                    for i in range(n):
                        other = j not in first or upper(first[j]) != upper(i)
                        if other and cost(j, i) <= most and i not in seen:
                            seen.add(i)
                            if i not in taken or place(taken[i], seen):
                                taken[i] = j
                                return True
                    return False

                if all(place(j, set()) for j in range(n)):
                    break
            table.append([taken[i] for i in range(n)])
            first = {j: i for i, j in taken.items()}
    return tables


def params(mib):
    return pltpu.CompilerParams(vmem_limit_bytes=mib << 20)


def shards(
    single,
    restype,
    restype_table,
    chain,
    live,
    pair,
    pair_gain,
    pair_weight,
    chain_bias,
    single_gain,
    w_qkvg,
    w_out,
):
    samples, tok, width = single.shape
    row_len, col_len, channels = pair.shape
    heads = chain_bias.shape[0]
    n_row, n_col = lax.axis_size("qrow"), lax.axis_size("kcol")
    shape = jax.ShapeDtypeStruct
    own = samples * tok

    stay = lambda *arrays: [pltpu.with_memory_space_constraint(x, pltpu.HBM) for x in arrays]
    hbm = lambda count: [pl.BlockSpec(memory_space=pltpu.HBM)] * count
    dma = pltpu.SemaphoreType.DMA
    normed, copies = pl.pallas_call(
        norm_kernel,
        name="norm",
        out_shape=(shape((own, width), BF), shape((n_col // 2, own, width), BF)),
        in_specs=hbm(4),
        out_specs=(vmem(), vmem()),
        scratch_shapes=[
            pltpu.SMEM((tok,), jnp.int32),
            pltpu.VMEM((samples, tok, width), BF),
            pltpu.VMEM(restype_table.shape, BF),
            pltpu.VMEM((width,), F32),
            dma((4,)),
        ],
        compiler_params=params(4),
    )(*stay(restype, single, restype_table, single_gain))

    tables = near_swaps(n_row)
    turned = []
    for table in tables:
        swap = [(c * n_col + j, i * n_col + c) for c in range(n_row) for i, j in enumerate(table[c])]
        turned.append(lax.ppermute(normed, ("qrow", "kcol"), swap))
    near = [list(range(n_col // 2)), list(range(n_col // 2, n_col))]
    row_tokens = lax.all_to_all(copies, "kcol", 0, 0, axis_index_groups=near)

    where = jnp.stack([lax.axis_index("qrow"), lax.axis_index("kcol")]).astype(jnp.int32)
    block = row_len // 8

    def bias_of(late):
        chunks = 4
        out = [pltpu.HBM((heads, chunks * block, col_len), F32)]
        out += [shape((width, 2 * width), BF) if late else pltpu.HBM((own, width), F32)]
        out += [shape((width, width), BF)] * late
        return pl.pallas_call(
            functools.partial(bias_kernel, late * chunks * block, late),
            name="bias_" + str(late),
            out_shape=out,
            in_specs=[vmem(), smem()] + hbm(8),
            out_specs=[vmem()] * len(out),
            scratch_shapes=[
                pltpu.SMEM(chain.shape, jnp.int32),
                pltpu.SMEM((heads,), F32),
                pltpu.VMEM((chain.shape[0] // col_len, col_len), jnp.int32),
                pltpu.VMEM((1, col_len), jnp.int32),
                pltpu.VMEM((1, channels), F32),
                pltpu.VMEM((heads, channels), F32),
                pltpu.VMEM((chunks, block, col_len, channels), BF),
                dma((6,)),
                dma((chunks,)),
            ]
            + ([] if late else [pltpu.VMEM((width, width), BF)])
            + [dma((2,))],
            compiler_params=params(10),
            cost_estimate=pl.CostEstimate(flops=5 * 10**8, bytes_accessed=10 * 10**6, transcendentals=0),
        )(
            normed,
            where,
            *stay(
                chain,
                chain_bias,
                chain.reshape(-1, col_len),
                live.reshape(1, col_len),
                pair_gain.reshape(1, channels),
                pair_weight.T,
                pair,
                w_qkvg,
            ),
        )

    bias_a, gate = bias_of(0)
    bias_b, w_kv, w_q = bias_of(1)
    sides = [[i for i in range(n_row) if i // 2 % 2 == side] for side in range(2)]
    turned_copies = pl.pallas_call(
        copies_kernel,
        name="copies",
        out_shape=shape((n_row // 2, 2 * own, width), BF),
        in_specs=[vmem()] * 2 + hbm(1),
        out_specs=vmem(),
        compiler_params=params(4),
    )(*turned, *stay(bias_a))
    turned_copies, row_tokens = lax.optimization_barrier((turned_copies, row_tokens))
    col_tokens = lax.all_to_all(turned_copies, "qrow", 0, 0, axis_index_groups=sides)
    other_tokens = lax.ppermute(row_tokens, "kcol", [(i, (i + n_col // 2) % n_col) for i in range(n_col)])
    col_tokens = col_tokens.reshape(n_row, own, width)
    queries = pl.pallas_call(
        query_kernel,
        name="query",
        out_shape=shape((samples, row_len, width), BF),
        in_specs=[smem()] + [vmem()] * 3,
        out_specs=vmem(),
        scratch_shapes=[pltpu.VMEM((n_col, own, width), BF)],
        compiler_params=params(6),
    )(where, row_tokens, other_tokens, w_q)
    order = [tables[k][c][i] for c in range(n_col) for side in sides for i in side for k in range(2)]
    order = jnp.asarray(order, jnp.int32)

    rows = own * width // 128 + tok
    partial = pl.pallas_call(
        attend_kernel,
        name="attend",
        out_shape=shape((n_col, rows, 128), BF),
        in_specs=[smem()] * 2 + [vmem()] * 3 + hbm(2),
        out_specs=vmem(),
        scratch_shapes=[
            pltpu.VMEM(col_tokens.shape, BF),
            pltpu.VMEM((heads, row_len, col_len), F32),
            dma((2,)),
        ],
        compiler_params=params(16),
    )(where, order, col_tokens, w_kv, queries, *stay(bias_a, bias_b))

    gathered = lax.all_to_all(partial, "kcol", 0, 0)
    return pl.pallas_call(
        merge_kernel,
        name="merge",
        out_shape=shape((samples, tok, width), BF),
        in_specs=[vmem(), vmem(), vmem()],
        out_specs=vmem(),
        compiler_params=params(8),
    )(gathered, gate, w_out)


def solution(mesh):
    return jax.shard_map(
        shards,
        mesh=mesh,
        in_specs=(
            P(None, ("qrow", "kcol"), None),
            P(("qrow", "kcol")),
            P(),
            P(),
            P("kcol"),
            P("qrow", "kcol", None),
            P(),
            P(),
            P(),
            P(),
            P(),
            P(),
        ),
        out_specs=P(None, ("qrow", "kcol"), None),
        check_vma=False,
    )
```

```python
import functools
import math

import jax
import jax.numpy as jnp
from jax import lax
from jax.experimental import pallas as pl
from jax.experimental.pallas import tpu as pltpu
from jax.sharding import PartitionSpec as P

BF = jnp.bfloat16
F32 = jnp.float32
EPS = 1e-05


def vmem():
    return pl.BlockSpec(memory_space=pltpu.VMEM)


def smem():
    return pl.BlockSpec(memory_space=pltpu.SMEM)


def dot_nt(a, b):
    return lax.dot_general(a, b, (((1,), (1,)), ((), ())), preferred_element_type=F32)


def layer_norm(x):
    centred = x - jnp.mean(x, -1, keepdims=True)
    variance = jnp.mean(centred * centred, -1, keepdims=True)
    return centred * lax.rsqrt(variance + EPS)


def split3(x):
    hi = x.astype(BF)
    rest = x - hi.astype(F32)
    mid = rest.astype(BF)
    low = (rest - mid.astype(F32)).astype(BF)
    return hi, mid, low


def fetch(copies, sems):
    started = [pltpu.make_async_copy(src, dst, sems.at[i]) for i, (src, dst) in enumerate(copies)]
    for copy in started:
        copy.start()
    for copy in started:
        copy.wait()


def norm_kernel(
    restype_hbm, single_hbm, table_hbm, gain_hbm, normed_ref, copies_ref, restype_ref, single_ref, table_ref, gain_ref, sems
):
    fetch(
        [
            (restype_hbm, restype_ref),
            (single_hbm, single_ref),
            (table_hbm, table_ref),
            (gain_hbm, gain_ref),
        ],
        sems,
    )
    samples, tok, width = single_ref.shape
    kinds = table_ref.shape[0]
    row = lax.broadcasted_iota(jnp.int32, (tok, kinds), 0)
    col = lax.broadcasted_iota(jnp.int32, (tok, kinds), 1)
    kind = jnp.zeros((tok, kinds), jnp.int32)
    for t in range(tok):
        kind = jnp.where(row == t, restype_ref[t], kind)
    one_hot = jnp.where(kind == col, 1.0, 0.0).astype(BF)
    emb = jnp.dot(one_hot, table_ref[...], preferred_element_type=F32)
    x = single_ref[...].astype(F32) + emb[None]
    normed = layer_norm(x) * gain_ref[...].reshape(1, 1, width)
    normed = normed.reshape(samples * tok, width).astype(BF)
    normed_ref[...] = normed
    for j in range(copies_ref.shape[0]):
        copies_ref[j] = normed


def copies_kernel(one_ref, two_ref, after_ref, copies_ref):
    per = one_ref.shape[0]
    for j in range(copies_ref.shape[0]):
        copies_ref[j, :per] = one_ref[...]
        copies_ref[j, per:] = two_ref[...]


def bias_kernel(start, late, own_ref, where_ref, *refs):
    ins, refs = refs[:8], refs[8:]
    pair_hbm, w_hbm = ins[6:]
    out_ref, extra_ref, refs = refs[0], refs[1], refs[2:]
    if late:
        wq_ref, refs = refs[0], refs[1:]
    chain_ref, cbias_ref, chain_rows_ref, live_ref, gain_ref, weight_ref, pair_ref, sems, pair_sems = refs[:9]
    w_ref, w_sem = (extra_ref, refs[9]) if late else refs[9:]
    chunks, block, keys, channels = pair_ref.shape
    heads = weight_ref.shape[0]
    width = own_ref.shape[1]
    loads = [
        pltpu.make_async_copy(pair_hbm.at[pl.ds(start + i * block, block)], pair_ref.at[i], pair_sems.at[i])
        for i in range(chunks)
    ]
    for load in loads[:2]:
        load.start()
    small = list(zip(ins[:6], (chain_ref, cbias_ref, chain_rows_ref, live_ref, gain_ref, weight_ref)))
    small = [pltpu.make_async_copy(src, dst, sems.at[i]) for i, (src, dst) in enumerate(small)]
    for load in small + loads[2:]:
        load.start()
    place = pl.ds(width, 2 * width) if late else pl.ds(3 * width, width)
    load_w = [pltpu.make_async_copy(w_hbm.at[:, place], w_ref, w_sem.at[0])]
    if late:
        load_w.append(pltpu.make_async_copy(w_hbm.at[:, pl.ds(0, width)], wq_ref, w_sem.at[1]))
    for load in small:
        load.wait()
    weight = weight_ref[...] * gain_ref[...]
    lhs = jnp.concatenate(split3(weight), 0)
    total = jnp.sum(weight, -1, keepdims=True)
    row = lax.broadcasted_iota(jnp.int32, (heads, keys), 0)
    column = jnp.zeros((heads, keys), F32)
    for h in range(heads):
        column = jnp.where(row == h, cbias_ref[h], column)
    base = where_ref[0] * pair_hbm.shape[0] + start
    col_chain = chain_rows_ref[pl.ds(where_ref[1], 1), :]
    alive = jnp.broadcast_to(live_ref[...] == 1, (heads, keys))
    for i in range(chunks):
        loads[i].wait()
        if i == 0:
            for load in load_w:
                load.start()
        for q in range(0, block, 2):
            turned = pair_ref[i, q : q + 2].reshape(2 * keys, channels).T
            x = turned.astype(F32)
            mean = jnp.sum(x, 0, keepdims=True) * (1.0 / channels)
            centred = x - mean
            variance = jnp.sum(centred * centred, 0, keepdims=True) * (1.0 / channels)
            res = jnp.dot(lhs, turned, preferred_element_type=F32)
            res = res[:heads] + res[heads : 2 * heads] + res[2 * heads :]
            res = (res - total * mean) * lax.rsqrt(variance + EPS)
            for k in range(2):
                at = i * block + q + k
                part = res[:, k * keys : (k + 1) * keys]
                same = col_chain == chain_ref[base + at]
                part = part + jnp.where(same, column, 0.0)
                out_ref[:, at, :] = jnp.where(alive, part, -1e30)
    for load in load_w:
        load.wait()
    if not late:
        pre = jnp.dot(own_ref[...], w_ref[...], preferred_element_type=F32)
        extra_ref[...] = jax.nn.sigmoid(pre)


def query_kernel(where_ref, rows_ref, others_ref, w_ref, q_ref, x_ref):
    near, per, width = rows_ref.shape
    ours = lax.div(where_ref[1], near) * near
    x_ref[pl.ds(ours, near)] = rows_ref[...]
    x_ref[pl.ds(near - ours, near)] = others_ref[...]
    x = x_ref[...].reshape(2 * near * per, width)
    query = jnp.dot(x, w_ref[...], preferred_element_type=F32).reshape(2 * near, 2, per // 2, width)
    for s in range(2):
        q_ref[s] = query[:, s].reshape(near * per, width).astype(BF)


def attend_kernel(
    where_ref, order_ref, cols_ref, wkv_ref, q_ref, bias_a_hbm, bias_b_hbm, out_ref, x_ref, bias_ref, sems
):
    parts, per, width = cols_ref.shape
    half = per // 2
    heads, queries, keys = bias_ref.shape
    few = bias_a_hbm.shape[1]
    size = width // heads
    scale = 1.0 / math.sqrt(size)
    loads = [
        pltpu.make_async_copy(bias_a_hbm, bias_ref.at[:, pl.ds(0, few)], sems.at[0]),
        pltpu.make_async_copy(bias_b_hbm, bias_ref.at[:, pl.ds(few, queries - few)], sems.at[1]),
    ]
    for load in loads:
        load.start()
    base = (where_ref[1] * 2 + lax.rem(lax.div(where_ref[0], 2), 2)) * parts
    for i in range(parts):
        x_ref[pl.ds(order_ref[base + i], 1)] = cols_ref[pl.ds(i, 1)]
    x = x_ref[...].reshape(parts * per, width)

    def project(w):
        return jnp.dot(x, w, preferred_element_type=F32).reshape(parts, 2, half, width)

    kf, vf = project(wkv_ref[:, :width]), project(wkv_ref[:, width:])
    span = 256
    wins = width // span

    def members(t):
        return [h for h in range(heads) if h * size < (t + 1) * span and (h + 1) * size > t * span]

    def mask_of(h, t):
        spot = lax.broadcasted_iota(jnp.int32, (1, span), 1) + t * span
        return jnp.where((spot >= h * size) & (spot < (h + 1) * size), 1.0, 0.0).astype(BF)

    lane = lax.broadcasted_iota(jnp.int32, (queries, 128), 1)
    stats = []
    for s in range(2):
        q = q_ref[s]
        k = kf[:, s].reshape(keys, width).astype(BF)
        v = vf[:, s].reshape(keys, width).astype(BF)
        raw = {}
        for t in range(wins):
            cut = slice(t * span, (t + 1) * span)
            lhs = jnp.concatenate([q[:, cut] * mask_of(h, t) for h in members(t)], 0)
            res = dot_nt(lhs, k[:, cut])
            for i, h in enumerate(members(t)):
                piece = res[i * queries : (i + 1) * queries]
                raw[h] = raw[h] + piece if h in raw else piece
        if s == 0:
            for load in loads:
                load.wait()
        tops = jnp.zeros((queries, 128), F32)
        tots = jnp.zeros((queries, 128), F32)
        rounded = []
        for h in range(heads):
            sc = raw[h] * scale + bias_ref[h]
            top = jnp.max(sc, -1, keepdims=True)
            w = jnp.exp(sc - top)
            rounded.append(w.astype(BF))
            tots = jnp.where(lane == h, jnp.sum(w, -1, keepdims=True), tots)
            tops = jnp.where(lane == h, top, tops)
        for t in range(wins):
            cut = slice(t * span, (t + 1) * span)
            o = jnp.dot(
                jnp.concatenate([rounded[h] for h in members(t)], 1),
                jnp.concatenate([v[:, cut] * mask_of(h, t) for h in members(t)], 0),
                preferred_element_type=F32,
            )
            at = (s * wins + t) * per
            tiles = [o[:, i * 128 : (i + 1) * 128].reshape(parts, half, 128) for i in range(2)]
            out_ref[:, at : at + per, :] = jnp.concatenate(tiles, 1).astype(BF)
        hi, mid, low = split3(tops)
        total_hi, total_low, _ = split3(tots)
        mine = hi.astype(F32)
        for i, p in enumerate((mid, low, total_hi, total_low)):
            mine = mine + pltpu.roll(p.astype(F32), heads * (i + 1), 1)
        stats.append(mine.reshape(parts, half, 128))
    out_ref[:, 2 * wins * per :, :] = jnp.concatenate(stats, 1).astype(BF)


def merge_kernel(parts_ref, gate_ref, wout_ref, out_ref):
    parts, rows, _ = parts_ref.shape
    per, width = gate_ref.shape
    half = per // 2
    tiles = width // 128
    heads = 16
    size = width // heads
    st = parts_ref[:, tiles * per :, :].astype(F32).reshape(parts * per, 128)
    top = st + pltpu.roll(st, 128 - heads, 1) + pltpu.roll(st, 128 - 2 * heads, 1)
    tot = pltpu.roll(st, 128 - 3 * heads, 1) + pltpu.roll(st, 128 - 4 * heads, 1)
    lane = lax.broadcasted_iota(jnp.int32, (parts * per, 128), 1)
    top = jnp.where(lane < heads, top, 0.0).reshape(parts, per, 128)
    tot = jnp.where(lane < heads, tot, 1.0).reshape(parts, per, 128)
    e = jnp.exp(top - jnp.max(top, 0, keepdims=True))
    f = e / jnp.sum(e * tot, 0, keepdims=True)
    f = jnp.where(lane < heads, f.reshape(parts * per, 128), 0.0)
    hrow = lax.broadcasted_iota(jnp.int32, (128, width), 0) * size
    col = lax.broadcasted_iota(jnp.int32, (128, width), 1)
    spread = jnp.where((col >= hrow) & (col < hrow + size), 1.0, 0.0).astype(BF)
    hi = f.astype(BF)
    low = (f - hi.astype(F32)).astype(BF)
    factor = jnp.dot(jnp.concatenate([hi, low], 1), jnp.concatenate([spread, spread], 0), preferred_element_type=F32)
    attended = []
    for i in range(tiles):
        at = [(s * (tiles // 2) + i // 2) * per for s in range(2)]
        num = [parts_ref[:, a : a + per, :].astype(F32)[:, i % 2 * half : i % 2 * half + half] for a in at]
        num = jnp.concatenate(num, 1)
        attended.append(jnp.sum(num * factor[:, i * 128 : (i + 1) * 128].reshape(parts, per, 128), 0))
    gated = (gate_ref[...] * jnp.concatenate(attended, 1)).astype(BF)
    update = jnp.dot(gated, wout_ref[...], preferred_element_type=F32)
    out_ref[...] = update.reshape(out_ref.shape).astype(BF)


def near_swaps(n):
    ring = lambda a, b, size: min((a - b) % size, (b - a) % size)
    upper = lambda i: i // 2 % 2
    tables = ([], [])
    for c in range(n):

        def cost(j, i):
            hops = ring(c // 4, i // 4, 4) + ring(j % 8, c % 8, 8)
            hops += ring(upper(c) * 2 + j // 8, upper(i) * 2 + c // 8, 4)
            return 2 * hops + (c % 2 != i % 2)

        first = {}
        for table in tables:
            for most in range(100):
                taken = {}

                def place(j, seen):
                    for i in range(n):
                        other = j not in first or upper(first[j]) != upper(i)
                        if other and cost(j, i) <= most and i not in seen:
                            seen.add(i)
                            if i not in taken or place(taken[i], seen):
                                taken[i] = j
                                return True
                    return False

                if all(place(j, set()) for j in range(n)):
                    break
            table.append([taken[i] for i in range(n)])
            first = {j: i for i, j in taken.items()}
    return tables


def params(mib):
    return pltpu.CompilerParams(vmem_limit_bytes=mib << 20)


def shards(
    single,
    restype,
    restype_table,
    chain,
    live,
    pair,
    pair_gain,
    pair_weight,
    chain_bias,
    single_gain,
    w_qkvg,
    w_out,
):
    samples, tok, width = single.shape
    row_len, col_len, channels = pair.shape
    heads = chain_bias.shape[0]
    n_row, n_col = lax.axis_size("qrow"), lax.axis_size("kcol")
    shape = jax.ShapeDtypeStruct
    own = samples * tok

    stay = lambda *arrays: [pltpu.with_memory_space_constraint(x, pltpu.HBM) for x in arrays]
    hbm = lambda count: [pl.BlockSpec(memory_space=pltpu.HBM)] * count
    dma = pltpu.SemaphoreType.DMA
    normed, copies = pl.pallas_call(
        norm_kernel,
        name="norm",
        out_shape=(shape((own, width), BF), shape((n_col // 2, own, width), BF)),
        in_specs=hbm(4),
        out_specs=(vmem(), vmem()),
        scratch_shapes=[
            pltpu.SMEM((tok,), jnp.int32),
            pltpu.VMEM((samples, tok, width), BF),
            pltpu.VMEM(restype_table.shape, BF),
            pltpu.VMEM((width,), F32),
            dma((4,)),
        ],
        compiler_params=params(4),
    )(*stay(restype, single, restype_table, single_gain))

    tables = near_swaps(n_row)
    turned = []
    for table in tables:
        swap = [(c * n_col + j, i * n_col + c) for c in range(n_row) for i, j in enumerate(table[c])]
        turned.append(lax.ppermute(normed, ("qrow", "kcol"), swap))
    near = [list(range(n_col // 2)), list(range(n_col // 2, n_col))]
    row_tokens = lax.all_to_all(copies, "kcol", 0, 0, axis_index_groups=near)

    where = jnp.stack([lax.axis_index("qrow"), lax.axis_index("kcol")]).astype(jnp.int32)
    block = row_len // 8

    def bias_of(late):
        chunks = 4
        out = [pltpu.HBM((heads, chunks * block, col_len), F32)]
        out += [shape((width, 2 * width), BF) if late else pltpu.HBM((own, width), F32)]
        out += [shape((width, width), BF)] * late
        return pl.pallas_call(
            functools.partial(bias_kernel, late * chunks * block, late),
            name="bias_" + str(late),
            out_shape=out,
            in_specs=[vmem(), smem()] + hbm(8),
            out_specs=[vmem()] * len(out),
            scratch_shapes=[
                pltpu.SMEM(chain.shape, jnp.int32),
                pltpu.SMEM((heads,), F32),
                pltpu.VMEM((chain.shape[0] // col_len, col_len), jnp.int32),
                pltpu.VMEM((1, col_len), jnp.int32),
                pltpu.VMEM((1, channels), F32),
                pltpu.VMEM((heads, channels), F32),
                pltpu.VMEM((chunks, block, col_len, channels), BF),
                dma((6,)),
                dma((chunks,)),
            ]
            + ([] if late else [pltpu.VMEM((width, width), BF)])
            + [dma((2,))],
            compiler_params=params(10),
            cost_estimate=pl.CostEstimate(flops=5 * 10**8, bytes_accessed=10 * 10**6, transcendentals=0),
        )(
            normed,
            where,
            *stay(
                chain,
                chain_bias,
                chain.reshape(-1, col_len),
                live.reshape(1, col_len),
                pair_gain.reshape(1, channels),
                pair_weight.T,
                pair,
                w_qkvg,
            ),
        )

    bias_a, gate = bias_of(0)
    bias_b, w_kv, w_q = bias_of(1)
    sides = [[i for i in range(n_row) if i // 2 % 2 == side] for side in range(2)]
    turned_copies = pl.pallas_call(
        copies_kernel,
        name="copies",
        out_shape=shape((n_row // 2, 2 * own, width), BF),
        in_specs=[vmem()] * 2 + hbm(1),
        out_specs=vmem(),
        compiler_params=params(4),
    )(*turned, *stay(bias_a))
    turned_copies, row_tokens = lax.optimization_barrier((turned_copies, row_tokens))
    col_tokens = lax.all_to_all(turned_copies, "qrow", 0, 0, axis_index_groups=sides)
    other_tokens = lax.ppermute(row_tokens, "kcol", [(i, (i + n_col // 2) % n_col) for i in range(n_col)])
    col_tokens = col_tokens.reshape(n_row, own, width)
    queries = pl.pallas_call(
        query_kernel,
        name="query",
        out_shape=shape((samples, row_len, width), BF),
        in_specs=[smem()] + [vmem()] * 3,
        out_specs=vmem(),
        scratch_shapes=[pltpu.VMEM((n_col, own, width), BF)],
        compiler_params=params(6),
    )(where, row_tokens, other_tokens, w_q)
    order = [tables[k][c][i] for c in range(n_col) for side in sides for i in side for k in range(2)]
    order = jnp.asarray(order, jnp.int32)

    rows = own * width // 128 + own
    partial = pl.pallas_call(
        attend_kernel,
        name="attend",
        out_shape=shape((n_col, rows, 128), BF),
        in_specs=[smem()] * 2 + [vmem()] * 3 + hbm(2),
        out_specs=vmem(),
        scratch_shapes=[
            pltpu.VMEM(col_tokens.shape, BF),
            pltpu.VMEM((heads, row_len, col_len), F32),
            dma((2,)),
        ],
        compiler_params=params(16),
    )(where, order, col_tokens, w_kv, queries, *stay(bias_a, bias_b))

    gathered = lax.all_to_all(partial, "kcol", 0, 0)
    return pl.pallas_call(
        merge_kernel,
        name="merge",
        out_shape=shape((samples, tok, width), BF),
        in_specs=[vmem(), vmem(), vmem()],
        out_specs=vmem(),
        compiler_params=params(8),
    )(gathered, gate, w_out)


def solution(mesh):
    return jax.shard_map(
        shards,
        mesh=mesh,
        in_specs=(
            P(None, ("qrow", "kcol"), None),
            P(("qrow", "kcol")),
            P(),
            P(),
            P("kcol"),
            P("qrow", "kcol", None),
            P(),
            P(),
            P(),
            P(),
            P(),
            P(),
        ),
        out_specs=P(None, ("qrow", "kcol"), None),
        check_vma=False,
    )
```

```python
import functools
import math

import jax
import jax.numpy as jnp
from jax import lax
from jax.experimental import pallas as pl
from jax.experimental.pallas import tpu as pltpu
from jax.sharding import PartitionSpec as P

BF = jnp.bfloat16
F32 = jnp.float32
EPS = 1e-05


def vmem():
    return pl.BlockSpec(memory_space=pltpu.VMEM)


def smem():
    return pl.BlockSpec(memory_space=pltpu.SMEM)


def dot_nt(a, b):
    return lax.dot_general(a, b, (((1,), (1,)), ((), ())), preferred_element_type=F32)


def layer_norm(x):
    centred = x - jnp.mean(x, -1, keepdims=True)
    variance = jnp.mean(centred * centred, -1, keepdims=True)
    return centred * lax.rsqrt(variance + EPS)


def split3(x):
    hi = x.astype(BF)
    rest = x - hi.astype(F32)
    mid = rest.astype(BF)
    low = (rest - mid.astype(F32)).astype(BF)
    return hi, mid, low


def fetch(copies, sems):
    started = [pltpu.make_async_copy(src, dst, sems.at[i]) for i, (src, dst) in enumerate(copies)]
    for copy in started:
        copy.start()
    for copy in started:
        copy.wait()


def norm_kernel(
    restype_hbm, single_hbm, table_hbm, gain_hbm, normed_ref, copies_ref, restype_ref, single_ref, table_ref, gain_ref, sems
):
    fetch(
        [
            (restype_hbm, restype_ref),
            (single_hbm, single_ref),
            (table_hbm, table_ref),
            (gain_hbm, gain_ref),
        ],
        sems,
    )
    rows, width = single_ref.shape
    tok = restype_ref.shape[0]
    samples = rows // tok
    kinds = table_ref.shape[0]
    row = lax.broadcasted_iota(jnp.int32, (tok, kinds), 0)
    col = lax.broadcasted_iota(jnp.int32, (tok, kinds), 1)
    kind = jnp.zeros((tok, kinds), jnp.int32)
    for t in range(tok):
        kind = jnp.where(row == t, restype_ref[t], kind)
    one_hot = jnp.where(kind == col, 1.0, 0.0).astype(BF)
    emb = jnp.dot(one_hot, table_ref[...], preferred_element_type=F32)
    x = single_ref[...].astype(F32).reshape(samples, tok, width) + emb[None]
    normed = layer_norm(x) * gain_ref[...].reshape(1, 1, width)
    normed = normed.reshape(samples * tok, width).astype(BF)
    normed_ref[...] = normed
    for j in range(copies_ref.shape[0]):
        copies_ref[j] = normed


def copies_kernel(one_ref, two_ref, after_ref, copies_ref):
    per = one_ref.shape[0]
    for j in range(copies_ref.shape[0]):
        copies_ref[j, :per] = one_ref[...]
        copies_ref[j, per:] = two_ref[...]


def bias_kernel(start, late, own_ref, where_ref, *refs):
    ins, refs = refs[:8], refs[8:]
    pair_hbm, w_hbm = ins[6:]
    out_ref, extra_ref, refs = refs[0], refs[1], refs[2:]
    if late:
        wq_ref, refs = refs[0], refs[1:]
    chain_ref, cbias_ref, chain_rows_ref, live_ref, gain_ref, weight_ref, pair_ref, sems, pair_sems = refs[:9]
    w_ref, w_sem = (extra_ref, refs[9]) if late else refs[9:]
    chunks, block, keys, channels = pair_ref.shape
    heads = weight_ref.shape[0]
    width = own_ref.shape[1]
    loads = [
        pltpu.make_async_copy(pair_hbm.at[pl.ds(start + i * block, block)], pair_ref.at[i], pair_sems.at[i])
        for i in range(chunks)
    ]
    for load in loads[:2]:
        load.start()
    small = list(zip(ins[:6], (chain_ref, cbias_ref, chain_rows_ref, live_ref, gain_ref, weight_ref)))
    small = [pltpu.make_async_copy(src, dst, sems.at[i]) for i, (src, dst) in enumerate(small)]
    for load in small + loads[2:]:
        load.start()
    place = pl.ds(width, 2 * width) if late else pl.ds(3 * width, width)
    load_w = [pltpu.make_async_copy(w_hbm.at[:, place], w_ref, w_sem.at[0])]
    if late:
        load_w.append(pltpu.make_async_copy(w_hbm.at[:, pl.ds(0, width)], wq_ref, w_sem.at[1]))
    for load in small:
        load.wait()
    weight = weight_ref[...] * gain_ref[...]
    lhs = jnp.concatenate(split3(weight), 0)
    total = jnp.sum(weight, -1, keepdims=True)
    row = lax.broadcasted_iota(jnp.int32, (heads, keys), 0)
    column = jnp.zeros((heads, keys), F32)
    for h in range(heads):
        column = jnp.where(row == h, cbias_ref[h], column)
    base = where_ref[0] * pair_hbm.shape[0] + start
    col_chain = chain_rows_ref[pl.ds(where_ref[1], 1), :]
    alive = jnp.broadcast_to(live_ref[...] == 1, (heads, keys))
    for i in range(chunks):
        loads[i].wait()
        if i == 0:
            for load in load_w:
                load.start()
        for q in range(0, block, 2):
            turned = pair_ref[i, q : q + 2].reshape(2 * keys, channels).T
            x = turned.astype(F32)
            mean = jnp.sum(x, 0, keepdims=True) * (1.0 / channels)
            centred = x - mean
            variance = jnp.sum(centred * centred, 0, keepdims=True) * (1.0 / channels)
            res = jnp.dot(lhs, turned, preferred_element_type=F32)
            res = res[:heads] + res[heads : 2 * heads] + res[2 * heads :]
            res = (res - total * mean) * lax.rsqrt(variance + EPS)
            for k in range(2):
                at = i * block + q + k
                part = res[:, k * keys : (k + 1) * keys]
                same = col_chain == chain_ref[base + at]
                part = part + jnp.where(same, column, 0.0)
                out_ref[:, at, :] = jnp.where(alive, part, -1e30)
    for load in load_w:
        load.wait()
    if not late:
        pre = jnp.dot(own_ref[...], w_ref[...], preferred_element_type=F32)
        extra_ref[...] = jax.nn.sigmoid(pre)


def query_kernel(where_ref, rows_ref, others_ref, w_ref, q_ref, x_ref):
    near, per, width = rows_ref.shape
    ours = lax.div(where_ref[1], near) * near
    x_ref[pl.ds(ours, near)] = rows_ref[...]
    x_ref[pl.ds(near - ours, near)] = others_ref[...]
    x = x_ref[...].reshape(2 * near * per, width)
    query = jnp.dot(x, w_ref[...], preferred_element_type=F32).reshape(2 * near, 2, per // 2, width)
    for s in range(2):
        q_ref[s] = query[:, s].reshape(near * per, width).astype(BF)


def attend_kernel(
    where_ref, order_ref, cols_ref, wkv_ref, q_ref, bias_a_hbm, bias_b_hbm, out_ref, x_ref, bias_ref, sems
):
    parts, per, width = cols_ref.shape
    half = per // 2
    heads, queries, keys = bias_ref.shape
    few = bias_a_hbm.shape[1]
    size = width // heads
    scale = 1.0 / math.sqrt(size)
    loads = [
        pltpu.make_async_copy(bias_a_hbm, bias_ref.at[:, pl.ds(0, few)], sems.at[0]),
        pltpu.make_async_copy(bias_b_hbm, bias_ref.at[:, pl.ds(few, queries - few)], sems.at[1]),
    ]
    for load in loads:
        load.start()
    base = (where_ref[1] * 2 + lax.rem(lax.div(where_ref[0], 2), 2)) * parts
    for i in range(parts):
        x_ref[pl.ds(order_ref[base + i], 1)] = cols_ref[pl.ds(i, 1)]
    x = x_ref[...].reshape(parts * per, width)

    def project(w):
        return jnp.dot(x, w, preferred_element_type=F32).reshape(parts, 2, half, width)

    kf, vf = project(wkv_ref[:, :width]), project(wkv_ref[:, width:])
    span = 256
    wins = width // span

    def members(t):
        return [h for h in range(heads) if h * size < (t + 1) * span and (h + 1) * size > t * span]

    def mask_of(h, t):
        spot = lax.broadcasted_iota(jnp.int32, (1, span), 1) + t * span
        return jnp.where((spot >= h * size) & (spot < (h + 1) * size), 1.0, 0.0).astype(BF)

    lane = lax.broadcasted_iota(jnp.int32, (queries, 128), 1)
    stats = []
    for s in range(2):
        q = q_ref[s]
        k = kf[:, s].reshape(keys, width).astype(BF)
        v = vf[:, s].reshape(keys, width).astype(BF)
        raw = {}
        for t in range(wins):
            cut = slice(t * span, (t + 1) * span)
            lhs = jnp.concatenate([q[:, cut] * mask_of(h, t) for h in members(t)], 0)
            res = dot_nt(lhs, k[:, cut])
            for i, h in enumerate(members(t)):
                piece = res[i * queries : (i + 1) * queries]
                raw[h] = raw[h] + piece if h in raw else piece
        if s == 0:
            for load in loads:
                load.wait()
        tops = jnp.zeros((queries, 128), F32)
        tots = jnp.zeros((queries, 128), F32)
        rounded = []
        for h in range(heads):
            sc = raw[h] * scale + bias_ref[h]
            top = jnp.max(sc, -1, keepdims=True)
            w = jnp.exp(sc - top)
            rounded.append(w.astype(BF))
            tots = jnp.where(lane == h, jnp.sum(w, -1, keepdims=True), tots)
            tops = jnp.where(lane == h, top, tops)
        for t in range(wins):
            cut = slice(t * span, (t + 1) * span)
            o = jnp.dot(
                jnp.concatenate([rounded[h] for h in members(t)], 1),
                jnp.concatenate([v[:, cut] * mask_of(h, t) for h in members(t)], 0),
                preferred_element_type=F32,
            )
            at = (s * wins + t) * per
            tiles = [o[:, i * 128 : (i + 1) * 128].reshape(parts, half, 128) for i in range(2)]
            out_ref[:, at : at + per, :] = jnp.concatenate(tiles, 1).astype(BF)
        hi, mid, low = split3(tops)
        total_hi, total_low, _ = split3(tots)
        mine = hi.astype(F32)
        for i, p in enumerate((mid, low, total_hi, total_low)):
            mine = mine + pltpu.roll(p.astype(F32), heads * (i + 1), 1)
        stats.append(mine.reshape(parts, half, 128))
    out_ref[:, 2 * wins * per :, :] = jnp.concatenate(stats, 1).astype(BF)


def merge_kernel(parts_ref, gate_ref, wout_ref, out_ref):
    parts, rows, _ = parts_ref.shape
    per, width = gate_ref.shape
    half = per // 2
    tiles = width // 128
    heads = 16
    size = width // heads
    st = parts_ref[:, tiles * per :, :].astype(F32).reshape(parts * per, 128)
    top = st + pltpu.roll(st, 128 - heads, 1) + pltpu.roll(st, 128 - 2 * heads, 1)
    tot = pltpu.roll(st, 128 - 3 * heads, 1) + pltpu.roll(st, 128 - 4 * heads, 1)
    lane = lax.broadcasted_iota(jnp.int32, (parts * per, 128), 1)
    top = jnp.where(lane < heads, top, 0.0).reshape(parts, per, 128)
    tot = jnp.where(lane < heads, tot, 1.0).reshape(parts, per, 128)
    e = jnp.exp(top - jnp.max(top, 0, keepdims=True))
    f = e / jnp.sum(e * tot, 0, keepdims=True)
    f = jnp.where(lane < heads, f.reshape(parts * per, 128), 0.0)
    hrow = lax.broadcasted_iota(jnp.int32, (128, width), 0) * size
    col = lax.broadcasted_iota(jnp.int32, (128, width), 1)
    spread = jnp.where((col >= hrow) & (col < hrow + size), 1.0, 0.0).astype(BF)
    hi = f.astype(BF)
    low = (f - hi.astype(F32)).astype(BF)
    factor = jnp.dot(jnp.concatenate([hi, low], 1), jnp.concatenate([spread, spread], 0), preferred_element_type=F32)
    attended = []
    for i in range(tiles):
        at = [(s * (tiles // 2) + i // 2) * per for s in range(2)]
        num = [parts_ref[:, a : a + per, :].astype(F32)[:, i % 2 * half : i % 2 * half + half] for a in at]
        num = jnp.concatenate(num, 1)
        attended.append(jnp.sum(num * factor[:, i * 128 : (i + 1) * 128].reshape(parts, per, 128), 0))
    gated = (gate_ref[...] * jnp.concatenate(attended, 1)).astype(BF)
    update = jnp.dot(gated, wout_ref[...], preferred_element_type=F32)
    out_ref[...] = update.reshape(out_ref.shape).astype(BF)


def near_swaps(n):
    ring = lambda a, b, size: min((a - b) % size, (b - a) % size)
    upper = lambda i: i // 2 % 2
    tables = ([], [])
    for c in range(n):

        def cost(j, i):
            hops = ring(c // 4, i // 4, 4) + ring(j % 8, c % 8, 8)
            hops += ring(upper(c) * 2 + j // 8, upper(i) * 2 + c // 8, 4)
            return 2 * hops + (c % 2 != i % 2)

        first = {}
        for table in tables:
            for most in range(100):
                taken = {}

                def place(j, seen):
                    for i in range(n):
                        other = j not in first or upper(first[j]) != upper(i)
                        if other and cost(j, i) <= most and i not in seen:
                            seen.add(i)
                            if i not in taken or place(taken[i], seen):
                                taken[i] = j
                                return True
                    return False

                if all(place(j, set()) for j in range(n)):
                    break
            table.append([taken[i] for i in range(n)])
            first = {j: i for i, j in taken.items()}
    return tables


def params(mib):
    return pltpu.CompilerParams(vmem_limit_bytes=mib << 20)


def shards(
    single,
    restype,
    restype_table,
    chain,
    live,
    pair,
    pair_gain,
    pair_weight,
    chain_bias,
    single_gain,
    w_qkvg,
    w_out,
):
    samples, tok, width = single.shape
    row_len, col_len, channels = pair.shape
    heads = chain_bias.shape[0]
    n_row, n_col = lax.axis_size("qrow"), lax.axis_size("kcol")
    shape = jax.ShapeDtypeStruct
    own = samples * tok

    stay = lambda *arrays: [pltpu.with_memory_space_constraint(x, pltpu.HBM) for x in arrays]
    hbm = lambda count: [pl.BlockSpec(memory_space=pltpu.HBM)] * count
    dma = pltpu.SemaphoreType.DMA
    normed, copies = pl.pallas_call(
        norm_kernel,
        name="norm",
        out_shape=(shape((own, width), BF), shape((n_col // 2, own, width), BF)),
        in_specs=hbm(4),
        out_specs=(vmem(), vmem()),
        scratch_shapes=[
            pltpu.SMEM((tok,), jnp.int32),
            pltpu.VMEM((own, width), BF),
            pltpu.VMEM(restype_table.shape, BF),
            pltpu.VMEM((width,), F32),
            dma((4,)),
        ],
        compiler_params=params(4),
    )(*stay(restype, single.reshape(own, width), restype_table, single_gain))

    tables = near_swaps(n_row)
    turned = []
    for table in tables:
        swap = [(c * n_col + j, i * n_col + c) for c in range(n_row) for i, j in enumerate(table[c])]
        turned.append(lax.ppermute(normed, ("qrow", "kcol"), swap))
    near = [list(range(n_col // 2)), list(range(n_col // 2, n_col))]
    row_tokens = lax.all_to_all(copies, "kcol", 0, 0, axis_index_groups=near)

    where = jnp.stack([lax.axis_index("qrow"), lax.axis_index("kcol")]).astype(jnp.int32)
    block = row_len // 8

    def bias_of(late):
        chunks = 4
        out = [pltpu.HBM((heads, chunks * block, col_len), F32)]
        out += [shape((width, 2 * width), BF) if late else pltpu.HBM((own, width), F32)]
        out += [shape((width, width), BF)] * late
        return pl.pallas_call(
            functools.partial(bias_kernel, late * chunks * block, late),
            name="bias_" + str(late),
            out_shape=out,
            in_specs=[vmem(), smem()] + hbm(8),
            out_specs=[vmem()] * len(out),
            scratch_shapes=[
                pltpu.SMEM(chain.shape, jnp.int32),
                pltpu.SMEM((heads,), F32),
                pltpu.VMEM((chain.shape[0] // col_len, col_len), jnp.int32),
                pltpu.VMEM((1, col_len), jnp.int32),
                pltpu.VMEM((1, channels), F32),
                pltpu.VMEM((heads, channels), F32),
                pltpu.VMEM((chunks, block, col_len, channels), BF),
                dma((6,)),
                dma((chunks,)),
            ]
            + ([] if late else [pltpu.VMEM((width, width), BF)])
            + [dma((2,))],
            compiler_params=params(10),
            cost_estimate=pl.CostEstimate(flops=5 * 10**8, bytes_accessed=10 * 10**6, transcendentals=0),
        )(
            normed,
            where,
            *stay(
                chain,
                chain_bias,
                chain.reshape(-1, col_len),
                live.reshape(1, col_len),
                pair_gain.reshape(1, channels),
                pair_weight.T,
                pair,
                w_qkvg,
            ),
        )

    bias_a, gate = bias_of(0)
    bias_b, w_kv, w_q = bias_of(1)
    sides = [[i for i in range(n_row) if i // 2 % 2 == side] for side in range(2)]
    turned_copies = pl.pallas_call(
        copies_kernel,
        name="copies",
        out_shape=shape((n_row // 2, 2 * own, width), BF),
        in_specs=[vmem()] * 2 + hbm(1),
        out_specs=vmem(),
        compiler_params=params(4),
    )(*turned, *stay(bias_a))
    turned_copies, row_tokens = lax.optimization_barrier((turned_copies, row_tokens))
    col_tokens = lax.all_to_all(turned_copies, "qrow", 0, 0, axis_index_groups=sides)
    other_tokens = lax.ppermute(row_tokens, "kcol", [(i, (i + n_col // 2) % n_col) for i in range(n_col)])
    col_tokens = col_tokens.reshape(n_row, own, width)
    queries = pl.pallas_call(
        query_kernel,
        name="query",
        out_shape=shape((samples, row_len, width), BF),
        in_specs=[smem()] + [vmem()] * 3,
        out_specs=vmem(),
        scratch_shapes=[pltpu.VMEM((n_col, own, width), BF)],
        compiler_params=params(6),
    )(where, row_tokens, other_tokens, w_q)
    order = [tables[k][c][i] for c in range(n_col) for side in sides for i in side for k in range(2)]
    order = jnp.asarray(order, jnp.int32)

    rows = own * width // 128 + own
    partial = pl.pallas_call(
        attend_kernel,
        name="attend",
        out_shape=shape((n_col, rows, 128), BF),
        in_specs=[smem()] * 2 + [vmem()] * 3 + hbm(2),
        out_specs=vmem(),
        scratch_shapes=[
            pltpu.VMEM(col_tokens.shape, BF),
            pltpu.VMEM((heads, row_len, col_len), F32),
            dma((2,)),
        ],
        compiler_params=params(16),
    )(where, order, col_tokens, w_kv, queries, *stay(bias_a, bias_b))

    gathered = lax.all_to_all(partial, "kcol", 0, 0)
    return pl.pallas_call(
        merge_kernel,
        name="merge",
        out_shape=shape((samples, tok, width), BF),
        in_specs=[vmem(), vmem(), vmem()],
        out_specs=vmem(),
        compiler_params=params(8),
    )(gathered, gate, w_out)


def solution(mesh):
    return jax.shard_map(
        shards,
        mesh=mesh,
        in_specs=(
            P(None, ("qrow", "kcol"), None),
            P(("qrow", "kcol")),
            P(),
            P(),
            P("kcol"),
            P("qrow", "kcol", None),
            P(),
            P(),
            P(),
            P(),
            P(),
            P(),
        ),
        out_specs=P(None, ("qrow", "kcol"), None),
        check_vma=False,
    )
```

```python
import functools
import math

import jax
import jax.numpy as jnp
from jax import lax
from jax.experimental import pallas as pl
from jax.experimental.pallas import tpu as pltpu
from jax.sharding import PartitionSpec as P

BF = jnp.bfloat16
F32 = jnp.float32
EPS = 1e-05


def vmem():
    return pl.BlockSpec(memory_space=pltpu.VMEM)


def smem():
    return pl.BlockSpec(memory_space=pltpu.SMEM)


def dot_nt(a, b):
    return lax.dot_general(a, b, (((1,), (1,)), ((), ())), preferred_element_type=F32)


def layer_norm(x):
    centred = x - jnp.mean(x, -1, keepdims=True)
    variance = jnp.mean(centred * centred, -1, keepdims=True)
    return centred * lax.rsqrt(variance + EPS)


def split3(x):
    hi = x.astype(BF)
    rest = x - hi.astype(F32)
    mid = rest.astype(BF)
    low = (rest - mid.astype(F32)).astype(BF)
    return hi, mid, low


def fetch(copies, sems):
    started = [pltpu.make_async_copy(src, dst, sems.at[i]) for i, (src, dst) in enumerate(copies)]
    for copy in started:
        copy.start()
    for copy in started:
        copy.wait()


def norm_kernel(
    restype_hbm, single_hbm, table_hbm, gain_hbm, normed_ref, copies_ref, restype_ref, single_ref, table_ref, gain_ref, sems
):
    fetch(
        [
            (restype_hbm, restype_ref),
            (single_hbm, single_ref),
            (table_hbm, table_ref),
            (gain_hbm, gain_ref),
        ],
        sems,
    )
    rows, width = single_ref.shape
    tok = restype_ref.shape[0]
    samples = rows // tok
    kinds = table_ref.shape[0]
    row = lax.broadcasted_iota(jnp.int32, (tok, kinds), 0)
    col = lax.broadcasted_iota(jnp.int32, (tok, kinds), 1)
    kind = jnp.zeros((tok, kinds), jnp.int32)
    for t in range(tok):
        kind = jnp.where(row == t, restype_ref[t], kind)
    one_hot = jnp.where(kind == col, 1.0, 0.0).astype(BF)
    emb = jnp.dot(one_hot, table_ref[...], preferred_element_type=F32)
    x = single_ref[...].astype(F32).reshape(samples, tok, width) + emb[None]
    normed = layer_norm(x) * gain_ref[...].reshape(1, 1, width)
    normed = normed.reshape(samples * tok, width).astype(BF)
    normed_ref[...] = normed
    for j in range(copies_ref.shape[0]):
        copies_ref[j] = normed


def copies_kernel(one_ref, two_ref, after_ref, copies_ref):
    per = one_ref.shape[0]
    for j in range(copies_ref.shape[0]):
        copies_ref[j, :per] = one_ref[...]
        copies_ref[j, per:] = two_ref[...]


def bias_kernel(start, late, own_ref, where_ref, *refs):
    ins, refs = refs[:8], refs[8:]
    pair_hbm, w_hbm = ins[6:]
    out_ref, extra_ref, refs = refs[0], refs[1], refs[2:]
    if late:
        wq_ref, refs = refs[0], refs[1:]
    chain_ref, cbias_ref, chain_rows_ref, live_ref, gain_ref, weight_ref, pair_ref, sems, pair_sems = refs[:9]
    w_ref, w_sem = (extra_ref, refs[9]) if late else refs[9:]
    chunks, block, keys, channels = pair_ref.shape
    heads = weight_ref.shape[0]
    width = own_ref.shape[1]
    loads = [
        pltpu.make_async_copy(pair_hbm.at[pl.ds(start + i * block, block)], pair_ref.at[i], pair_sems.at[i])
        for i in range(chunks)
    ]
    for load in loads[:2]:
        load.start()
    small = list(zip(ins[:6], (chain_ref, cbias_ref, chain_rows_ref, live_ref, gain_ref, weight_ref)))
    small = [pltpu.make_async_copy(src, dst, sems.at[i]) for i, (src, dst) in enumerate(small)]
    for load in small + loads[2:]:
        load.start()
    place = pl.ds(width, 2 * width) if late else pl.ds(3 * width, width)
    load_w = [pltpu.make_async_copy(w_hbm.at[:, place], w_ref, w_sem.at[0])]
    if late:
        load_w.append(pltpu.make_async_copy(w_hbm.at[:, pl.ds(0, width)], wq_ref, w_sem.at[1]))
    for load in small:
        load.wait()
    weight = weight_ref[...] * gain_ref[...]
    lhs = jnp.concatenate(split3(weight), 0)
    total = jnp.sum(weight, -1, keepdims=True)
    row = lax.broadcasted_iota(jnp.int32, (heads, keys), 0)
    column = jnp.zeros((heads, keys), F32)
    for h in range(heads):
        column = jnp.where(row == h, cbias_ref[h], column)
    base = where_ref[0] * pair_hbm.shape[0] + start
    col_chain = chain_rows_ref[pl.ds(where_ref[1], 1), :]
    alive = jnp.broadcast_to(live_ref[...] == 1, (heads, keys))
    for i in range(chunks):
        loads[i].wait()
        if i == 0:
            for load in load_w:
                load.start()
        for q in range(0, block, 2):
            turned = pair_ref[i, q : q + 2].reshape(2 * keys, channels).T
            x = turned.astype(F32)
            mean = jnp.sum(x, 0, keepdims=True) * (1.0 / channels)
            centred = x - mean
            variance = jnp.sum(centred * centred, 0, keepdims=True) * (1.0 / channels)
            res = jnp.dot(lhs, turned, preferred_element_type=F32)
            res = res[:heads] + res[heads : 2 * heads] + res[2 * heads :]
            res = (res - total * mean) * lax.rsqrt(variance + EPS)
            for k in range(2):
                at = i * block + q + k
                part = res[:, k * keys : (k + 1) * keys]
                same = col_chain == chain_ref[base + at]
                part = part + jnp.where(same, column, 0.0)
                out_ref[:, at, :] = jnp.where(alive, part, -1e30)
    for load in load_w:
        load.wait()
    if not late:
        pre = jnp.dot(own_ref[...], w_ref[...], preferred_element_type=F32)
        extra_ref[...] = jax.nn.sigmoid(pre)


def query_kernel(where_ref, rows_ref, others_ref, w_ref, q_ref, x_ref):
    near, per, width = rows_ref.shape
    ours = lax.div(where_ref[1], near) * near
    x_ref[pl.ds(ours, near)] = rows_ref[...]
    x_ref[pl.ds(near - ours, near)] = others_ref[...]
    x = x_ref[...].reshape(2 * near * per, width)
    query = jnp.dot(x, w_ref[...], preferred_element_type=F32).reshape(2 * near, 2, per // 2, width)
    for s in range(2):
        q_ref[s] = query[:, s].reshape(near * per, width).astype(BF)


def attend_kernel(
    where_ref, order_ref, cols_ref, wkv_ref, q_ref, bias_a_hbm, bias_b_hbm, out_ref, x_ref, bias_ref, sems
):
    parts, per, width = cols_ref.shape
    half = per // 2
    heads, queries, keys = bias_ref.shape
    few = bias_a_hbm.shape[1]
    size = width // heads
    scale = 1.0 / math.sqrt(size)
    loads = [
        pltpu.make_async_copy(bias_a_hbm, bias_ref.at[:, pl.ds(0, few)], sems.at[0]),
        pltpu.make_async_copy(bias_b_hbm, bias_ref.at[:, pl.ds(few, queries - few)], sems.at[1]),
    ]
    for load in loads:
        load.start()
    base = (where_ref[1] * 2 + lax.rem(lax.div(where_ref[0], 2), 2)) * parts
    for i in range(parts):
        x_ref[pl.ds(order_ref[base + i], 1)] = cols_ref[pl.ds(i, 1)]
    x = x_ref[...].reshape(parts * per, width)

    def project(w):
        return jnp.dot(x, w, preferred_element_type=F32).reshape(parts, 2, half, width)

    kf, vf = project(wkv_ref[:, :width]), project(wkv_ref[:, width:])
    span = 256
    wins = width // span

    def members(t):
        return [h for h in range(heads) if h * size < (t + 1) * span and (h + 1) * size > t * span]

    def mask_of(h, t):
        spot = lax.broadcasted_iota(jnp.int32, (1, span), 1) + t * span
        return jnp.where((spot >= h * size) & (spot < (h + 1) * size), 1.0, 0.0).astype(BF)

    lane = lax.broadcasted_iota(jnp.int32, (queries, 128), 1)
    stats = []
    for s in range(2):
        q = q_ref[s]
        k = kf[:, s].reshape(keys, width).astype(BF)
        v = vf[:, s].reshape(keys, width).astype(BF)
        raw = {}
        for t in range(wins):
            cut = slice(t * span, (t + 1) * span)
            lhs = jnp.concatenate([q[:, cut] * mask_of(h, t) for h in members(t)], 0)
            res = dot_nt(lhs, k[:, cut])
            for i, h in enumerate(members(t)):
                piece = res[i * queries : (i + 1) * queries]
                raw[h] = raw[h] + piece if h in raw else piece
        if s == 0:
            for load in loads:
                load.wait()
        tops = jnp.zeros((queries, 128), F32)
        tots = jnp.zeros((queries, 128), F32)
        rounded = []
        for h in range(heads):
            sc = raw[h] * scale + bias_ref[h]
            top = jnp.max(sc, -1, keepdims=True)
            w = jnp.exp(sc - top)
            rounded.append(w.astype(BF))
            tots = jnp.where(lane == h, jnp.sum(w, -1, keepdims=True), tots)
            tops = jnp.where(lane == h, top, tops)
        for t in range(wins):
            cut = slice(t * span, (t + 1) * span)
            o = jnp.dot(
                jnp.concatenate([rounded[h] for h in members(t)], 1),
                jnp.concatenate([v[:, cut] * mask_of(h, t) for h in members(t)], 0),
                preferred_element_type=F32,
            )
            at = (s * wins + t) * per
            tiles = [o[:, i * 128 : (i + 1) * 128].reshape(parts, half, 128) for i in range(2)]
            out_ref[:, at : at + per, :] = jnp.concatenate(tiles, 1).astype(BF)
        hi, mid, low = split3(tops)
        total_hi, total_low, _ = split3(tots)
        mine = hi.astype(F32)
        for i, p in enumerate((mid, low, total_hi, total_low)):
            mine = mine + pltpu.roll(p.astype(F32), heads * (i + 1), 1)
        stats.append(mine.reshape(parts, half, 128))
    out_ref[:, 2 * wins * per :, :] = jnp.concatenate(stats, 1).astype(BF)


def merge_kernel(parts_ref, gate_ref, wout_ref, out_ref):
    parts, rows, _ = parts_ref.shape
    per, width = gate_ref.shape
    half = per // 2
    tiles = width // 128
    heads = 16
    size = width // heads
    st = parts_ref[:, tiles * per :, :].astype(F32).reshape(parts * per, 128)
    top = st + pltpu.roll(st, 128 - heads, 1) + pltpu.roll(st, 128 - 2 * heads, 1)
    tot = pltpu.roll(st, 128 - 3 * heads, 1) + pltpu.roll(st, 128 - 4 * heads, 1)
    lane = lax.broadcasted_iota(jnp.int32, (parts * per, 128), 1)
    top = jnp.where(lane < heads, top, 0.0).reshape(parts, per, 128)
    tot = jnp.where(lane < heads, tot, 1.0).reshape(parts, per, 128)
    e = jnp.exp(top - jnp.max(top, 0, keepdims=True))
    f = e / jnp.sum(e * tot, 0, keepdims=True)
    f = jnp.where(lane < heads, f.reshape(parts * per, 128), 0.0)
    hrow = lax.broadcasted_iota(jnp.int32, (128, width), 0) * size
    col = lax.broadcasted_iota(jnp.int32, (128, width), 1)
    spread = jnp.where((col >= hrow) & (col < hrow + size), 1.0, 0.0).astype(BF)
    hi = f.astype(BF)
    low = (f - hi.astype(F32)).astype(BF)
    factor = jnp.dot(jnp.concatenate([hi, low], 1), jnp.concatenate([spread, spread], 0), preferred_element_type=F32)
    attended = []
    for i in range(tiles):
        at = [(s * (tiles // 2) + i // 2) * per for s in range(2)]
        num = [parts_ref[:, a : a + per, :].astype(F32)[:, i % 2 * half : i % 2 * half + half] for a in at]
        num = jnp.concatenate(num, 1)
        attended.append(jnp.sum(num * factor[:, i * 128 : (i + 1) * 128].reshape(parts, per, 128), 0))
    gated = (gate_ref[...] * jnp.concatenate(attended, 1)).astype(BF)
    update = jnp.dot(gated, wout_ref[...], preferred_element_type=F32)
    out_ref[...] = update.reshape(out_ref.shape).astype(BF)


def near_swaps(n):
    ring = lambda a, b, size: min((a - b) % size, (b - a) % size)
    upper = lambda i: i // 2 % 2
    tables = ([], [])
    for c in range(n):

        def cost(j, i):
            hops = ring(c // 4, i // 4, 4) + ring(j % 8, c % 8, 8)
            hops += ring(upper(c) * 2 + j // 8, upper(i) * 2 + c // 8, 4)
            return 2 * hops + (c % 2 != i % 2)

        first = {}
        for table in tables:
            for most in range(100):
                taken = {}

                def place(j, seen):
                    for i in range(n):
                        other = j not in first or upper(first[j]) != upper(i)
                        if other and cost(j, i) <= most and i not in seen:
                            seen.add(i)
                            if i not in taken or place(taken[i], seen):
                                taken[i] = j
                                return True
                    return False

                if all(place(j, set()) for j in range(n)):
                    break
            table.append([taken[i] for i in range(n)])
            first = {j: i for i, j in taken.items()}
    return tables


def params(mib):
    return pltpu.CompilerParams(vmem_limit_bytes=mib << 20)


def shards(
    single,
    restype,
    restype_table,
    chain,
    live,
    pair,
    pair_gain,
    pair_weight,
    chain_bias,
    single_gain,
    w_qkvg,
    w_out,
):
    samples, tok, width = single.shape
    row_len, col_len, channels = pair.shape
    heads = chain_bias.shape[0]
    n_row, n_col = lax.axis_size("qrow"), lax.axis_size("kcol")
    shape = jax.ShapeDtypeStruct
    own = samples * tok

    stay = lambda *arrays: [pltpu.with_memory_space_constraint(x, pltpu.HBM) for x in arrays]
    hbm = lambda count: [pl.BlockSpec(memory_space=pltpu.HBM)] * count
    dma = pltpu.SemaphoreType.DMA
    normed, copies = pl.pallas_call(
        norm_kernel,
        name="norm",
        out_shape=(shape((own, width), BF), shape((n_col // 2, own, width), BF)),
        in_specs=hbm(4),
        out_specs=(vmem(), vmem()),
        scratch_shapes=[
            pltpu.SMEM((tok,), jnp.int32),
            pltpu.VMEM((own, width), BF),
            pltpu.VMEM(restype_table.shape, BF),
            pltpu.VMEM((width,), F32),
            dma((4,)),
        ],
        compiler_params=params(4),
    )(*stay(restype, single.reshape(own, width), restype_table, single_gain))

    tables = near_swaps(n_row)
    turned = []
    for table in tables:
        swap = [(c * n_col + j, i * n_col + c) for c in range(n_row) for i, j in enumerate(table[c])]
        turned.append(lax.ppermute(normed, ("qrow", "kcol"), swap))
    near = [list(range(n_col // 2)), list(range(n_col // 2, n_col))]
    row_tokens = lax.all_to_all(copies, "kcol", 0, 0, axis_index_groups=near)

    where = jnp.stack([lax.axis_index("qrow"), lax.axis_index("kcol")]).astype(jnp.int32)
    block = row_len // 8

    def bias_of(late):
        chunks = 5 if late else 3
        out = [pltpu.HBM((heads, chunks * block, col_len), F32)]
        out += [shape((width, 2 * width), BF) if late else pltpu.HBM((own, width), F32)]
        out += [shape((width, width), BF)] * late
        return pl.pallas_call(
            functools.partial(bias_kernel, late * 3 * block, late),
            name="bias_" + str(late),
            out_shape=out,
            in_specs=[vmem(), smem()] + hbm(8),
            out_specs=[vmem()] * len(out),
            scratch_shapes=[
                pltpu.SMEM(chain.shape, jnp.int32),
                pltpu.SMEM((heads,), F32),
                pltpu.VMEM((chain.shape[0] // col_len, col_len), jnp.int32),
                pltpu.VMEM((1, col_len), jnp.int32),
                pltpu.VMEM((1, channels), F32),
                pltpu.VMEM((heads, channels), F32),
                pltpu.VMEM((chunks, block, col_len, channels), BF),
                dma((6,)),
                dma((chunks,)),
            ]
            + ([] if late else [pltpu.VMEM((width, width), BF)])
            + [dma((2,))],
            compiler_params=params(10),
            cost_estimate=pl.CostEstimate(flops=5 * 10**8, bytes_accessed=10 * 10**6, transcendentals=0),
        )(
            normed,
            where,
            *stay(
                chain,
                chain_bias,
                chain.reshape(-1, col_len),
                live.reshape(1, col_len),
                pair_gain.reshape(1, channels),
                pair_weight.T,
                pair,
                w_qkvg,
            ),
        )

    bias_a, gate = bias_of(0)
    bias_b, w_kv, w_q = bias_of(1)
    sides = [[i for i in range(n_row) if i // 2 % 2 == side] for side in range(2)]
    turned_copies = pl.pallas_call(
        copies_kernel,
        name="copies",
        out_shape=shape((n_row // 2, 2 * own, width), BF),
        in_specs=[vmem()] * 2 + hbm(1),
        out_specs=vmem(),
        compiler_params=params(4),
    )(*turned, *stay(bias_a))
    turned_copies, row_tokens = lax.optimization_barrier((turned_copies, row_tokens))
    col_tokens = lax.all_to_all(turned_copies, "qrow", 0, 0, axis_index_groups=sides)
    other_tokens = lax.ppermute(row_tokens, "kcol", [(i, (i + n_col // 2) % n_col) for i in range(n_col)])
    col_tokens = col_tokens.reshape(n_row, own, width)
    queries = pl.pallas_call(
        query_kernel,
        name="query",
        out_shape=shape((samples, row_len, width), BF),
        in_specs=[smem()] + [vmem()] * 3,
        out_specs=vmem(),
        scratch_shapes=[pltpu.VMEM((n_col, own, width), BF)],
        compiler_params=params(6),
    )(where, row_tokens, other_tokens, w_q)
    order = [tables[k][c][i] for c in range(n_col) for side in sides for i in side for k in range(2)]
    order = jnp.asarray(order, jnp.int32)

    rows = own * width // 128 + own
    partial = pl.pallas_call(
        attend_kernel,
        name="attend",
        out_shape=shape((n_col, rows, 128), BF),
        in_specs=[smem()] * 2 + [vmem()] * 3 + hbm(2),
        out_specs=vmem(),
        scratch_shapes=[
            pltpu.VMEM(col_tokens.shape, BF),
            pltpu.VMEM((heads, row_len, col_len), F32),
            dma((2,)),
        ],
        compiler_params=params(16),
    )(where, order, col_tokens, w_kv, queries, *stay(bias_a, bias_b))

    gathered = lax.all_to_all(partial, "kcol", 0, 0)
    return pl.pallas_call(
        merge_kernel,
        name="merge",
        out_shape=shape((samples, tok, width), BF),
        in_specs=[vmem(), vmem(), vmem()],
        out_specs=vmem(),
        compiler_params=params(8),
    )(gathered, gate, w_out)


def solution(mesh):
    return jax.shard_map(
        shards,
        mesh=mesh,
        in_specs=(
            P(None, ("qrow", "kcol"), None),
            P(("qrow", "kcol")),
            P(),
            P(),
            P("kcol"),
            P("qrow", "kcol", None),
            P(),
            P(),
            P(),
            P(),
            P(),
            P(),
        ),
        out_specs=P(None, ("qrow", "kcol"), None),
        check_vma=False,
    )
```

```python
import functools
import math

import jax
import jax.numpy as jnp
from jax import lax
from jax.experimental import pallas as pl
from jax.experimental.pallas import tpu as pltpu
from jax.sharding import PartitionSpec as P

BF = jnp.bfloat16
F32 = jnp.float32
EPS = 1e-05


def vmem():
    return pl.BlockSpec(memory_space=pltpu.VMEM)


def smem():
    return pl.BlockSpec(memory_space=pltpu.SMEM)


def dot_nt(a, b):
    return lax.dot_general(a, b, (((1,), (1,)), ((), ())), preferred_element_type=F32)


def layer_norm(x):
    centred = x - jnp.mean(x, -1, keepdims=True)
    variance = jnp.mean(centred * centred, -1, keepdims=True)
    return centred * lax.rsqrt(variance + EPS)


def split3(x):
    hi = x.astype(BF)
    rest = x - hi.astype(F32)
    mid = rest.astype(BF)
    low = (rest - mid.astype(F32)).astype(BF)
    return hi, mid, low


def fetch(copies, sems):
    started = [pltpu.make_async_copy(src, dst, sems.at[i]) for i, (src, dst) in enumerate(copies)]
    for copy in started:
        copy.start()
    for copy in started:
        copy.wait()


def norm_kernel(
    restype_hbm, single_hbm, table_hbm, gain_hbm, normed_ref, copies_ref, restype_ref, single_ref, table_ref, gain_ref, sems
):
    fetch(
        [
            (restype_hbm, restype_ref),
            (single_hbm, single_ref),
            (table_hbm, table_ref),
            (gain_hbm, gain_ref),
        ],
        sems,
    )
    rows, width = single_ref.shape
    tok = restype_ref.shape[0]
    samples = rows // tok
    kinds = table_ref.shape[0]
    row = lax.broadcasted_iota(jnp.int32, (tok, kinds), 0)
    col = lax.broadcasted_iota(jnp.int32, (tok, kinds), 1)
    kind = jnp.zeros((tok, kinds), jnp.int32)
    for t in range(tok):
        kind = jnp.where(row == t, restype_ref[t], kind)
    one_hot = jnp.where(kind == col, 1.0, 0.0).astype(BF)
    emb = jnp.dot(one_hot, table_ref[...], preferred_element_type=F32)
    x = single_ref[...].astype(F32).reshape(samples, tok, width) + emb[None]
    normed = layer_norm(x) * gain_ref[...].reshape(1, 1, width)
    normed = normed.reshape(samples * tok, width).astype(BF)
    normed_ref[...] = normed
    for j in range(copies_ref.shape[0]):
        copies_ref[j] = normed


def copies_kernel(one_ref, two_ref, after_ref, copies_ref):
    per = one_ref.shape[0]
    for j in range(copies_ref.shape[0]):
        copies_ref[j, :per] = one_ref[...]
        copies_ref[j, per:] = two_ref[...]


def bias_kernel(start, late, own_ref, where_ref, *refs):
    ins, refs = refs[:8], refs[8:]
    pair_hbm, w_hbm = ins[6:]
    out_ref, extra_ref, refs = refs[0], refs[1], refs[2:]
    if late:
        wq_ref, refs = refs[0], refs[1:]
    chain_ref, cbias_ref, chain_rows_ref, live_ref, gain_ref, weight_ref, pair_ref, sems, pair_sems = refs[:9]
    w_ref, w_sem = (extra_ref, refs[9]) if late else refs[9:]
    chunks, block, keys, channels = pair_ref.shape
    heads = weight_ref.shape[0]
    width = own_ref.shape[1]
    loads = [
        pltpu.make_async_copy(pair_hbm.at[pl.ds(start + i * block, block)], pair_ref.at[i], pair_sems.at[i])
        for i in range(chunks)
    ]
    for load in loads[:2]:
        load.start()
    small = list(zip(ins[:6], (chain_ref, cbias_ref, chain_rows_ref, live_ref, gain_ref, weight_ref)))
    small = [pltpu.make_async_copy(src, dst, sems.at[i]) for i, (src, dst) in enumerate(small)]
    for load in small + loads[2:]:
        load.start()
    place = pl.ds(width, 2 * width) if late else pl.ds(3 * width, width)
    load_w = [pltpu.make_async_copy(w_hbm.at[:, place], w_ref, w_sem.at[0])]
    if late:
        load_w.append(pltpu.make_async_copy(w_hbm.at[:, pl.ds(0, width)], wq_ref, w_sem.at[1]))
    for load in small:
        load.wait()
    weight = weight_ref[...] * gain_ref[...]
    lhs = jnp.concatenate(split3(weight), 0)
    total = jnp.sum(weight, -1, keepdims=True)
    row = lax.broadcasted_iota(jnp.int32, (heads, keys), 0)
    column = jnp.zeros((heads, keys), F32)
    for h in range(heads):
        column = jnp.where(row == h, cbias_ref[h], column)
    base = where_ref[0] * pair_hbm.shape[0] + start
    col_chain = chain_rows_ref[pl.ds(where_ref[1], 1), :]
    alive = jnp.broadcast_to(live_ref[...] == 1, (heads, keys))
    for i in range(chunks):
        loads[i].wait()
        if i == 1:
            for load in load_w:
                load.start()
        for q in range(0, block, 2):
            turned = pair_ref[i, q : q + 2].reshape(2 * keys, channels).T
            x = turned.astype(F32)
            mean = jnp.sum(x, 0, keepdims=True) * (1.0 / channels)
            centred = x - mean
            variance = jnp.sum(centred * centred, 0, keepdims=True) * (1.0 / channels)
            res = jnp.dot(lhs, turned, preferred_element_type=F32)
            res = res[:heads] + res[heads : 2 * heads] + res[2 * heads :]
            res = (res - total * mean) * lax.rsqrt(variance + EPS)
            for k in range(2):
                at = i * block + q + k
                part = res[:, k * keys : (k + 1) * keys]
                same = col_chain == chain_ref[base + at]
                part = part + jnp.where(same, column, 0.0)
                out_ref[:, at, :] = jnp.where(alive, part, -1e30)
    for load in load_w:
        load.wait()
    if not late:
        pre = jnp.dot(own_ref[...], w_ref[...], preferred_element_type=F32)
        extra_ref[...] = jax.nn.sigmoid(pre)


def query_kernel(where_ref, rows_ref, others_ref, w_ref, q_ref, x_ref):
    near, per, width = rows_ref.shape
    ours = lax.div(where_ref[1], near) * near
    x_ref[pl.ds(ours, near)] = rows_ref[...]
    x_ref[pl.ds(near - ours, near)] = others_ref[...]
    x = x_ref[...].reshape(2 * near * per, width)
    query = jnp.dot(x, w_ref[...], preferred_element_type=F32).reshape(2 * near, 2, per // 2, width)
    for s in range(2):
        q_ref[s] = query[:, s].reshape(near * per, width).astype(BF)


def attend_kernel(
    where_ref, order_ref, cols_ref, wkv_ref, q_ref, bias_a_hbm, bias_b_hbm, out_ref, x_ref, bias_ref, sems
):
    parts, per, width = cols_ref.shape
    half = per // 2
    heads, queries, keys = bias_ref.shape
    few = bias_a_hbm.shape[1]
    size = width // heads
    scale = 1.0 / math.sqrt(size)
    loads = [
        pltpu.make_async_copy(bias_a_hbm, bias_ref.at[:, pl.ds(0, few)], sems.at[0]),
        pltpu.make_async_copy(bias_b_hbm, bias_ref.at[:, pl.ds(few, queries - few)], sems.at[1]),
    ]
    for load in loads:
        load.start()
    base = (where_ref[1] * 2 + lax.rem(lax.div(where_ref[0], 2), 2)) * parts
    for i in range(parts):
        x_ref[pl.ds(order_ref[base + i], 1)] = cols_ref[pl.ds(i, 1)]
    x = x_ref[...].reshape(parts * per, width)

    def project(w):
        return jnp.dot(x, w, preferred_element_type=F32).reshape(parts, 2, half, width)

    kf, vf = project(wkv_ref[:, :width]), project(wkv_ref[:, width:])
    span = 256
    wins = width // span

    def members(t):
        return [h for h in range(heads) if h * size < (t + 1) * span and (h + 1) * size > t * span]

    def mask_of(h, t):
        spot = lax.broadcasted_iota(jnp.int32, (1, span), 1) + t * span
        return jnp.where((spot >= h * size) & (spot < (h + 1) * size), 1.0, 0.0).astype(BF)

    lane = lax.broadcasted_iota(jnp.int32, (queries, 128), 1)
    stats = []
    for s in range(2):
        q = q_ref[s]
        k = kf[:, s].reshape(keys, width).astype(BF)
        v = vf[:, s].reshape(keys, width).astype(BF)
        raw = {}
        for t in range(wins):
            cut = slice(t * span, (t + 1) * span)
            lhs = jnp.concatenate([q[:, cut] * mask_of(h, t) for h in members(t)], 0)
            res = dot_nt(lhs, k[:, cut])
            for i, h in enumerate(members(t)):
                piece = res[i * queries : (i + 1) * queries]
                raw[h] = raw[h] + piece if h in raw else piece
        if s == 0:
            for load in loads:
                load.wait()
        tops = jnp.zeros((queries, 128), F32)
        tots = jnp.zeros((queries, 128), F32)
        rounded = []
        for h in range(heads):
            sc = raw[h] * scale + bias_ref[h]
            top = jnp.max(sc, -1, keepdims=True)
            w = jnp.exp(sc - top)
            rounded.append(w.astype(BF))
            tots = jnp.where(lane == h, jnp.sum(w, -1, keepdims=True), tots)
            tops = jnp.where(lane == h, top, tops)
        for t in range(wins):
            cut = slice(t * span, (t + 1) * span)
            o = jnp.dot(
                jnp.concatenate([rounded[h] for h in members(t)], 1),
                jnp.concatenate([v[:, cut] * mask_of(h, t) for h in members(t)], 0),
                preferred_element_type=F32,
            )
            at = (s * wins + t) * per
            tiles = [o[:, i * 128 : (i + 1) * 128].reshape(parts, half, 128) for i in range(2)]
            out_ref[:, at : at + per, :] = jnp.concatenate(tiles, 1).astype(BF)
        hi, mid, low = split3(tops)
        total_hi, total_low, _ = split3(tots)
        mine = hi.astype(F32)
        for i, p in enumerate((mid, low, total_hi, total_low)):
            mine = mine + pltpu.roll(p.astype(F32), heads * (i + 1), 1)
        stats.append(mine.reshape(parts, half, 128))
    out_ref[:, 2 * wins * per :, :] = jnp.concatenate(stats, 1).astype(BF)


def merge_kernel(parts_ref, gate_ref, wout_ref, out_ref):
    parts, rows, _ = parts_ref.shape
    per, width = gate_ref.shape
    half = per // 2
    tiles = width // 128
    heads = 16
    size = width // heads
    st = parts_ref[:, tiles * per :, :].astype(F32).reshape(parts * per, 128)
    top = st + pltpu.roll(st, 128 - heads, 1) + pltpu.roll(st, 128 - 2 * heads, 1)
    tot = pltpu.roll(st, 128 - 3 * heads, 1) + pltpu.roll(st, 128 - 4 * heads, 1)
    lane = lax.broadcasted_iota(jnp.int32, (parts * per, 128), 1)
    top = jnp.where(lane < heads, top, 0.0).reshape(parts, per, 128)
    tot = jnp.where(lane < heads, tot, 1.0).reshape(parts, per, 128)
    e = jnp.exp(top - jnp.max(top, 0, keepdims=True))
    f = e / jnp.sum(e * tot, 0, keepdims=True)
    f = jnp.where(lane < heads, f.reshape(parts * per, 128), 0.0)
    hrow = lax.broadcasted_iota(jnp.int32, (128, width), 0) * size
    col = lax.broadcasted_iota(jnp.int32, (128, width), 1)
    spread = jnp.where((col >= hrow) & (col < hrow + size), 1.0, 0.0).astype(BF)
    hi = f.astype(BF)
    low = (f - hi.astype(F32)).astype(BF)
    factor = jnp.dot(jnp.concatenate([hi, low], 1), jnp.concatenate([spread, spread], 0), preferred_element_type=F32)
    attended = []
    for i in range(tiles):
        at = [(s * (tiles // 2) + i // 2) * per for s in range(2)]
        num = [parts_ref[:, a : a + per, :].astype(F32)[:, i % 2 * half : i % 2 * half + half] for a in at]
        num = jnp.concatenate(num, 1)
        attended.append(jnp.sum(num * factor[:, i * 128 : (i + 1) * 128].reshape(parts, per, 128), 0))
    gated = (gate_ref[...] * jnp.concatenate(attended, 1)).astype(BF)
    update = jnp.dot(gated, wout_ref[...], preferred_element_type=F32)
    out_ref[...] = update.reshape(out_ref.shape).astype(BF)


def near_swaps(n):
    ring = lambda a, b, size: min((a - b) % size, (b - a) % size)
    upper = lambda i: i // 2 % 2
    tables = ([], [])
    for c in range(n):

        def cost(j, i):
            hops = ring(c // 4, i // 4, 4) + ring(j % 8, c % 8, 8)
            hops += ring(upper(c) * 2 + j // 8, upper(i) * 2 + c // 8, 4)
            return 2 * hops + (c % 2 != i % 2)

        first = {}
        for table in tables:
            for most in range(100):
                taken = {}

                def place(j, seen):
                    for i in range(n):
                        other = j not in first or upper(first[j]) != upper(i)
                        if other and cost(j, i) <= most and i not in seen:
                            seen.add(i)
                            if i not in taken or place(taken[i], seen):
                                taken[i] = j
                                return True
                    return False

                if all(place(j, set()) for j in range(n)):
                    break
            table.append([taken[i] for i in range(n)])
            first = {j: i for i, j in taken.items()}
    return tables


def params(mib):
    return pltpu.CompilerParams(vmem_limit_bytes=mib << 20)


def shards(
    single,
    restype,
    restype_table,
    chain,
    live,
    pair,
    pair_gain,
    pair_weight,
    chain_bias,
    single_gain,
    w_qkvg,
    w_out,
):
    samples, tok, width = single.shape
    row_len, col_len, channels = pair.shape
    heads = chain_bias.shape[0]
    n_row, n_col = lax.axis_size("qrow"), lax.axis_size("kcol")
    shape = jax.ShapeDtypeStruct
    own = samples * tok

    stay = lambda *arrays: [pltpu.with_memory_space_constraint(x, pltpu.HBM) for x in arrays]
    hbm = lambda count: [pl.BlockSpec(memory_space=pltpu.HBM)] * count
    dma = pltpu.SemaphoreType.DMA
    normed, copies = pl.pallas_call(
        norm_kernel,
        name="norm",
        out_shape=(shape((own, width), BF), shape((n_col // 2, own, width), BF)),
        in_specs=hbm(4),
        out_specs=(vmem(), vmem()),
        scratch_shapes=[
            pltpu.SMEM((tok,), jnp.int32),
            pltpu.VMEM((own, width), BF),
            pltpu.VMEM(restype_table.shape, BF),
            pltpu.VMEM((width,), F32),
            dma((4,)),
        ],
        compiler_params=params(4),
    )(*stay(restype, single.reshape(own, width), restype_table, single_gain))

    tables = near_swaps(n_row)
    turned = []
    for table in tables:
        swap = [(c * n_col + j, i * n_col + c) for c in range(n_row) for i, j in enumerate(table[c])]
        turned.append(lax.ppermute(normed, ("qrow", "kcol"), swap))
    near = [list(range(n_col // 2)), list(range(n_col // 2, n_col))]
    row_tokens = lax.all_to_all(copies, "kcol", 0, 0, axis_index_groups=near)

    where = jnp.stack([lax.axis_index("qrow"), lax.axis_index("kcol")]).astype(jnp.int32)
    block = row_len // 8

    def bias_of(late):
        chunks = 4
        out = [pltpu.HBM((heads, chunks * block, col_len), F32)]
        out += [shape((width, 2 * width), BF) if late else pltpu.HBM((own, width), F32)]
        out += [shape((width, width), BF)] * late
        return pl.pallas_call(
            functools.partial(bias_kernel, late * chunks * block, late),
            name="bias_" + str(late),
            out_shape=out,
            in_specs=[vmem(), smem()] + hbm(8),
            out_specs=[vmem()] * len(out),
            scratch_shapes=[
                pltpu.SMEM(chain.shape, jnp.int32),
                pltpu.SMEM((heads,), F32),
                pltpu.VMEM((chain.shape[0] // col_len, col_len), jnp.int32),
                pltpu.VMEM((1, col_len), jnp.int32),
                pltpu.VMEM((1, channels), F32),
                pltpu.VMEM((heads, channels), F32),
                pltpu.VMEM((chunks, block, col_len, channels), BF),
                dma((6,)),
                dma((chunks,)),
            ]
            + ([] if late else [pltpu.VMEM((width, width), BF)])
            + [dma((2,))],
            compiler_params=params(10),
            cost_estimate=pl.CostEstimate(flops=5 * 10**8, bytes_accessed=10 * 10**6, transcendentals=0),
        )(
            normed,
            where,
            *stay(
                chain,
                chain_bias,
                chain.reshape(-1, col_len),
                live.reshape(1, col_len),
                pair_gain.reshape(1, channels),
                pair_weight.T,
                pair,
                w_qkvg,
            ),
        )

    bias_a, gate = bias_of(0)
    bias_b, w_kv, w_q = bias_of(1)
    sides = [[i for i in range(n_row) if i // 2 % 2 == side] for side in range(2)]
    turned_copies = pl.pallas_call(
        copies_kernel,
        name="copies",
        out_shape=shape((n_row // 2, 2 * own, width), BF),
        in_specs=[vmem()] * 2 + hbm(1),
        out_specs=vmem(),
        compiler_params=params(4),
    )(*turned, *stay(bias_a))
    turned_copies, row_tokens = lax.optimization_barrier((turned_copies, row_tokens))
    col_tokens = lax.all_to_all(turned_copies, "qrow", 0, 0, axis_index_groups=sides)
    other_tokens = lax.ppermute(row_tokens, "kcol", [(i, (i + n_col // 2) % n_col) for i in range(n_col)])
    col_tokens = col_tokens.reshape(n_row, own, width)
    queries = pl.pallas_call(
        query_kernel,
        name="query",
        out_shape=shape((samples, row_len, width), BF),
        in_specs=[smem()] + [vmem()] * 3,
        out_specs=vmem(),
        scratch_shapes=[pltpu.VMEM((n_col, own, width), BF)],
        compiler_params=params(6),
    )(where, row_tokens, other_tokens, w_q)
    order = [tables[k][c][i] for c in range(n_col) for side in sides for i in side for k in range(2)]
    order = jnp.asarray(order, jnp.int32)

    rows = own * width // 128 + own
    partial = pl.pallas_call(
        attend_kernel,
        name="attend",
        out_shape=shape((n_col, rows, 128), BF),
        in_specs=[smem()] * 2 + [vmem()] * 3 + hbm(2),
        out_specs=vmem(),
        scratch_shapes=[
            pltpu.VMEM(col_tokens.shape, BF),
            pltpu.VMEM((heads, row_len, col_len), F32),
            dma((2,)),
        ],
        compiler_params=params(16),
    )(where, order, col_tokens, w_kv, queries, *stay(bias_a, bias_b))

    gathered = lax.all_to_all(partial, "kcol", 0, 0)
    return pl.pallas_call(
        merge_kernel,
        name="merge",
        out_shape=shape((samples, tok, width), BF),
        in_specs=[vmem(), vmem(), vmem()],
        out_specs=vmem(),
        compiler_params=params(8),
    )(gathered, gate, w_out)


def solution(mesh):
    return jax.shard_map(
        shards,
        mesh=mesh,
        in_specs=(
            P(None, ("qrow", "kcol"), None),
            P(("qrow", "kcol")),
            P(),
            P(),
            P("kcol"),
            P("qrow", "kcol", None),
            P(),
            P(),
            P(),
            P(),
            P(),
            P(),
        ),
        out_specs=P(None, ("qrow", "kcol"), None),
        check_vma=False,
    )
```
